512 devices in a mesh: phase: 8 (over y, core), tensor: 16 (over x, z_lo), seq: 4 (over z_hi).
Axes of the slice: x: 4, y: 4, z: 16 (z_hi: 4, z_lo: 4; z = z_hi * 4 + z_lo), core: 2. Of those that a mesh axis runs over, the one named last changes fastest.
Arguments:
- hidden: bfloat16 [8, 512, 8192], P('phase', 'seq', 'tensor'), may hold values from -52 to 52
- segment_ids: int32 [8, 512], P('phase', 'seq'), may hold values from 0 to 1, never falling along the last dimension, each value on 1 to 320 neighbouring positions
- gain_attn: bfloat16 [8, 8192], P('phase', 'tensor'), may hold values from 0.5 to 1.5
- gain_ffn: bfloat16 [8, 8192], P('phase', 'tensor'), may hold values from 0.5 to 1.5
- w_query: bfloat16 [8, 8192, 8192], P('phase', 'seq', 'tensor'), may hold values from -2 to 2
- w_key: bfloat16 [8, 8192, 1024], P('phase', 'seq', 'tensor'), may hold values from -2 to 2
- w_value: bfloat16 [8, 8192, 1024], P('phase', 'seq', 'tensor'), may hold values from -0.0625 to 0.0625
Outputs:
- passed: bfloat16 [8, 512, 8192], P('phase', 'seq', 'tensor')
- hessians: bfloat16 [8, 8192, 8192], P('phase', 'tensor', 'seq')
- ffn_diagonal: float32 [8, 8192], P('phase', ('tensor', 'seq'))
The draws below stay inside these ranges and needn't reach their ends.
Inputs may be any that keep to these rules, and one draw needn't show every extreme that they name: `segment_ids`: in each section the tokens form two contiguous documents, document 0 first, each holding at least one token.
All inputs are finite; a program needn't handle non-finite values.
Results may differ from the reference program's by a relative error of at most 0.017.
Values may be sent and summed in bfloat16 or wider, within the bound.
No kernel may reach another device: no remote copies, remote signals or barrier semaphores. Data moves between devices by JAX's collectives and lax.ppermute only.
A program may use at most 64 MiB of HBM per device.

```python
import math
import jax
import jax.numpy as jnp
import numpy as np
from jax import lax

D = 8192
HEADS = 64
HD = 128
KVH = 8
DOCS = 2
TOKENS = 512
SECTIONS = 8


def draw_hidden(key, part):
    key = jax.random.fold_in(key, 11)
    base_key, row_key = jax.random.split(key)
    shape = (SECTIONS, TOKENS, D)
    column = jnp.arange(D, dtype=jnp.float32) / D
    base = jnp.clip(jax.random.normal(base_key, shape, jnp.float32), -6.0, 6.0)
    rise = jnp.sqrt(1.0 + 2.0 * column)
    row_scale = jnp.exp(jax.random.uniform(row_key, (SECTIONS, TOKENS, 1), jnp.float32, jnp.log(0.5), jnp.log(5.0)))
    return (base * row_scale * rise[None, None, :]).astype(jnp.bfloat16)


def projection_draw(key, columns):
    base = jnp.clip(jax.random.normal(key, (SECTIONS, D, columns), jnp.float32), -6.0, 6.0)
    return (base / jnp.sqrt(jnp.float32(D))).astype(jnp.bfloat16)


def draw_w_query(key, part):
    key = jax.random.fold_in(key, 12)
    return projection_draw(key, HEADS * HD)


def draw_w_key(key, part):
    key = jax.random.fold_in(key, 13)
    return projection_draw(key, KVH * HD)


def shard_levels(rng, extent, cuts, low, top_value):
    level = 1.0
    for dim, parts in cuts:
        draws = jax.random.uniform(jax.random.fold_in(jax.random.fold_in(rng, 6), dim), (parts,), jnp.float32, low / len(cuts), top_value / len(cuts))
        level = level * jnp.repeat(jnp.exp(draws), extent[dim] // parts).reshape((-1,) + (1,) * (len(extent) - 1 - dim))
    return level


def split_up(number_of, total, bound, lean):
    weights = [(1 << 20) // math.isqrt(rank ** lean) + 1 for rank in range(2, number_of + 1)]
    surplus, given = total - bound - (number_of - 1), [1] * (number_of - 1)
    while surplus > 0:
        movable = [i for i in range(number_of - 1) if given[i] < bound]
        whole, remaining = sum([weights[i] for i in movable]), surplus
        for i in movable:
            extra = min(bound - given[i], max(1, remaining * weights[i] // whole), surplus)
            given[i] = given[i] + extra
            surplus = surplus - extra
    return np.array([bound] + given)


def ragged_sizes(rng, count, total, most, slope):
    if count == 2:
        one = jax.random.randint(rng, (), max(1, total - most), min(most, total - 1) + 1)
        return jnp.stack([one, total - one])
    tallies = jnp.asarray(split_up(count, total, most, slope), jnp.int32)
    couples = (count - 1) // 2
    giver, sink = tallies[1:1 + 2 * couples:2], tallies[2:2 + 2 * couples:2]
    room = jnp.minimum(giver - 1, most - sink)
    shifted = jax.random.randint(jax.random.fold_in(rng, 1), (couples,), 0, 1 << 20) % (room + 1)
    tallies = tallies.at[1:1 + 2 * couples:2].set(giver - shifted).at[2:2 + 2 * couples:2].set(sink + shifted)
    return tallies[jax.random.permutation(jax.random.fold_in(rng, 2), count)]


def bell_draw(key, extent, width, bound, shards=(), kind=jnp.bfloat16):
    entries = jax.random.normal(key, extent, jnp.float32) * width
    if len(shards) > 0:
        entries = shard_levels(key, extent, shards, -0.22, 0.18) * entries
    return jnp.clip(entries, min=-bound, max=bound).astype(kind)


def setup_inputs(seed: int = 0) -> dict:
    key_list = jax.random.split(jax.random.key(seed), 8)
    hidden = draw_hidden(jax.random.fold_in(key_list[7], 71), 0)
    segment_ids = jax.vmap(lambda own: jnp.searchsorted(jnp.cumsum(ragged_sizes(own, DOCS, TOKENS, (5 * TOKENS) // 8, 1)), jnp.arange(TOKENS), side="right"))(jax.random.split(key_list[1], SECTIONS)).reshape((SECTIONS, TOKENS)).astype(jnp.int32)
    gain_attn = jnp.clip(1.0 + 0.1 * jax.random.normal(key_list[2], (SECTIONS, D), jnp.float32), 0.5, 1.5).astype(jnp.bfloat16)
    gain_ffn = jnp.clip(1.0 + 0.1 * jax.random.normal(key_list[3], (SECTIONS, D), jnp.float32), 0.5, 1.5).astype(jnp.bfloat16)
    w_query = draw_w_query(jax.random.fold_in(key_list[7], 71), 0)
    w_key = draw_w_key(jax.random.fold_in(key_list[7], 71), 0)
    w_value = bell_draw(key_list[6], (SECTIONS, D, KVH * HD), D ** -0.5, 0.0625, ((0, 8), (1, 4), (2, 16)))
    return dict(hidden=hidden, segment_ids=segment_ids, gain_attn=gain_attn, gain_ffn=gain_ffn, w_query=w_query, w_key=w_key, w_value=w_value)


norm_eps = 1e-05
rope_base = 500000.0

def normalize_rows(values, gain):
    mean_sq = lax.optimization_barrier(jnp.mean(values * values, axis=-1, keepdims=True))
    return (values * lax.rsqrt(mean_sq + norm_eps) * gain.astype(jnp.float32)[None, :]).astype(jnp.bfloat16)

def rotate_pairs(values, positions):
    half_dim = values.shape[-1] // 2
    freq = rope_base ** (-(jnp.arange(half_dim, dtype=jnp.float32) * 2.0 / values.shape[-1]))
    angle = positions[:, None] * freq[None, :]
    cosine = jnp.cos(angle)[:, None, :]
    sine = jnp.sin(angle)[:, None, :]
    first = values[..., :half_dim]
    second = values[..., half_dim:]
    return jnp.concatenate([first * cosine - second * sine, second * cosine + first * sine], axis=-1)

def reference(hidden, segment_ids, gain_attn, gain_ffn, w_query, w_key, w_value):
    group = HEADS // KVH
    positions = jnp.arange(TOKENS, dtype=jnp.float32)
    token_ids = jnp.arange(TOKENS, dtype=jnp.int32)
    feature_ids = jnp.arange(D, dtype=jnp.int32)
    upper = feature_ids[:, None] <= feature_ids[None, :]
    scale = 2.0 / TOKENS
    outputs = []
    hess_list = []
    diag_list = []
    for section in range(SECTIONS):
        resid = hidden[section].astype(jnp.float32)
        normed_attn = normalize_rows(resid, gain_attn[section])
        query = jnp.dot(normed_attn, w_query[section], preferred_element_type=jnp.float32).reshape(TOKENS, HEADS, HD)
        key = jnp.dot(normed_attn, w_key[section], preferred_element_type=jnp.float32).reshape(TOKENS, KVH, HD)
        value = jnp.dot(normed_attn, w_value[section], preferred_element_type=jnp.float32).reshape(TOKENS, KVH, HD)
        query = rotate_pairs(query, positions).reshape(TOKENS, KVH, group, HD)
        key = rotate_pairs(key, positions)
        segs = segment_ids[section]
        allowed = (token_ids[None, :] <= token_ids[:, None]) & (segs[None, :] == segs[:, None])
        scores = jnp.einsum('tkgd,nkd->tkgn', query, key, precision=lax.Precision.HIGHEST) / jnp.sqrt(jnp.float32(HD))
        scores = jnp.where(allowed[:, None, None, :], scores, jnp.float32(-1e+30))
        peak = lax.optimization_barrier(jnp.max(scores, axis=-1, keepdims=True))
        weights = jnp.where(allowed[:, None, None, :], jnp.exp(scores - peak), jnp.float32(0.0))
        total = lax.optimization_barrier(jnp.sum(weights, axis=-1))
        context = jnp.einsum('tkgn,nkd->tkgd', weights, value, precision=lax.Precision.HIGHEST) / total[..., None]
        section_out = (resid + context.reshape(TOKENS, HEADS * HD)).astype(jnp.bfloat16)
        normed_ffn = normalize_rows(section_out.astype(jnp.float32), gain_ffn[section])
        attn_hessian = jnp.dot(normed_attn.T, normed_attn, preferred_element_type=jnp.float32) * scale
        ffn_hessian = jnp.dot(normed_ffn.T, normed_ffn, preferred_element_type=jnp.float32) * scale
        hess_list.append(jnp.where(upper, attn_hessian, ffn_hessian).astype(jnp.bfloat16))
        ffn_float = normed_ffn.astype(jnp.float32)
        diag_list.append(lax.optimization_barrier(jnp.sum(ffn_float * ffn_float, axis=0)) * scale)
        outputs.append(section_out)
    passed = jnp.roll(jnp.stack(outputs), 1, axis=0)
    return (passed, jnp.stack(hess_list), jnp.stack(diag_list))
```

```python
import jax
import jax.numpy as jnp
from jax import lax
from jax.sharding import Mesh, PartitionSpec as P

HD = 128
norm_eps = 1e-05
rope_base = 500000.0
ZL = ("za", "zb")
TENSOR = ("x", "za", "zb")
GROUP = TENSOR + ("seq",)
ALL = ("phase",) + GROUP
f32 = jnp.float32
bf16 = jnp.bfloat16


def spread(value, axis):
    count = lax.axis_size(axis)
    copies = jnp.broadcast_to(value[None], (count,) + value.shape)
    return lax.all_to_all(copies, axis, 0, 0)


def swap_x_seq(value):
    nx, nz, ns = lax.axis_size("x"), lax.axis_size(ZL), lax.axis_size("seq")
    pairs = [
        ((x * nz + z) * ns + s, (s * nz + z) * ns + x)
        for x in range(nx)
        for z in range(nz)
        for s in range(ns)
    ]
    return lax.ppermute(value, GROUP, pairs)


def swap_and_pass(value):
    np_, nx, nz, ns = (lax.axis_size(a) for a in ("phase", "x", ZL, "seq"))
    pairs = [
        (
            ((p * nx + x) * nz + z) * ns + s,
            ((((p + 1) % np_) * nx + s) * nz + z) * ns + x,
        )
        for p in range(np_)
        for x in range(nx)
        for z in range(nz)
        for s in range(ns)
    ]
    return lax.ppermute(value, ALL, pairs)


def three_parts(value):
    parts = []
    for _ in range(3):
        part = lax.reduce_precision(value, 8, 7)
        parts.append(part.astype(bf16))
        value = value - part
    return jnp.stack(parts)


def padded_rows(rows, count):
    return jnp.concatenate([rows, jnp.zeros((count - rows.shape[0], rows.shape[1]), rows.dtype)])


def rotate(values, positions):
    half = HD // 2
    freq = rope_base ** (-(jnp.arange(half, dtype=f32) * 2.0 / HD))
    angle = positions[:, None] * freq[None, :]
    cosine, sine = jnp.cos(angle), jnp.sin(angle)
    first, second = values[..., :half], values[..., half:]
    return jnp.concatenate(
        [first * cosine - second * sine, second * cosine + first * sine], axis=-1
    )


def on_device(hidden, segment_ids, gain_attn, gain_ffn, w_query, w_key, w_value):
    x_pos = lax.axis_index("x")
    zl_pos = lax.axis_index(ZL)
    seq_pos = lax.axis_index("seq")
    ns = lax.axis_size("seq")
    rows, feats = hidden.shape[1:]
    tokens = rows * ns
    width = feats * lax.axis_size(TENSOR)
    heads = feats // HD

    extra = jnp.concatenate(
        [gain_attn, gain_ffn, jnp.pad(segment_ids.astype(bf16), ((0, 0), (0, feats - rows)))]
    )
    swapped = swap_x_seq(jnp.concatenate([hidden[0], padded_rows(extra, 16)]))
    resid = swapped[:rows].astype(f32)
    gain_a = swapped[rows].astype(f32)
    gain_f = swapped[rows + 1].astype(f32)
    docs_own = swapped[rows + 2, :rows]

    scaled = (resid * gain_a[None, :]).astype(bf16)
    part_sq = jnp.sum(resid * resid, axis=1)
    attn_lo = lax.all_gather(scaled, ZL)
    attn_cols = spread(attn_lo, "x")
    attn_sq = lax.psum(part_sq, ZL)

    def project(weight):
        w = weight[0].reshape(4, feats, weight.shape[2])
        return lax.dot_general(
            attn_cols, w, (((1, 3), (0, 1)), ((), ())), preferred_element_type=f32
        ).astype(bf16)

    q_part = project(w_query)
    k_part, v_part = project(w_key), project(w_value)
    q_part = q_part.reshape(ns, rows, heads, HD).transpose(0, 2, 1, 3).reshape(ns, heads * rows, HD)
    message = jnp.concatenate([q_part, jnp.concatenate([k_part, v_part], 2)], 1)
    by_block = lax.all_to_all(message, "x", 0, 0)
    sq_rows = padded_rows(three_parts(attn_sq), 16)
    message = jnp.concatenate([by_block, jnp.broadcast_to(sq_rows[None], (ns, 16, rows))], 1)
    arrived = jnp.sum(lax.all_to_all(message, "seq", 0, 0).astype(f32), axis=0)
    query = arrived[: heads * rows].reshape(heads, rows, HD)
    kv = arrived[heads * rows : (heads + 1) * rows]
    total_sq = jnp.sum(arrived[(heads + 1) * rows : (heads + 1) * rows + 3], axis=0)
    r_own = lax.rsqrt(total_sq / width + norm_eps)
    query = query * r_own[None, :, None]
    kv = (kv * r_own[:, None]).astype(bf16)
    tail = jnp.concatenate([three_parts(r_own), docs_own[None]])
    kv_all = spread(jnp.concatenate([kv, padded_rows(tail, 16)]), ("x", "zb"))
    kv_all = kv_all.reshape(ns, 2, rows + 16, HD)
    kv_both = kv_all[:, :, :rows].astype(f32)
    keys = jnp.concatenate([kv_both[:, 0, :, : HD // 2], kv_both[:, 1, :, : HD // 2]], -1)
    values = jnp.concatenate([kv_both[:, 0, :, HD // 2 :], kv_both[:, 1, :, HD // 2 :]], -1)
    keys, values = keys.reshape(tokens, HD), values.reshape(tokens, HD)
    r_attn = jnp.sum(kv_all[:, 0, rows : rows + 3].astype(f32), axis=1).reshape(tokens)
    docs = kv_all[:, 0, rows + 3].reshape(tokens)

    key_ids = jnp.arange(tokens, dtype=jnp.int32)
    own_ids = x_pos * rows + jnp.arange(rows, dtype=jnp.int32)
    inv_root = 1.0 / jnp.sqrt(f32(HD))
    query = rotate(query, own_ids.astype(f32)) * inv_root
    keys = rotate(keys, key_ids.astype(f32))
    allowed = (key_ids[None, :] <= own_ids[:, None]) & (docs[None, :] == docs_own[:, None])
    scores = jnp.einsum("hrd,nd->hrn", query, keys, precision=lax.Precision.HIGHEST)
    scores = jnp.where(allowed[None], scores, f32(-1e30))
    peak = jnp.max(scores, axis=-1, keepdims=True)
    weights = jnp.where(allowed[None], jnp.exp(scores - peak), f32(0.0))
    total = jnp.sum(weights, axis=-1, keepdims=True)
    context = jnp.einsum("hrn,nd->hrd", weights, values, precision=lax.Precision.HIGHEST) / total
    context = context.transpose(1, 0, 2).reshape(rows, feats)
    section_out = (resid + context).astype(bf16)
    passed = swap_and_pass(section_out)[None]

    out_float = section_out.astype(f32)
    out_sq = jnp.sum(out_float * out_float, axis=1)
    out_scaled = (out_float * gain_f[None, :]).astype(bf16)
    ffn_lo = lax.all_gather(out_scaled, ZL)
    ffn_cols = spread(ffn_lo, "x")
    sq_all = jnp.sum(spread(out_sq[None], ZL + ("seq",)), axis=(0, 1))
    r_ffn = lax.rsqrt(spread(sq_all[None], "x").reshape(tokens) / width + norm_eps)
    ffn_rows = lax.all_gather(swap_x_seq(out_scaled), "seq", axis=0, tiled=True)
    attn_own = (hidden[0].astype(f32) * gain_attn.astype(f32)).astype(bf16)
    attn_rows = lax.all_gather(attn_own, "seq", axis=0, tiled=True)

    scale = 2.0 / tokens

    def hessian(rows_, r, cols):
        left = (rows_.astype(f32) * (r * r * scale)[:, None]).astype(bf16)
        return lax.dot_general(
            left.reshape(ns, rows, feats), cols, (((0, 1), (0, 2)), ((), ())),
            preferred_element_type=f32,
        )

    upper_part = hessian(attn_rows, r_attn, attn_cols)
    lower_part = hessian(ffn_rows, r_ffn, ffn_cols)
    row_ids = (x_pos * 4 + zl_pos) * feats + jnp.arange(feats, dtype=jnp.int32)
    col_ids = seq_pos * 4 * feats + jnp.arange(4 * feats, dtype=jnp.int32).reshape(4, feats)
    hessians = jnp.where(row_ids[:, None, None] <= col_ids[None], upper_part, lower_part)
    hessians = hessians.astype(bf16).reshape(1, feats, 4 * feats)
    diag_width = feats // ns
    own_cols = lax.dynamic_slice_in_dim(ffn_rows, seq_pos * diag_width, diag_width, 1).astype(f32)
    own_cols = own_cols * r_ffn[:, None]
    ffn_diagonal = (jnp.sum(own_cols * own_cols, axis=0) * scale)[None]
    return (passed, hessians, ffn_diagonal)


def solution(mesh):
    phase, tensor, seq = (mesh.shape[a] for a in ("phase", "tensor", "seq"))
    lines = Mesh(
        mesh.devices.reshape(phase, tensor // 4, 2, 2, seq), ("phase", "x", "za", "zb", "seq")
    )
    tiled = P("phase", "seq", TENSOR)
    return jax.shard_map(
        on_device,
        mesh=lines,
        in_specs=(
            tiled,
            P("phase", "seq"),
            P("phase", TENSOR),
            P("phase", TENSOR),
            tiled,
            tiled,
            tiled,
        ),
        out_specs=(tiled, P("phase", TENSOR, "seq"), P("phase", GROUP)),
        check_vma=False,
    )
```

```python
import functools

import jax
import jax.numpy as jnp
from jax import lax
from jax.experimental import pallas as pl
from jax.experimental.pallas import tpu as pltpu
from jax.sharding import Mesh, PartitionSpec as P

HD = 128
norm_eps = 1e-05
rope_base = 500000.0
ZL = ("za", "zb")
TENSOR = ("x", "za", "zb")
GROUP = TENSOR + ("seq",)
ALL = ("phase",) + GROUP
f32 = jnp.float32
bf16 = jnp.bfloat16
LIMIT = 24 * 1024 * 1024


def spread(value, axis):
    count = lax.axis_size(axis)
    copies = jnp.broadcast_to(value[None], (count,) + value.shape)
    return lax.all_to_all(copies, axis, 0, 0)


def swap_x_seq(value):
    nx, nz, ns = lax.axis_size("x"), lax.axis_size(ZL), lax.axis_size("seq")
    pairs = [
        ((x * nz + z) * ns + s, (s * nz + z) * ns + x)
        for x in range(nx)
        for z in range(nz)
        for s in range(ns)
    ]
    return lax.ppermute(value, GROUP, pairs)


def swap_and_pass(value):
    np_, nx, nz, ns = (lax.axis_size(a) for a in ("phase", "x", ZL, "seq"))
    pairs = [
        (
            ((p * nx + x) * nz + z) * ns + s,
            ((((p + 1) % np_) * nx + s) * nz + z) * ns + x,
        )
        for p in range(np_)
        for x in range(nx)
        for z in range(nz)
        for s in range(ns)
    ]
    return lax.ppermute(value, ALL, pairs)


def project_kernel(cols, wq, wk, wv, q_out, kv_out, q_acc, kv_acc):
    step = pl.program_id(0)
    blocks, rows, feats = cols.shape
    left = cols[...].reshape(blocks * rows, feats)
    kv_w = jnp.concatenate([wk[...], wv[...]], 0)
    kv = lax.dot_general(left, kv_w, (((1,), (1,)), ((), ())), preferred_element_type=f32)
    q = jnp.dot(left, wq[...], preferred_element_type=f32)

    @pl.when(step == 0)
    def _():
        q_acc[...] = q
        kv_acc[...] = kv

    @pl.when(step > 0)
    def _():
        q_acc[...] += q
        kv_acc[...] += kv

    @pl.when(step == pl.num_programs(0) - 1)
    def _():
        for k in range(blocks):
            block = pl.ds(k * rows, rows)
            kv_out[k] = kv_acc[block, :].astype(bf16)
            for h in range(q_acc.shape[1] // HD):
                q_out[k, pl.ds(h * rows, rows), :] = q_acc[block, pl.ds(h * HD, HD)].astype(bf16)


def project(cols, w_query, w_key, w_value):
    blocks, parts, rows, feats = cols.shape
    q_width, kv_width = w_query.shape[2], 2 * w_key.shape[2]
    heads = q_width // HD
    kv_spec = pl.BlockSpec((None, w_key.shape[2], feats), lambda z: (0, 0, z))
    return pl.pallas_call(
        project_kernel,
        grid=(parts,),
        in_specs=[
            pl.BlockSpec((blocks, None, rows, feats), lambda z: (0, z, 0, 0)),
            pl.BlockSpec((None, feats, q_width), lambda z: (0, z, 0)),
            kv_spec,
            kv_spec,
        ],
        out_specs=[
            pl.BlockSpec((blocks, heads * rows, HD), lambda z: (0, 0, 0)),
            pl.BlockSpec((blocks, rows, kv_width), lambda z: (0, 0, 0)),
        ],
        out_shape=[
            jax.ShapeDtypeStruct((blocks, heads * rows, HD), bf16),
            jax.ShapeDtypeStruct((blocks, rows, kv_width), bf16),
        ],
        scratch_shapes=[
            pltpu.VMEM((blocks * rows, q_width), f32),
            pltpu.VMEM((blocks * rows, kv_width), f32),
        ],
        compiler_params=pltpu.CompilerParams(vmem_limit_bytes=LIMIT),
        name="project",
    )(cols, w_query, w_key.swapaxes(1, 2), w_value.swapaxes(1, 2))


def rotate(values, cosine, sine):
    return values * cosine + pltpu.roll(values, HD // 2, 1) * sine


def attend_kernel(
    place, q_in, kv_in, r_own, r_all, docs_own, docs_all, cos_own, sin_own, cos_all, sin_all,
    resid, out, keys, values,
):
    rows = out.shape[0]
    tokens = keys.shape[0]

    @pl.when(pl.program_id(0) == 0)
    def _():
        lower = lax.broadcasted_iota(jnp.int32, (rows, HD), 1) < HD // 2
        for k in range(tokens // rows):
            first = kv_in[2 * k].astype(f32)
            second = kv_in[2 * k + 1].astype(f32)
            block = pl.ds(k * rows, rows)
            key = jnp.where(lower, first, pltpu.roll(second, HD // 2, 1))
            keys[block, :] = rotate(key, cos_all[block, :], sin_all[block, :])
            values[block, :] = jnp.where(lower, pltpu.roll(first, HD // 2, 1), second)

    query = jnp.sum(q_in[...].astype(f32), axis=0)
    query = rotate(query, cos_own[...], sin_own[...]) * r_own[...]
    scores = lax.dot_general(
        query, keys[...], (((1,), (1,)), ((), ())),
        preferred_element_type=f32, precision=lax.Precision.HIGHEST,
    )
    scores = scores * r_all[...]
    key_ids = lax.broadcasted_iota(jnp.int32, scores.shape, 1)
    own_ids = lax.broadcasted_iota(jnp.int32, scores.shape, 0) + place[0] * rows
    allowed = (key_ids <= own_ids) & (docs_all[...] == docs_own[...])
    scores = jnp.where(allowed, scores, f32(-1e30))
    peak = jnp.max(scores, axis=-1, keepdims=True)
    weights = jnp.where(allowed, jnp.exp(scores - peak), f32(0.0))
    total = jnp.sum(weights, axis=-1, keepdims=True)
    context = jnp.dot(
        weights * r_all[...], values[...],
        preferred_element_type=f32, precision=lax.Precision.HIGHEST,
    ) / total
    out[...] = (resid[...].astype(f32) + context).astype(bf16)


def attend(place, q_in, kv_in, r_own, r_all, docs_own, docs_all, tables_own, tables_all, resid):
    rows, feats = resid.shape
    tokens = r_all.shape[1]
    whole = pl.BlockSpec(memory_space=pltpu.VMEM)
    return pl.pallas_call(
        attend_kernel,
        grid=(feats // HD,),
        in_specs=[
            pl.BlockSpec(memory_space=pltpu.SMEM),
            pl.BlockSpec((q_in.shape[0], rows, HD), lambda h: (0, h, 0)),
        ]
        + [whole] * 9
        + [pl.BlockSpec((rows, HD), lambda h: (0, h))],
        out_specs=pl.BlockSpec((rows, HD), lambda h: (0, h)),
        out_shape=jax.ShapeDtypeStruct((rows, feats), bf16),
        scratch_shapes=[pltpu.VMEM((tokens, HD), f32), pltpu.VMEM((tokens, HD), f32)],
        compiler_params=pltpu.CompilerParams(vmem_limit_bytes=LIMIT),
        name="attend",
    )(place, q_in, kv_in, r_own, r_all, docs_own, docs_all, *tables_own, *tables_all, resid)


def product(left, cols):
    blocks, rows, feats = cols.shape
    return jnp.dot(left[...], cols[...].reshape(blocks * rows, feats), preferred_element_type=f32)


def upper_kernel(place, left, cols, out):
    @pl.when(place[1] <= place[2] + pl.program_id(0))
    def _():
        out[...] = product(left, cols).astype(bf16)


def lower_kernel(place, left, cols, upper, out):
    row, col = place[1], place[2] + pl.program_id(0)

    @pl.when(row < col)
    def _():
        out[...] = upper[...]

    @pl.when(row > col)
    def _():
        out[...] = product(left, cols).astype(bf16)

    @pl.when(row == col)
    def _():
        lower = product(left, cols).astype(bf16)
        row_ids = lax.broadcasted_iota(jnp.int32, lower.shape, 0)
        col_ids = lax.broadcasted_iota(jnp.int32, lower.shape, 1)
        out[...] = jnp.where(row_ids <= col_ids, upper[...], lower)


def hessian(kernel, place, left, cols, *upper):
    blocks, parts, rows, feats = cols.shape
    tile = pl.BlockSpec((feats, feats), lambda z: (0, z))
    return pl.pallas_call(
        kernel,
        grid=(parts,),
        in_specs=[
            pl.BlockSpec(memory_space=pltpu.SMEM),
            pl.BlockSpec((feats, blocks * rows), lambda z: (0, 0)),
            pl.BlockSpec((blocks, None, rows, feats), lambda z: (0, z, 0, 0)),
        ]
        + [tile] * len(upper),
        out_specs=tile,
        out_shape=jax.ShapeDtypeStruct((feats, parts * feats), bf16),
        compiler_params=pltpu.CompilerParams(vmem_limit_bytes=LIMIT),
        name="hessian",
    )(place, left, cols, *upper)


def on_device(hidden, segment_ids, gain_attn, gain_ffn, w_query, w_key, w_value):
    x_pos = lax.axis_index("x")
    zl_pos = lax.axis_index(ZL)
    seq_pos = lax.axis_index("seq")
    nx, nz, ns = lax.axis_size("x"), lax.axis_size(ZL), lax.axis_size("seq")
    rows, feats = hidden.shape[1:]
    tokens = rows * ns
    width = feats * nx * nz
    scale = 2.0 / tokens
    place = jnp.stack([x_pos, x_pos * nz + zl_pos, seq_pos * nz]).astype(jnp.int32)

    resid = swap_x_seq(hidden[0])
    gains = spread(jnp.concatenate([gain_attn, gain_ffn]), TENSOR)
    gains = lax.dynamic_slice_in_dim(gains.astype(f32), seq_pos * nz, nz, 0)

    def columns(block, gain):
        group = spread(block, ZL).astype(f32)
        cols = spread((group * gain[:, None, :]).astype(bf16), "x")
        small = jnp.stack([jnp.sum(group * group, axis=(0, 2)), segment_ids[0].astype(f32)])
        small = spread(small, ("x", "seq")).reshape(nx, ns, 2, rows)
        total = jnp.sum(small[:, :, 0], axis=1).reshape(tokens)
        return cols, lax.rsqrt(total / width + norm_eps), small[0, :, 1].reshape(tokens)

    def left_side(blocks, gain, r):
        left = blocks.astype(f32).reshape(tokens, feats) * (r * r * scale)[:, None]
        return (left * gain.astype(f32)).astype(bf16).T

    attn_cols, r_attn, docs = columns(resid, gains[:, 0])
    q_part, kv_part = project(attn_cols, w_query, w_key, w_value)
    kv = lax.all_to_all(lax.all_to_all(kv_part, "x", 0, 0), "seq", 0, 0)
    kv = spread(jnp.sum(kv.astype(f32), axis=0).astype(bf16), ("x", "zb"))
    query = lax.all_to_all(lax.all_to_all(q_part, "x", 0, 0), "seq", 0, 0)

    half = HD // 2
    freq = rope_base ** (-(jnp.arange(half, dtype=f32) * 2.0 / HD))
    angle = jnp.arange(tokens, dtype=f32)[:, None] * freq[None, :]
    cosine, sine = jnp.cos(angle), jnp.sin(angle)
    tables = (jnp.concatenate([cosine] * 2, 1), jnp.concatenate([-sine, sine], 1))
    own = functools.partial(lax.dynamic_slice_in_dim, start_index=x_pos * rows, slice_size=rows)
    inv_root = 1.0 / jnp.sqrt(f32(HD))
    section_out = attend(
        place,
        query,
        kv,
        own(r_attn * inv_root)[:, None],
        r_attn[None],
        own(docs)[:, None],
        docs[None],
        tuple(own(t) for t in tables),
        tables,
        resid,
    )
    attn_rows = spread(hidden[0], "seq")
    attn_left = left_side(attn_rows, gain_attn, r_attn)
    upper = hessian(upper_kernel, place, attn_left, attn_cols)

    passed = swap_and_pass(section_out)[None]
    ffn_cols, r_ffn, _ = columns(section_out, gains[:, 1])
    ffn_rows = lax.all_to_all(spread(section_out, "seq"), "x", 0, 0)
    ffn_left = left_side(ffn_rows, gain_ffn, r_ffn)
    hessians = hessian(lower_kernel, place, ffn_left, ffn_cols, upper)[None]
    diag_width = feats // ns
    own_cols = lax.dynamic_slice_in_dim(
        ffn_rows.reshape(tokens, feats), seq_pos * diag_width, diag_width, 1
    ).astype(f32)
    own_gain = lax.dynamic_slice_in_dim(gain_ffn[0], seq_pos * diag_width, diag_width)
    own_cols = own_cols * r_ffn[:, None] * own_gain.astype(f32)
    ffn_diagonal = (jnp.sum(own_cols * own_cols, axis=0) * scale)[None]
    return (passed, hessians, ffn_diagonal)


def solution(mesh):
    phase, tensor, seq = (mesh.shape[a] for a in ("phase", "tensor", "seq"))
    lines = Mesh(
        mesh.devices.reshape(phase, tensor // 4, 2, 2, seq), ("phase", "x", "za", "zb", "seq")
    )
    tiled = P("phase", "seq", TENSOR)
    return jax.shard_map(
        on_device,
        mesh=lines,
        in_specs=(
            tiled,
            P("phase", "seq"),
            P("phase", TENSOR),
            P("phase", TENSOR),
            tiled,
            tiled,
            tiled,
        ),
        out_specs=(tiled, P("phase", TENSOR, "seq"), P("phase", GROUP)),
        check_vma=False,
    )
```

```python
import jax
import jax.numpy as jnp
from jax import lax
from jax.experimental import pallas as pl
from jax.experimental.pallas import tpu as pltpu
from jax.sharding import Mesh, PartitionSpec as P

HD = 128
norm_eps = 1e-05
rope_base = 500000.0
ZL = ("za", "zb")
TENSOR = ("x", "za", "zb")
GROUP = TENSOR + ("seq",)
f32 = jnp.float32
bf16 = jnp.bfloat16
LIMIT = 24 * 1024 * 1024


def swap_x_seq(value):
    nx, nz, ns = lax.axis_size("x"), lax.axis_size(ZL), lax.axis_size("seq")
    pairs = [
        ((x * nz + z) * ns + s, (s * nz + z) * ns + x)
        for x in range(nx)
        for z in range(nz)
        for s in range(ns)
    ]
    return lax.ppermute(value, GROUP, pairs)


def three_parts(value):
    parts = []
    for _ in range(3):
        part = lax.reduce_precision(value, 8, 7)
        parts.append(part.astype(bf16))
        value = value - part
    return jnp.stack(parts)


def pad_to(rows, count, width):
    return jnp.pad(rows, ((0, count - rows.shape[0]), (0, width - rows.shape[1])))


def project_kernel(cols, gain, wq, wk, wv, out, q_acc, kv_acc):
    step = pl.program_id(0)
    blocks, rows, feats = cols.shape
    left = (cols[...].reshape(blocks * rows, feats).astype(f32) * gain[...]).astype(bf16)
    kv_w = jnp.concatenate([wk[...], wv[...]], 0)
    kv = lax.dot_general(left, kv_w, (((1,), (1,)), ((), ())), preferred_element_type=f32)
    q = jnp.dot(left, wq[...], preferred_element_type=f32)

    @pl.when(step == 0)
    def _():
        q_acc[...] = q
        kv_acc[...] = kv

    @pl.when(step > 0)
    def _():
        q_acc[...] += q
        kv_acc[...] += kv

    @pl.when(step == pl.num_programs(0) - 1)
    def _():
        heads = q_acc.shape[1] // HD
        for k in range(blocks):
            block = pl.ds(k * rows, rows)
            out[k, pl.ds(heads * rows, rows), :] = kv_acc[block, :].astype(bf16)
            for h in range(heads):
                out[k, pl.ds(h * rows, rows), :] = q_acc[block, pl.ds(h * HD, HD)].astype(bf16)


def project(cols, gain, w_query, w_key, w_value):
    blocks, parts, rows, feats = cols.shape
    q_width, kv_width = w_query.shape[2], 2 * w_key.shape[2]
    heads = q_width // HD
    kv_spec = pl.BlockSpec((None, w_key.shape[2], feats), lambda z: (0, 0, z))
    return pl.pallas_call(
        project_kernel,
        grid=(parts,),
        in_specs=[
            pl.BlockSpec((blocks, None, rows, feats), lambda z: (0, z, 0, 0)),
            pl.BlockSpec((None, 1, feats), lambda z: (z, 0, 0)),
            pl.BlockSpec((None, feats, q_width), lambda z: (0, z, 0)),
            kv_spec,
            kv_spec,
        ],
        out_specs=pl.BlockSpec((blocks, (heads + 1) * rows, HD), lambda z: (0, 0, 0)),
        out_shape=jax.ShapeDtypeStruct((blocks, (heads + 1) * rows, HD), bf16),
        scratch_shapes=[
            pltpu.VMEM((blocks * rows, q_width), f32),
            pltpu.VMEM((blocks * rows, kv_width), f32),
        ],
        compiler_params=pltpu.CompilerParams(vmem_limit_bytes=LIMIT),
        name="project",
    )(cols, gain, w_query, w_key.swapaxes(1, 2), w_value.swapaxes(1, 2))


def rotate(values, cosine, sine):
    return values * cosine + pltpu.roll(values, HD // 2, 1) * sine


def column_of(row):
    n = row.shape[1]
    same = lax.broadcasted_iota(jnp.int32, (n, n), 0) == lax.broadcasted_iota(jnp.int32, (n, n), 1)
    return jnp.sum(jnp.where(same, row, f32(0.0)), axis=1, keepdims=True)


def attend_kernel(
    place, q_in, kv_in, cos_own, sin_own, cos_all, sin_all, resid, copies, out,
    keys, values, r_all, docs_all, r_own, docs_own,
):
    rows = out.shape[0]
    tokens = keys.shape[0]

    @pl.when(pl.program_id(0) == 0)
    def _():
        lower = lax.broadcasted_iota(jnp.int32, (rows, HD), 1) < HD // 2
        for k in range(tokens // rows):
            first = kv_in[2 * k, pl.ds(0, rows), :].astype(f32)
            second = kv_in[2 * k + 1, pl.ds(0, rows), :].astype(f32)
            tail = kv_in[2 * k, pl.ds(rows, 16), :].astype(f32)
            block = pl.ds(k * rows, rows)
            key = jnp.where(lower, first, pltpu.roll(second, HD // 2, 1))
            keys[block, :] = rotate(key, cos_all[block, :], sin_all[block, :])
            values[block, :] = jnp.where(lower, pltpu.roll(first, HD // 2, 1), second)
            r = tail[0:1] + tail[1:2] + tail[2:3]
            r_all[:, block] = r
            docs_all[:, block] = tail[3:4]

            @pl.when(place[0] == k)
            def _():
                r_own[...] = column_of(r) * (1.0 / HD**0.5)
                docs_own[...] = column_of(tail[3:4])

    query = jnp.sum(q_in[...].astype(f32), axis=0)
    query = rotate(query, cos_own[...], sin_own[...]) * r_own[...]
    scores = lax.dot_general(
        query, keys[...], (((1,), (1,)), ((), ())),
        preferred_element_type=f32, precision=lax.Precision.HIGHEST,
    )
    scores = scores * r_all[...]
    key_ids = lax.broadcasted_iota(jnp.int32, scores.shape, 1)
    own_ids = lax.broadcasted_iota(jnp.int32, scores.shape, 0) + place[0] * rows
    allowed = (key_ids <= own_ids) & (docs_all[...] == docs_own[...])
    scores = jnp.where(allowed, scores, f32(-1e30))
    peak = jnp.max(scores, axis=-1, keepdims=True)
    weights = jnp.where(allowed, jnp.exp(scores - peak), f32(0.0))
    total = jnp.sum(weights, axis=-1, keepdims=True)
    context = jnp.dot(
        weights * r_all[...], values[...],
        preferred_element_type=f32, precision=lax.Precision.HIGHEST,
    ) / total
    result = (resid[...].astype(f32) + context).astype(bf16)
    out[...] = result
    for copy in range(copies.shape[0]):
        copies[copy] = result


def attend(place, q_in, kv_in, tables_own, tables_all, resid, copies):
    heads = q_in.shape[1] // HD - 1
    rows, feats, tokens = q_in.shape[1] // (heads + 1), heads * HD, tables_all[0].shape[0]
    whole = pl.BlockSpec(memory_space=pltpu.VMEM)
    return pl.pallas_call(
        attend_kernel,
        grid=(heads,),
        in_specs=[
            pl.BlockSpec(memory_space=pltpu.SMEM),
            pl.BlockSpec((q_in.shape[0], rows, HD), lambda h: (0, h, 0)),
        ]
        + [whole] * 5
        + [pl.BlockSpec((rows, HD), lambda h: (0, h))],
        out_specs=[
            pl.BlockSpec((copies, rows, HD), lambda h: (0, 0, h)),
            pl.BlockSpec((rows, HD), lambda h: (0, h)),
        ],
        out_shape=[
            jax.ShapeDtypeStruct((copies, rows, feats), bf16),
            jax.ShapeDtypeStruct((rows, feats), bf16),
        ],
        scratch_shapes=[
            pltpu.VMEM((tokens, HD), f32),
            pltpu.VMEM((tokens, HD), f32),
            pltpu.VMEM((1, tokens), f32),
            pltpu.VMEM((1, tokens), f32),
            pltpu.VMEM((rows, 1), f32),
            pltpu.VMEM((rows, 1), f32),
        ],
        compiler_params=pltpu.CompilerParams(vmem_limit_bytes=LIMIT),
        name="attend",
    )(place, q_in, kv_in, *tables_own, *tables_all, resid)


def product(left, cols, gain):
    blocks, rows, feats = cols.shape
    right = cols[...].reshape(blocks * rows, feats)
    return (jnp.dot(left[...], right, preferred_element_type=f32) * gain[...]).astype(bf16)


def upper_kernel(place, left, cols, gain, out):
    @pl.when(place[1] <= place[2] + pl.program_id(0))
    def _():
        out[...] = product(left, cols, gain)


def lower_kernel(place, left, cols, gain, upper, out):
    row, col = place[1], place[2] + pl.program_id(0)

    @pl.when(row < col)
    def _():
        out[...] = upper[...]

    @pl.when(row > col)
    def _():
        out[...] = product(left, cols, gain)

    @pl.when(row == col)
    def _():
        lower = product(left, cols, gain)
        row_ids = lax.broadcasted_iota(jnp.int32, lower.shape, 0)
        col_ids = lax.broadcasted_iota(jnp.int32, lower.shape, 1)
        out[...] = jnp.where(row_ids <= col_ids, upper[...], lower)


def hessian(kernel, place, left, cols, gain, *upper):
    blocks, parts, rows, feats = cols.shape
    tile = pl.BlockSpec((feats, feats), lambda z: (0, z))
    return pl.pallas_call(
        kernel,
        grid=(parts,),
        in_specs=[
            pl.BlockSpec(memory_space=pltpu.SMEM),
            pl.BlockSpec((feats, blocks * rows), lambda z: (0, 0)),
            pl.BlockSpec((blocks, None, rows, feats), lambda z: (0, z, 0, 0)),
            pl.BlockSpec((None, 1, feats), lambda z: (z, 0, 0)),
        ]
        + [tile] * len(upper),
        out_specs=tile,
        out_shape=jax.ShapeDtypeStruct((feats, parts * feats), bf16),
        compiler_params=pltpu.CompilerParams(vmem_limit_bytes=LIMIT),
        name="hessian",
    )(place, left, cols, gain, *upper)


def on_device(hidden, segment_ids, gain_attn, gain_ffn, w_query, w_key, w_value):
    x_pos = lax.axis_index("x")
    zl_pos = lax.axis_index(ZL)
    seq_pos = lax.axis_index("seq")
    nx, nz, ns = lax.axis_size("x"), lax.axis_size(ZL), lax.axis_size("seq")
    rows, feats = hidden.shape[1:]
    tokens = rows * ns
    width = feats * nx * nz
    scale = 2.0 / tokens
    place = jnp.stack([x_pos, x_pos * nz + zl_pos, seq_pos * nz]).astype(jnp.int32)

    def copied(value, count):
        return jnp.broadcast_to(value[None], (count,) + value.shape)

    def square_rows(group):
        group = group.astype(f32)
        return pad_to(three_parts(jnp.sum(group * group, axis=(0, 2))), 16, feats)

    def r_of(parts):
        return lax.rsqrt(jnp.sum(parts.astype(f32), axis=(0, 1)) / width + norm_eps)

    def left_side(blocks, gain, r):
        left = blocks.astype(f32).reshape(tokens, feats) * (r * r * scale)[:, None]
        return (left * gain.astype(f32)).astype(bf16).T

    resid = swap_x_seq(hidden[0])
    extra = swap_x_seq(
        pad_to(
            jnp.concatenate([gain_attn, gain_ffn, pad_to(segment_ids.astype(bf16), 1, feats)]),
            16,
            feats,
        )
    )
    group = lax.all_to_all(copied(jnp.concatenate([resid, extra]), nz), ZL, 0, 0)
    gain_a = group[:, rows : rows + 1].astype(f32)
    gain_f = group[:, rows + 1 : rows + 2].astype(f32)
    docs_own = extra[2, :rows]
    group = group[:, :rows]
    attn_cols = lax.all_to_all(copied(group, nx), "x", 0, 0)
    attn_rows = lax.all_gather(jnp.concatenate([hidden[0], square_rows(group)]), "seq")
    r_own = r_of(attn_rows[:, rows : rows + 3, :rows])
    tail = jnp.concatenate([three_parts(r_own), docs_own[None]])
    tail = pad_to(tail, 16, HD)

    message = project(attn_cols, gain_a, w_query, w_key, w_value)
    message = lax.all_to_all(message, "x", 0, 0)
    arrived = lax.all_to_all(message, "seq", 0, 0)
    heads = feats // HD
    kv = jnp.sum(arrived[:, heads * rows :].astype(f32), axis=0).astype(bf16)
    kv_all = lax.all_to_all(copied(jnp.concatenate([kv, tail]), 2 * nx), ("x", "zb"), 0, 0)

    half = HD // 2
    freq = rope_base ** (-(jnp.arange(half, dtype=f32) * 2.0 / HD))
    angle = jnp.arange(tokens, dtype=f32)[:, None] * freq[None, :]
    cosine, sine = jnp.cos(angle), jnp.sin(angle)
    tables = (jnp.concatenate([cosine] * 2, 1), jnp.concatenate([-sine, sine], 1))
    own = tuple(lax.dynamic_slice_in_dim(t, x_pos * rows, rows) for t in tables)
    copies, section_out = attend(place, arrived, kv_all, own, tables, resid, nz)

    r_attn = jnp.sum(
        kv_all.reshape(nx, 2, rows + 16, HD)[:, 0, rows : rows + 3].astype(f32), axis=1
    ).reshape(tokens)
    attn_left = left_side(attn_rows[:, :rows], gain_attn, r_attn)
    upper = hessian(upper_kernel, place, attn_left, attn_cols, gain_a)

    group = lax.all_to_all(copies, ZL, 0, 0)
    out_rows = swap_x_seq(section_out)
    count = lax.axis_size("phase")
    passed = lax.ppermute(out_rows, "phase", [(p, (p + 1) % count) for p in range(count)])[None]
    ffn_cols = lax.all_to_all(copied(group, nx), "x", 0, 0)
    ffn_rows = lax.all_gather(jnp.concatenate([out_rows, square_rows(group)]), "seq")
    r_ffn = lax.all_gather(r_of(ffn_rows[:, rows : rows + 3, :rows]), "x", tiled=True)
    ffn_rows = ffn_rows[:, :rows]
    ffn_left = left_side(ffn_rows, gain_ffn, r_ffn)
    hessians = hessian(lower_kernel, place, ffn_left, ffn_cols, gain_f, upper)[None]
    diag_width = feats // ns
    own_cols = lax.dynamic_slice_in_dim(
        ffn_rows.reshape(tokens, feats), seq_pos * diag_width, diag_width, 1
    ).astype(f32)
    own_gain = lax.dynamic_slice_in_dim(gain_ffn[0], seq_pos * diag_width, diag_width)
    own_cols = own_cols * r_ffn[:, None] * own_gain.astype(f32)
    ffn_diagonal = (jnp.sum(own_cols * own_cols, axis=0) * scale)[None]
    return (passed, hessians, ffn_diagonal)


def solution(mesh):
    phase, tensor, seq = (mesh.shape[a] for a in ("phase", "tensor", "seq"))
    lines = Mesh(
        mesh.devices.reshape(phase, tensor // 4, 2, 2, seq), ("phase", "x", "za", "zb", "seq")
    )
    tiled = P("phase", "seq", TENSOR)
    return jax.shard_map(
        on_device,
        mesh=lines,
        in_specs=(
            tiled,
            P("phase", "seq"),
            P("phase", TENSOR),
            P("phase", TENSOR),
            tiled,
            tiled,
            tiled,
        ),
        out_specs=(tiled, P("phase", TENSOR, "seq"), P("phase", GROUP)),
        check_vma=False,
    )
```

```python
import jax
import jax.numpy as jnp
from jax import lax
from jax.experimental import pallas as pl
from jax.experimental.pallas import tpu as pltpu
from jax.sharding import Mesh, PartitionSpec as P

HD = 128
norm_eps = 1e-05
rope_base = 500000.0
ZL = ("za", "zb")
TENSOR = ("x", "za", "zb")
GROUP = TENSOR + ("seq",)
f32 = jnp.float32
bf16 = jnp.bfloat16
LIMIT = 24 * 1024 * 1024


def swap_x_seq(value):
    nx, nz, ns = lax.axis_size("x"), lax.axis_size(ZL), lax.axis_size("seq")
    pairs = [
        ((x * nz + z) * ns + s, (s * nz + z) * ns + x)
        for x in range(nx)
        for z in range(nz)
        for s in range(ns)
    ]
    return lax.ppermute(value, GROUP, pairs)


def three_parts(value):
    parts = []
    for _ in range(3):
        part = lax.reduce_precision(value, 8, 7)
        parts.append(part.astype(bf16))
        value = value - part
    return jnp.stack(parts)


def pad_to(rows, count, width):
    return jnp.pad(rows, ((0, count - rows.shape[0]), (0, width - rows.shape[1])))


def project_kernel(cols, gain, wq, wk, wv, after, out, q_acc, kv_acc):
    step = pl.program_id(0)
    blocks, rows, feats = cols.shape
    left = (cols[...].reshape(blocks * rows, feats).astype(f32) * gain[...]).astype(bf16)
    kv_w = jnp.concatenate([wk[...], wv[...]], 0)
    kv = lax.dot_general(left, kv_w, (((1,), (1,)), ((), ())), preferred_element_type=f32)
    q = jnp.dot(left, wq[...], preferred_element_type=f32)

    @pl.when(step == 0)
    def _():
        q_acc[...] = q
        kv_acc[...] = kv

    @pl.when(step > 0)
    def _():
        q_acc[...] += q
        kv_acc[...] += kv

    @pl.when(step == pl.num_programs(0) - 1)
    def _():
        heads = q_acc.shape[1] // HD
        for k in range(blocks):
            block = pl.ds(k * rows, rows)
            out[k, pl.ds(heads * rows, rows), :] = kv_acc[block, :].astype(bf16)
            for h in range(heads):
                out[k, pl.ds(h * rows, rows), :] = q_acc[block, pl.ds(h * HD, HD)].astype(bf16)


def project(cols, gain, w_query, w_key, w_value, after):
    blocks, parts, rows, feats = cols.shape
    q_width, kv_width = w_query.shape[2], 2 * w_key.shape[2]
    heads = q_width // HD
    kv_spec = pl.BlockSpec((None, w_key.shape[2], feats), lambda z: (0, 0, z))
    return pl.pallas_call(
        project_kernel,
        grid=(parts,),
        in_specs=[
            pl.BlockSpec((blocks, None, rows, feats), lambda z: (0, z, 0, 0)),
            pl.BlockSpec((None, 1, feats), lambda z: (z, 0, 0)),
            pl.BlockSpec((None, feats, q_width), lambda z: (0, z, 0)),
            kv_spec,
            kv_spec,
            pl.BlockSpec(memory_space=pl.ANY),
        ],
        out_specs=pl.BlockSpec((blocks, (heads + 1) * rows, HD), lambda z: (0, 0, 0)),
        out_shape=jax.ShapeDtypeStruct((blocks, (heads + 1) * rows, HD), bf16),
        scratch_shapes=[
            pltpu.VMEM((blocks * rows, q_width), f32),
            pltpu.VMEM((blocks * rows, kv_width), f32),
        ],
        compiler_params=pltpu.CompilerParams(vmem_limit_bytes=LIMIT),
        name="project",
    )(cols, gain, w_query, w_key.swapaxes(1, 2), w_value.swapaxes(1, 2), after)


def take_kernel(value, after, out):
    out[...] = value[...]


def take_after(value, count, after):
    shape = (value.shape[0], count, value.shape[2])
    spec = pl.BlockSpec((1, count, value.shape[2]), lambda i: (i, 0, 0))
    return pl.pallas_call(
        take_kernel,
        grid=(value.shape[0],),
        in_specs=[spec, pl.BlockSpec(memory_space=pl.ANY)],
        out_specs=spec,
        out_shape=jax.ShapeDtypeStruct(shape, value.dtype),
        compiler_params=pltpu.CompilerParams(vmem_limit_bytes=LIMIT),
        name="take_after",
    )(value, after)


def rotate(values, cosine, sine):
    return values * cosine + pltpu.roll(values, HD // 2, 1) * sine


def column_of(row):
    n = row.shape[1]
    same = lax.broadcasted_iota(jnp.int32, (n, n), 0) == lax.broadcasted_iota(jnp.int32, (n, n), 1)
    return jnp.sum(jnp.where(same, row, f32(0.0)), axis=1, keepdims=True)


def attend_kernel(
    place, q_in, kv_own, kv_other, cos_own, sin_own, cos_all, sin_all, resid, copies, out,
    keys, values, r_all, docs_all, r_own, docs_own,
):
    rows = out.shape[0]
    tokens = keys.shape[0]

    @pl.when(pl.program_id(0) == 0)
    def _():
        lower = lax.broadcasted_iota(jnp.int32, (rows, HD), 1) < HD // 2
        for k in range(tokens // rows):
            mine = kv_own[k, pl.ds(0, rows), :].astype(f32)
            other = kv_other[k].astype(f32)
            first = jnp.where(place[3] == 0, mine, other)
            second = jnp.where(place[3] == 0, other, mine)
            tail = kv_own[k, pl.ds(rows, 16), :].astype(f32)
            block = pl.ds(k * rows, rows)
            key = jnp.where(lower, first, pltpu.roll(second, HD // 2, 1))
            keys[block, :] = rotate(key, cos_all[block, :], sin_all[block, :])
            values[block, :] = jnp.where(lower, pltpu.roll(first, HD // 2, 1), second)
            r = tail[0:1] + tail[1:2] + tail[2:3]
            r_all[:, block] = r
            docs_all[:, block] = tail[3:4]

            @pl.when(place[0] == k)
            def _():
                r_own[...] = column_of(r) * (1.0 / HD**0.5)
                docs_own[...] = column_of(tail[3:4])

    query = jnp.sum(q_in[...].astype(f32), axis=0)
    query = rotate(query, cos_own[...], sin_own[...]) * r_own[...]
    scores = lax.dot_general(
        query, keys[...], (((1,), (1,)), ((), ())),
        preferred_element_type=f32, precision=lax.Precision.HIGHEST,
    )
    scores = scores * r_all[...]
    key_ids = lax.broadcasted_iota(jnp.int32, scores.shape, 1)
    own_ids = lax.broadcasted_iota(jnp.int32, scores.shape, 0) + place[0] * rows
    allowed = (key_ids <= own_ids) & (docs_all[...] == docs_own[...])
    scores = jnp.where(allowed, scores, f32(-1e30))
    peak = jnp.max(scores, axis=-1, keepdims=True)
    weights = jnp.where(allowed, jnp.exp(scores - peak), f32(0.0))
    total = jnp.sum(weights, axis=-1, keepdims=True)
    context = jnp.dot(
        weights * r_all[...], values[...],
        preferred_element_type=f32, precision=lax.Precision.HIGHEST,
    ) / total
    result = (resid[...].astype(f32) + context).astype(bf16)
    out[...] = result
    for copy in range(copies.shape[0]):
        copies[copy] = result


def attend(place, q_in, kv_own, kv_other, tables_own, tables_all, resid, copies):
    rows, feats = resid.shape
    heads, tokens = feats // HD, tables_all[0].shape[0]
    whole = pl.BlockSpec(memory_space=pltpu.VMEM)
    return pl.pallas_call(
        attend_kernel,
        grid=(heads,),
        in_specs=[
            pl.BlockSpec(memory_space=pltpu.SMEM),
            pl.BlockSpec((q_in.shape[0], rows, HD), lambda h: (0, h, 0)),
        ]
        + [whole] * 6
        + [pl.BlockSpec((rows, HD), lambda h: (0, h))],
        out_specs=[
            pl.BlockSpec((copies, rows, HD), lambda h: (0, 0, h)),
            pl.BlockSpec((rows, HD), lambda h: (0, h)),
        ],
        out_shape=[
            jax.ShapeDtypeStruct((copies, rows, feats), bf16),
            jax.ShapeDtypeStruct((rows, feats), bf16),
        ],
        scratch_shapes=[
            pltpu.VMEM((tokens, HD), f32),
            pltpu.VMEM((tokens, HD), f32),
            pltpu.VMEM((1, tokens), f32),
            pltpu.VMEM((1, tokens), f32),
            pltpu.VMEM((rows, 1), f32),
            pltpu.VMEM((rows, 1), f32),
        ],
        compiler_params=pltpu.CompilerParams(vmem_limit_bytes=LIMIT),
        name="attend",
    )(place, q_in, kv_own, kv_other, *tables_own, *tables_all, resid)


def product(left, cols, gain):
    blocks, rows, feats = cols.shape
    right = cols[...].reshape(blocks * rows, feats)
    return (jnp.dot(left[...], right, preferred_element_type=f32) * gain[...]).astype(bf16)


def upper_kernel(place, left, cols, gain, out):
    @pl.when(place[1] <= place[2] + pl.program_id(0))
    def _():
        out[...] = product(left, cols, gain)


def lower_kernel(place, left, cols, gain, upper, out):
    row, col = place[1], place[2] + pl.program_id(0)

    @pl.when(row < col)
    def _():
        out[...] = upper[...]

    @pl.when(row > col)
    def _():
        out[...] = product(left, cols, gain)

    @pl.when(row == col)
    def _():
        lower = product(left, cols, gain)
        row_ids = lax.broadcasted_iota(jnp.int32, lower.shape, 0)
        col_ids = lax.broadcasted_iota(jnp.int32, lower.shape, 1)
        out[...] = jnp.where(row_ids <= col_ids, upper[...], lower)


def hessian(kernel, place, left, cols, gain, *upper):
    blocks, parts, rows, feats = cols.shape
    tile = pl.BlockSpec((feats, feats), lambda z: (0, z))
    return pl.pallas_call(
        kernel,
        grid=(parts,),
        in_specs=[
            pl.BlockSpec(memory_space=pltpu.SMEM),
            pl.BlockSpec((feats, blocks * rows), lambda z: (0, 0)),
            pl.BlockSpec((blocks, None, rows, feats), lambda z: (0, z, 0, 0)),
            pl.BlockSpec((None, 1, feats), lambda z: (z, 0, 0)),
        ]
        + [tile] * len(upper),
        out_specs=tile,
        out_shape=jax.ShapeDtypeStruct((feats, parts * feats), bf16),
        compiler_params=pltpu.CompilerParams(vmem_limit_bytes=LIMIT),
        name="hessian",
    )(place, left, cols, gain, *upper)


def on_device(hidden, segment_ids, gain_attn, gain_ffn, w_query, w_key, w_value):
    x_pos = lax.axis_index("x")
    zl_pos = lax.axis_index(ZL)
    seq_pos = lax.axis_index("seq")
    nx, nz, ns = lax.axis_size("x"), lax.axis_size(ZL), lax.axis_size("seq")
    rows, feats = hidden.shape[1:]
    tokens = rows * ns
    width = feats * nx * nz
    scale = 2.0 / tokens
    zb_pos = lax.axis_index("zb")
    place = jnp.stack([x_pos, x_pos * nz + zl_pos, seq_pos * nz, zb_pos]).astype(jnp.int32)

    def copied(value, count):
        return jnp.broadcast_to(value[None], (count,) + value.shape)

    def square_rows(group):
        group = group.astype(f32)
        return pad_to(three_parts(jnp.sum(group * group, axis=(0, 2))), 16, feats)

    def r_of(parts):
        return lax.rsqrt(jnp.sum(parts.astype(f32), axis=(0, 1)) / width + norm_eps)

    def left_side(blocks, gain, r):
        left = blocks.astype(f32).reshape(tokens, feats) * (r * r * scale)[:, None]
        return (left * gain.astype(f32)).astype(bf16).T

    resid = swap_x_seq(hidden[0])
    extra = swap_x_seq(
        pad_to(
            jnp.concatenate([gain_attn, gain_ffn, pad_to(segment_ids.astype(bf16), 1, feats)]),
            16,
            feats,
        )
    )
    group = lax.all_to_all(copied(jnp.concatenate([resid, extra]), nz), ZL, 0, 0)
    gain_a = group[:, rows : rows + 1].astype(f32)
    gain_f = group[:, rows + 1 : rows + 2].astype(f32)
    docs_own = extra[2, :rows]
    group = group[:, :rows]
    attn_cols = lax.all_to_all(copied(group, nx), "x", 0, 0)
    attn_rows = lax.all_gather(jnp.concatenate([hidden[0], square_rows(group)]), "seq")
    r_own = r_of(attn_rows[:, rows : rows + 3, :rows])
    tail = jnp.concatenate([three_parts(r_own), docs_own[None]])
    tail = pad_to(tail, 16, HD)

    message = project(attn_cols, gain_a, w_query, w_key, w_value, tail)
    message = lax.all_to_all(message, "x", 0, 0)
    q_rows = rows * feats // HD
    kv = lax.all_to_all(message[:, q_rows:], "seq", 0, 0)
    query = lax.all_to_all(take_after(message, q_rows, kv), "seq", 0, 0)
    kv = jnp.sum(kv.astype(f32), axis=0).astype(bf16)
    kv_all = lax.all_gather(jnp.concatenate([kv, tail]), "x")
    kv_other = lax.ppermute(kv_all[:, :rows], "zb", [(0, 1), (1, 0)])

    half = HD // 2
    freq = rope_base ** (-(jnp.arange(half, dtype=f32) * 2.0 / HD))
    angle = jnp.arange(tokens, dtype=f32)[:, None] * freq[None, :]
    cosine, sine = jnp.cos(angle), jnp.sin(angle)
    tables = (jnp.concatenate([cosine] * 2, 1), jnp.concatenate([-sine, sine], 1))
    own = tuple(lax.dynamic_slice_in_dim(t, x_pos * rows, rows) for t in tables)
    copies, section_out = attend(place, query, kv_all, kv_other, own, tables, resid, nz)

    r_attn = jnp.sum(kv_all[:, rows : rows + 3].astype(f32), axis=1).reshape(tokens)
    attn_left = left_side(attn_rows[:, :rows], gain_attn, r_attn)
    upper = hessian(upper_kernel, place, attn_left, attn_cols, gain_a)

    group = lax.all_to_all(copies, ZL, 0, 0)
    out_rows = swap_x_seq(section_out)
    ffn_cols = lax.all_to_all(copied(group, nx), "x", 0, 0)
    ffn_rows = lax.all_gather(jnp.concatenate([out_rows, square_rows(group)]), "seq")
    r_ffn = lax.all_gather(r_of(ffn_rows[:, rows : rows + 3, :rows]), "x", tiled=True)
    ffn_rows = ffn_rows[:, :rows]
    count = lax.axis_size("phase")
    passed = lax.dynamic_slice_in_dim(ffn_rows, seq_pos, 1, 0)
    passed = lax.ppermute(passed, "phase", [(p, (p + 1) % count) for p in range(count)])
    ffn_left = left_side(ffn_rows, gain_ffn, r_ffn)
    hessians = hessian(lower_kernel, place, ffn_left, ffn_cols, gain_f, upper)[None]
    diag_width = feats // ns
    own_cols = lax.dynamic_slice_in_dim(
        ffn_rows.reshape(tokens, feats), seq_pos * diag_width, diag_width, 1
    ).astype(f32)
    own_gain = lax.dynamic_slice_in_dim(gain_ffn[0], seq_pos * diag_width, diag_width)
    own_cols = own_cols * r_ffn[:, None] * own_gain.astype(f32)
    ffn_diagonal = (jnp.sum(own_cols * own_cols, axis=0) * scale)[None]
    return (passed, hessians, ffn_diagonal)


def solution(mesh):
    phase, tensor, seq = (mesh.shape[a] for a in ("phase", "tensor", "seq"))
    lines = Mesh(
        mesh.devices.reshape(phase, tensor // 4, 2, 2, seq), ("phase", "x", "za", "zb", "seq")
    )
    tiled = P("phase", "seq", TENSOR)
    return jax.shard_map(
        on_device,
        mesh=lines,
        in_specs=(
            tiled,
            P("phase", "seq"),
            P("phase", TENSOR),
            P("phase", TENSOR),
            tiled,
            tiled,
            tiled,
        ),
        out_specs=(tiled, P("phase", TENSOR, "seq"), P("phase", GROUP)),
        check_vma=False,
    )
```

```python
import functools

import jax
import jax.numpy as jnp
from jax import lax
from jax.experimental import pallas as pl
from jax.experimental.pallas import tpu as pltpu
from jax.sharding import Mesh, PartitionSpec as P

HD = 128
norm_eps = 1e-05
rope_base = 500000.0
ZL = ("za", "zb")
TENSOR = ("x", "za", "zb")
GROUP = TENSOR + ("seq",)
f32 = jnp.float32
bf16 = jnp.bfloat16
LIMIT = 24 * 1024 * 1024


def swap_x_seq(value):
    nx, nz, ns = lax.axis_size("x"), lax.axis_size(ZL), lax.axis_size("seq")
    pairs = [
        ((x * nz + z) * ns + s, (s * nz + z) * ns + x)
        for x in range(nx)
        for z in range(nz)
        for s in range(ns)
    ]
    return lax.ppermute(value, GROUP, pairs)


def to_upper(value, away):
    nx, nz, ns = lax.axis_size("x"), lax.axis_size(ZL), lax.axis_size("seq")
    pairs = [
        ((x * nz + z) * ns + s, (x * nz + z) * ns + (s + away) % ns)
        for x in range(nx)
        for z in range(nz)
        for s in range(ns)
        if (s + away) % ns >= x
    ]
    return lax.ppermute(value, GROUP, pairs)


def three_parts(value):
    parts = []
    for _ in range(3):
        part = lax.reduce_precision(value, 8, 7)
        parts.append(part.astype(bf16))
        value = value - part
    return jnp.stack(parts)


def pad_to(rows, count, width):
    return jnp.pad(rows, ((0, count - rows.shape[0]), (0, width - rows.shape[1])))


def project_kernel(cols, gain, wq, wk, wv, out, q_acc, kv_acc):
    step = pl.program_id(0)
    blocks, rows, feats = cols.shape
    left = (cols[...].reshape(blocks * rows, feats).astype(f32) * gain[...]).astype(bf16)
    kv_w = jnp.concatenate([wk[...], wv[...]], 0)
    kv = lax.dot_general(left, kv_w, (((1,), (1,)), ((), ())), preferred_element_type=f32)
    q = jnp.dot(left, wq[...], preferred_element_type=f32)

    @pl.when(step == 0)
    def _():
        q_acc[...] = q
        kv_acc[...] = kv

    @pl.when(step > 0)
    def _():
        q_acc[...] += q
        kv_acc[...] += kv

    @pl.when(step == pl.num_programs(0) - 1)
    def _():
        heads = q_acc.shape[1] // HD
        for k in range(blocks):
            block = pl.ds(k * rows, rows)
            out[k, pl.ds(heads * rows, rows), :] = kv_acc[block, :].astype(bf16)
            for h in range(heads):
                out[k, pl.ds(h * rows, rows), :] = q_acc[block, pl.ds(h * HD, HD)].astype(bf16)


def project(cols, gain, w_query, w_key, w_value):
    blocks, parts, rows, feats = cols.shape
    q_width, kv_width = w_query.shape[2], 2 * w_key.shape[2]
    heads = q_width // HD
    kv_spec = pl.BlockSpec((None, w_key.shape[2], feats), lambda z: (0, 0, z))
    return pl.pallas_call(
        project_kernel,
        grid=(parts,),
        in_specs=[
            pl.BlockSpec((blocks, None, rows, feats), lambda z: (0, z, 0, 0)),
            pl.BlockSpec((None, 1, feats), lambda z: (z, 0, 0)),
            pl.BlockSpec((None, feats, q_width), lambda z: (0, z, 0)),
            kv_spec,
            kv_spec,
        ],
        out_specs=pl.BlockSpec((blocks, (heads + 1) * rows, HD), lambda z: (0, 0, 0)),
        out_shape=jax.ShapeDtypeStruct((blocks, (heads + 1) * rows, HD), bf16),
        scratch_shapes=[
            pltpu.VMEM((blocks * rows, q_width), f32),
            pltpu.VMEM((blocks * rows, kv_width), f32),
        ],
        compiler_params=pltpu.CompilerParams(vmem_limit_bytes=LIMIT),
        name="project",
    )(cols, gain, w_query, w_key.swapaxes(1, 2), w_value.swapaxes(1, 2))


def take_kernel(value, after, out):
    out[...] = value[...]


def take_after(value, count, after):
    shape = (value.shape[0], count, value.shape[2])
    spec = pl.BlockSpec((1, count, value.shape[2]), lambda i: (i, 0, 0))
    return pl.pallas_call(
        take_kernel,
        grid=(value.shape[0],),
        in_specs=[spec, pl.BlockSpec(memory_space=pl.ANY)],
        out_specs=spec,
        out_shape=jax.ShapeDtypeStruct(shape, value.dtype),
        compiler_params=pltpu.CompilerParams(vmem_limit_bytes=LIMIT),
        name="take_after",
    )(value, after)


def rotate(values, cosine, sine):
    return values * cosine + pltpu.roll(values, HD // 2, 1) * sine


def column_of(row):
    n = row.shape[1]
    same = lax.broadcasted_iota(jnp.int32, (n, n), 0) == lax.broadcasted_iota(jnp.int32, (n, n), 1)
    return jnp.sum(jnp.where(same, row, f32(0.0)), axis=1, keepdims=True)


def row_of(column):
    n = column.shape[0]
    same = lax.broadcasted_iota(jnp.int32, (n, n), 0) == lax.broadcasted_iota(jnp.int32, (n, n), 1)
    return jnp.sum(jnp.where(same, column, f32(0.0)), axis=0, keepdims=True)


def attend_kernel(
    place, q_in, kv_own, kv_other, cos_own, sin_own, cos_all, sin_all, resid, after, copies, out,
    keys, values, r_all, docs_all, r_own, docs_own,
):
    rows = out.shape[0]
    tokens = keys.shape[0]

    @pl.when(pl.program_id(0) == 0)
    def _():
        lower = lax.broadcasted_iota(jnp.int32, (rows, HD), 1) < HD // 2
        for k in range(tokens // rows):
            mine = kv_own[k, pl.ds(0, rows), :].astype(f32)
            other = kv_other[k].astype(f32)
            first = jnp.where(place[3] == 0, mine, other)
            second = jnp.where(place[3] == 0, other, mine)
            tail = kv_own[k, pl.ds(rows, 16), :].astype(f32)
            block = pl.ds(k * rows, rows)
            key = jnp.where(lower, first, pltpu.roll(second, HD // 2, 1))
            keys[block, :] = rotate(key, cos_all[block, :], sin_all[block, :])
            values[block, :] = jnp.where(lower, pltpu.roll(first, HD // 2, 1), second)
            r = tail[0:1] + tail[1:2] + tail[2:3]
            r_all[:, block] = r
            docs_all[:, block] = tail[3:4]

            @pl.when(place[0] == k)
            def _():
                r_own[...] = column_of(r) * (1.0 / HD**0.5)
                docs_own[...] = column_of(tail[3:4])

    query = jnp.sum(q_in[...].astype(f32), axis=0)
    query = rotate(query, cos_own[...], sin_own[...]) * r_own[...]
    scores = lax.dot_general(
        query, keys[...], (((1,), (1,)), ((), ())),
        preferred_element_type=f32, precision=lax.Precision.HIGHEST,
    )
    scores = scores * r_all[...]
    key_ids = lax.broadcasted_iota(jnp.int32, scores.shape, 1)
    own_ids = lax.broadcasted_iota(jnp.int32, scores.shape, 0) + place[0] * rows
    allowed = (key_ids <= own_ids) & (docs_all[...] == docs_own[...])
    scores = jnp.where(allowed, scores, f32(-1e30))
    peak = jnp.max(scores, axis=-1, keepdims=True)
    weights = jnp.where(allowed, jnp.exp(scores - peak), f32(0.0))
    total = jnp.sum(weights, axis=-1, keepdims=True)
    context = jnp.dot(
        weights * r_all[...], values[...],
        preferred_element_type=f32, precision=lax.Precision.HIGHEST,
    ) / total
    result = (resid[...].astype(f32) + context).astype(bf16)
    out[...] = result
    for copy in range(copies.shape[0]):
        copies[copy] = result


def attend(place, q_in, kv_own, kv_other, tables_own, tables_all, resid, after, copies):
    rows, feats = resid.shape
    heads, tokens = feats // HD, tables_all[0].shape[0]
    whole = pl.BlockSpec(memory_space=pltpu.VMEM)
    return pl.pallas_call(
        attend_kernel,
        grid=(heads,),
        in_specs=[
            pl.BlockSpec(memory_space=pltpu.SMEM),
            pl.BlockSpec((q_in.shape[0], rows, HD), lambda h: (0, h, 0)),
        ]
        + [whole] * 6
        + [pl.BlockSpec((rows, HD), lambda h: (0, h)), pl.BlockSpec(memory_space=pl.ANY)],
        out_specs=[
            pl.BlockSpec((copies, rows, HD), lambda h: (0, 0, h)),
            pl.BlockSpec((rows, HD), lambda h: (0, h)),
        ],
        out_shape=[
            jax.ShapeDtypeStruct((copies, rows, feats), bf16),
            jax.ShapeDtypeStruct((rows, feats), bf16),
        ],
        scratch_shapes=[
            pltpu.VMEM((tokens, HD), f32),
            pltpu.VMEM((tokens, HD), f32),
            pltpu.VMEM((1, tokens), f32),
            pltpu.VMEM((1, tokens), f32),
            pltpu.VMEM((rows, 1), f32),
            pltpu.VMEM((rows, 1), f32),
        ],
        compiler_params=pltpu.CompilerParams(vmem_limit_bytes=LIMIT),
        name="attend",
    )(place, q_in, kv_own, kv_other, *tables_own, *tables_all, resid, after)


def left_block(block, gain, r, scale):
    turned = (block.astype(f32) * gain).T
    return turned, r * r * scale


def attn_left_kernel(scale, place, own, one, two, three, gain, kv, out):
    rows = own.shape[0]
    blocks = kv.shape[0]
    for away, ref in enumerate((own, one, two, three)):
        k = lax.rem(place[4] + blocks - away, blocks)
        parts = kv[k, pl.ds(rows, 16), :].astype(f32)
        r = parts[0:1] + parts[1:2] + parts[2:3]
        turned, weight = left_block(ref[...], gain[...].astype(f32), r, scale)
        out[:, pl.ds(pl.multiple_of(k * rows, rows), rows)] = (turned * weight).astype(bf16)


def attn_left(scale, place, rows, gain, kv_all):
    feats = gain.shape[1]
    tokens = rows[0].shape[0] * kv_all.shape[0]
    whole = pl.BlockSpec(memory_space=pltpu.VMEM)
    return pl.pallas_call(
        functools.partial(attn_left_kernel, scale),
        in_specs=[pl.BlockSpec(memory_space=pltpu.SMEM)] + [whole] * 6,
        out_specs=whole,
        out_shape=jax.ShapeDtypeStruct((feats, tokens), bf16),
        compiler_params=pltpu.CompilerParams(vmem_limit_bytes=LIMIT),
        name="attn_left",
    )(place, *rows, gain, kv_all)


def hessian_kernel(
    scale, place, left_a, cols_a, gain_a, ffn_rows, gain_row, r_ffn, cols_f, gain_f,
    out, diagonal, left_f, turned_f,
):
    blocks, rows, feats = cols_a.shape
    row, col = place[1], place[2] + pl.program_id(0)

    @pl.when(pl.program_id(0) == 0)
    def _():
        squares = jnp.zeros((rows, 1), f32)
        part = pl.multiple_of(place[4] * rows, rows)
        for k in range(blocks):
            turned, weight = left_block(
                ffn_rows[k, pl.ds(0, rows), :], gain_row[...].astype(f32), r_ffn[k], scale
            )
            turned_f[...] = turned
            mine = turned_f[pl.ds(part, rows), :]
            squares += jnp.sum(mine * mine * weight, axis=1, keepdims=True)
            left_f[:, pl.ds(k * rows, rows)] = (turned * weight).astype(bf16)
        diagonal[...] = row_of(squares)

    def product(left, cols, gain):
        right = cols[...].reshape(blocks * rows, feats)
        return (jnp.dot(left[...], right, preferred_element_type=f32) * gain[...]).astype(bf16)

    @pl.when(row < col)
    def _():
        out[...] = product(left_a, cols_a, gain_a)

    @pl.when(row > col)
    def _():
        out[...] = product(left_f, cols_f, gain_f)

    @pl.when(row == col)
    def _():
        upper = product(left_a, cols_a, gain_a)
        lower = product(left_f, cols_f, gain_f)
        row_ids = lax.broadcasted_iota(jnp.int32, lower.shape, 0)
        col_ids = lax.broadcasted_iota(jnp.int32, lower.shape, 1)
        out[...] = jnp.where(row_ids <= col_ids, upper, lower)


def hessian(scale, place, left_a, cols_a, gain_a, ffn_rows, gain_row, r_ffn, cols_f, gain_f):
    blocks, parts, rows, feats = cols_a.shape
    tokens = blocks * rows

    def upper_at(z, at):
        return jnp.clip(jnp.maximum(z, at[1] - at[2]), 0, parts - 1)

    def lower_at(z, at):
        return jnp.clip(jnp.minimum(z, at[1] - at[2]), 0, parts - 1)

    def side(pick):
        return [
            pl.BlockSpec((blocks, None, rows, feats), lambda z, at: (0, pick(z, at), 0, 0)),
            pl.BlockSpec((None, 1, feats), lambda z, at: (z, 0, 0)),
        ]

    def fixed(shape):
        return pl.BlockSpec(shape, lambda z, at: (0,) * len(shape))

    return pl.pallas_call(
        functools.partial(hessian_kernel, scale),
        grid_spec=pltpu.PrefetchScalarGridSpec(
            num_scalar_prefetch=1,
            grid=(parts,),
            in_specs=[fixed(left_a.shape)]
            + side(upper_at)
            + [fixed(ffn_rows.shape), fixed(gain_row.shape), fixed(r_ffn.shape)]
            + side(lower_at),
            out_specs=[
                pl.BlockSpec((feats, feats), lambda z, at: (0, z)),
                fixed((1, rows)),
            ],
            scratch_shapes=[pltpu.VMEM((feats, tokens), bf16), pltpu.VMEM((feats, rows), f32)],
        ),
        out_shape=[
            jax.ShapeDtypeStruct((feats, parts * feats), bf16),
            jax.ShapeDtypeStruct((1, rows), f32),
        ],
        compiler_params=pltpu.CompilerParams(vmem_limit_bytes=LIMIT),
        name="hessian",
    )(place, left_a, cols_a, gain_a, ffn_rows, gain_row, r_ffn, cols_f, gain_f)


def on_device(hidden, segment_ids, gain_attn, gain_ffn, w_query, w_key, w_value):
    x_pos = lax.axis_index("x")
    zl_pos = lax.axis_index(ZL)
    seq_pos = lax.axis_index("seq")
    nx, nz, ns = lax.axis_size("x"), lax.axis_size(ZL), lax.axis_size("seq")
    rows, feats = hidden.shape[1:]
    tokens = rows * ns
    width = feats * nx * nz
    scale = 2.0 / tokens
    zb_pos = lax.axis_index("zb")
    place = jnp.stack([x_pos, x_pos * nz + zl_pos, seq_pos * nz, zb_pos, seq_pos])
    place = place.astype(jnp.int32)

    def copied(value, count):
        return jnp.broadcast_to(value[None], (count,) + value.shape)

    def square_rows(group):
        group = group.astype(f32)
        return pad_to(three_parts(jnp.sum(group * group, axis=(0, 2))), 16, feats)

    def r_of(parts):
        return lax.rsqrt(jnp.sum(parts.astype(f32), axis=(0, 1)) / width + norm_eps)

    resid = swap_x_seq(hidden[0])
    extra = swap_x_seq(
        pad_to(
            jnp.concatenate([gain_attn, gain_ffn, pad_to(segment_ids.astype(bf16), 1, feats)]),
            16,
            feats,
        )
    )
    group = lax.all_to_all(copied(jnp.concatenate([resid, extra]), nz), ZL, 0, 0)
    gain_a = group[:, rows : rows + 1].astype(f32)
    gain_f = group[:, rows + 1 : rows + 2].astype(f32)
    docs_own = extra[2, :rows]
    group = group[:, :rows]
    attn_cols = lax.all_to_all(copied(group, nx), "x", 0, 0)
    own_rows = take_after(hidden, rows, group)[0]
    attn_rows = [own_rows] + [to_upper(own_rows, d) for d in range(1, ns)]

    message = project(attn_cols, gain_a, w_query, w_key, w_value)
    message = lax.all_to_all(message, "x", 0, 0)
    q_rows = rows * feats // HD
    squares = copied(square_rows(group)[:, :HD], ns)
    kv = lax.all_to_all(jnp.concatenate([message[:, q_rows:], squares], 1), "seq", 0, 0)
    query = lax.all_to_all(take_after(message, q_rows, kv), "seq", 0, 0)
    tail = jnp.concatenate([three_parts(r_of(kv[:, rows : rows + 3])), docs_own[None]])
    kv = jnp.sum(kv[:, :rows].astype(f32), axis=0).astype(bf16)
    kv_all = lax.all_gather(jnp.concatenate([kv, pad_to(tail, 16, HD)]), "x")
    kv_other = lax.ppermute(kv_all[:, :rows], "zb", [(0, 1), (1, 0)])
    left_a = attn_left(scale, place, attn_rows, gain_attn, kv_all)

    half = HD // 2
    freq = rope_base ** (-(jnp.arange(half, dtype=f32) * 2.0 / HD))
    angle = jnp.arange(tokens, dtype=f32)[:, None] * freq[None, :]
    cosine, sine = jnp.cos(angle), jnp.sin(angle)
    tables = (jnp.concatenate([cosine] * 2, 1), jnp.concatenate([-sine, sine], 1))
    own = tuple(lax.dynamic_slice_in_dim(t, x_pos * rows, rows) for t in tables)
    copies, section_out = attend(
        place, query, kv_all, kv_other, own, tables, resid, left_a, nz
    )

    group = lax.all_to_all(copies, ZL, 0, 0)
    out_rows = swap_x_seq(section_out)
    ffn_cols = lax.all_to_all(copied(group, nx), "x", 0, 0)
    ffn_rows = lax.all_gather(jnp.concatenate([out_rows, square_rows(group)]), "seq")
    r_ffn = lax.all_gather(r_of(ffn_rows[:, rows : rows + 3, :rows])[None], "x")
    count = lax.axis_size("phase")
    passed = lax.dynamic_slice_in_dim(ffn_rows[:, :rows], seq_pos, 1, 0)
    passed = lax.ppermute(passed, "phase", [(p, (p + 1) % count) for p in range(count)])
    hessians, ffn_diagonal = hessian(
        scale, place, left_a, attn_cols, gain_a, ffn_rows, gain_ffn, r_ffn, ffn_cols, gain_f
    )
    return (passed, hessians[None], ffn_diagonal)


def solution(mesh):
    phase, tensor, seq = (mesh.shape[a] for a in ("phase", "tensor", "seq"))
    lines = Mesh(
        mesh.devices.reshape(phase, tensor // 4, 2, 2, seq), ("phase", "x", "za", "zb", "seq")
    )
    tiled = P("phase", "seq", TENSOR)
    return jax.shard_map(
        on_device,
        mesh=lines,
        in_specs=(
            tiled,
            P("phase", "seq"),
            P("phase", TENSOR),
            P("phase", TENSOR),
            tiled,
            tiled,
            tiled,
        ),
        out_specs=(tiled, P("phase", TENSOR, "seq"), P("phase", GROUP)),
        check_vma=False,
    )
```

```python
import functools

import jax
import jax.numpy as jnp
from jax import lax
from jax.experimental import pallas as pl
from jax.experimental.pallas import tpu as pltpu
from jax.sharding import Mesh, PartitionSpec as P

HD = 128
norm_eps = 1e-05
rope_base = 500000.0
ZL = ("za", "zb")
TENSOR = ("x", "za", "zb")
GROUP = TENSOR + ("seq",)
f32 = jnp.float32
bf16 = jnp.bfloat16
LIMIT = 24 * 1024 * 1024


def swap_x_seq(value):
    nx, nz, ns = lax.axis_size("x"), lax.axis_size(ZL), lax.axis_size("seq")
    pairs = [
        ((x * nz + z) * ns + s, (s * nz + z) * ns + x)
        for x in range(nx)
        for z in range(nz)
        for s in range(ns)
    ]
    return lax.ppermute(value, GROUP, pairs)


def to_upper(value, away):
    nx, nz, ns = lax.axis_size("x"), lax.axis_size(ZL), lax.axis_size("seq")
    pairs = [
        ((x * nz + z) * ns + s, (x * nz + z) * ns + (s + away) % ns)
        for x in range(nx)
        for z in range(nz)
        for s in range(ns)
        if (s + away) % ns >= x
    ]
    return lax.ppermute(value, GROUP, pairs)


def project_kernel(cols, gain, wq, wk, wv, first, second, out, q_acc, kv_acc):
    step = pl.program_id(0)
    blocks, rows, feats = cols.shape
    left = (cols[...].reshape(blocks * rows, feats).astype(f32) * gain[...]).astype(bf16)
    kv_w = jnp.concatenate([wk[...], wv[...]], 0)
    kv = lax.dot_general(left, kv_w, (((1,), (1,)), ((), ())), preferred_element_type=f32)
    q = jnp.dot(left, wq[...], preferred_element_type=f32)

    @pl.when(step == 0)
    def _():
        q_acc[...] = q
        kv_acc[...] = kv

    @pl.when(step > 0)
    def _():
        q_acc[...] += q
        kv_acc[...] += kv

    @pl.when(step == pl.num_programs(0) - 1)
    def _():
        heads = q_acc.shape[1] // HD
        for k in range(blocks):
            block = pl.ds(k * rows, rows)
            out[k, pl.ds(heads * rows, rows), :] = kv_acc[block, :].astype(bf16)
            for h in range(heads):
                out[k, pl.ds(h * rows, rows), :] = q_acc[block, pl.ds(h * HD, HD)].astype(bf16)


def project(cols, gain, w_query, w_key, w_value, *after):
    blocks, parts, rows, feats = cols.shape
    q_width, kv_width = w_query.shape[2], 2 * w_key.shape[2]
    heads = q_width // HD
    kv_spec = pl.BlockSpec((None, w_key.shape[2], feats), lambda z: (0, 0, z))
    return pl.pallas_call(
        project_kernel,
        grid=(parts,),
        in_specs=[
            pl.BlockSpec((blocks, None, rows, feats), lambda z: (0, z, 0, 0)),
            pl.BlockSpec((None, 1, feats), lambda z: (z, 0, 0)),
            pl.BlockSpec((None, feats, q_width), lambda z: (0, z, 0)),
            kv_spec,
            kv_spec,
        ]
        + [pl.BlockSpec(memory_space=pl.ANY)] * len(after),
        out_specs=pl.BlockSpec((blocks, (heads + 1) * rows, HD), lambda z: (0, 0, 0)),
        out_shape=jax.ShapeDtypeStruct((blocks, (heads + 1) * rows, HD), bf16),
        scratch_shapes=[
            pltpu.VMEM((blocks * rows, q_width), f32),
            pltpu.VMEM((blocks * rows, kv_width), f32),
        ],
        compiler_params=params(),
        name="project",
    )(cols, gain, w_query, w_key.swapaxes(1, 2), w_value.swapaxes(1, 2), *after)


def fixed(shape):
    return pl.BlockSpec(shape, lambda *at: (0,) * len(shape))


def params():
    return pltpu.CompilerParams(vmem_limit_bytes=LIMIT)


def three_parts(value):
    parts = []
    for _ in range(3):
        part = value.astype(bf16)
        parts.append(part)
        value = value - part.astype(f32)
    return parts


def row_of(column):
    n = column.shape[0]
    same = lax.broadcasted_iota(jnp.int32, (n, n), 0) == lax.broadcasted_iota(jnp.int32, (n, n), 1)
    return jnp.sum(jnp.where(same, column, f32(0.0)), axis=0, keepdims=True)


def stacked(parts, more=()):
    rows = list(parts) + list(more)
    rows.append(jnp.zeros((16 - len(rows), rows[0].shape[1]), f32))
    return jnp.concatenate([row.astype(f32) for row in rows]).astype(bf16)


def add_squares(group, squares):
    rows = squares.shape[0]
    block = group[pl.ds(0, rows), :].astype(f32)
    part = jnp.sum(block * block, axis=1, keepdims=True)

    @pl.when(pl.program_id(0) == 0)
    def _():
        squares[...] = part

    @pl.when(pl.program_id(0) > 0)
    def _():
        squares[...] += part


def attn_copies_kernel(group, own, copies, kept, sums, gain_a, gain_f, squares):
    rows = own.shape[0]
    for k in range(copies.shape[0]):
        copies[k] = group[pl.ds(0, rows), :]
    gains = group[pl.ds(rows, 16), :].astype(f32)
    gain_a[...] = gains[0:1]
    gain_f[...] = gains[1:2]
    add_squares(group, squares)

    @pl.when(pl.program_id(0) == pl.num_programs(0) - 1)
    def _():
        kept[...] = own[...]
        sums[...] = stacked(three_parts(row_of(squares[...])))


def attn_copies(group, own, count):
    parts, tall, feats = group.shape
    rows = own.shape[0]
    gain = pl.BlockSpec((None, 1, feats), lambda z: (z, 0, 0))
    gain_shape = jax.ShapeDtypeStruct((parts, 1, feats), f32)
    return pl.pallas_call(
        attn_copies_kernel,
        grid=(parts,),
        in_specs=[pl.BlockSpec((None, tall, feats), lambda z: (z, 0, 0)), fixed(own.shape)],
        out_specs=[
            pl.BlockSpec((count, None, rows, feats), lambda z: (0, z, 0, 0)),
            fixed(own.shape),
            fixed((16, rows)),
            gain,
            gain,
        ],
        out_shape=[
            pltpu.HBM((count, parts, rows, feats), bf16),
            jax.ShapeDtypeStruct(own.shape, bf16),
            jax.ShapeDtypeStruct((16, rows), bf16),
            gain_shape,
            gain_shape,
        ],
        scratch_shapes=[pltpu.VMEM((rows, 1), f32)],
        compiler_params=params(),
        name="attn_copies",
    )(group, own)


def ffn_copies_kernel(group, own, copies, message, squares):
    rows, feats = own.shape
    for k in range(copies.shape[0]):
        copies[k] = group[...]
    add_squares(group, squares)

    @pl.when(pl.program_id(0) == pl.num_programs(0) - 1)
    def _():
        message[pl.ds(0, rows), :] = own[...]
        sums = stacked(three_parts(row_of(squares[...])))
        message[pl.ds(rows, 16), :] = jnp.concatenate([sums] * (feats // rows), 1)


def ffn_copies(group, own, count):
    parts, rows, feats = group.shape
    return pl.pallas_call(
        ffn_copies_kernel,
        grid=(parts,),
        in_specs=[pl.BlockSpec((None, rows, feats), lambda z: (z, 0, 0)), fixed(own.shape)],
        out_specs=[
            pl.BlockSpec((count, None, rows, feats), lambda z: (0, z, 0, 0)),
            fixed((rows + 16, feats)),
        ],
        out_shape=[
            pltpu.HBM((count, parts, rows, feats), bf16),
            jax.ShapeDtypeStruct((rows + 16, feats), bf16),
        ],
        scratch_shapes=[pltpu.VMEM((rows, 1), f32)],
        compiler_params=params(),
        name="ffn_copies",
    )(group, own)


def kv_message_kernel(message, sums, after, out):
    rows = message.shape[0]
    out[pl.ds(0, rows), :] = message[...]
    out[pl.ds(rows, 16), :] = sums[...]


def kv_message(message, sums, after):
    blocks, tall, width = message.shape
    rows = sums.shape[1]
    last = tall // rows - 1
    return pl.pallas_call(
        kv_message_kernel,
        grid=(blocks,),
        in_specs=[
            pl.BlockSpec((None, rows, width), lambda i: (i, last, 0)),
            fixed(sums.shape),
            pl.BlockSpec(memory_space=pl.ANY),
        ],
        out_specs=pl.BlockSpec((None, rows + 16, width), lambda i: (i, 0, 0)),
        out_shape=jax.ShapeDtypeStruct((blocks, rows + 16, width), bf16),
        compiler_params=params(),
        name="kv_message",
    )(message, sums, after)


def take_kernel(value, after, out):
    out[...] = value[...]


def take_after(value, count, after):
    shape = (value.shape[0], count, value.shape[2])
    spec = pl.BlockSpec((1, count, value.shape[2]), lambda i: (i, 0, 0))
    return pl.pallas_call(
        take_kernel,
        grid=(value.shape[0],),
        in_specs=[spec, pl.BlockSpec(memory_space=pl.ANY)],
        out_specs=spec,
        out_shape=pltpu.HBM(shape, value.dtype),
        compiler_params=params(),
        name="take_after",
    )(value, after)


def kv_sum_kernel(width, arrived, docs, out):
    rows = out.shape[0] - 16
    out[pl.ds(0, rows), :] = jnp.sum(arrived[:, pl.ds(0, rows), :].astype(f32), axis=0).astype(bf16)
    sums = jnp.sum(arrived[:, pl.ds(rows, 16), :].astype(f32), axis=0)
    r = lax.rsqrt((sums[0:1] + sums[1:2] + sums[2:3]) / width + norm_eps)
    own = docs[...].astype(f32)[2:3, :rows]
    out[pl.ds(rows, 16), :] = stacked(three_parts(r), [own])


def kv_sum(width, arrived, docs):
    return pl.pallas_call(
        functools.partial(kv_sum_kernel, width),
        grid=(1,),
        in_specs=[fixed(arrived.shape), fixed(docs.shape)],
        out_specs=fixed(arrived.shape[1:]),
        out_shape=jax.ShapeDtypeStruct(arrived.shape[1:], bf16),
        compiler_params=params(),
        name="kv_sum",
    )(arrived, docs)


def rotate(values, table):
    lower = lax.broadcasted_iota(jnp.int32, table.shape, 1) < HD // 2
    swapped = pltpu.roll(table, HD // 2, 1)
    cosine = jnp.where(lower, table, swapped)
    sine = jnp.where(lower, -swapped, table)
    return values * cosine + pltpu.roll(values, HD // 2, 1) * sine


def column_of(row):
    n = row.shape[1]
    same = lax.broadcasted_iota(jnp.int32, (n, n), 0) == lax.broadcasted_iota(jnp.int32, (n, n), 1)
    return jnp.sum(jnp.where(same, row, f32(0.0)), axis=1, keepdims=True)


def attend_kernel(
    q_in, kv_own, kv_other, table, resid, after, copies, out,
    keys, values, r_all, docs_all, r_own, docs_own,
):
    rows = out.shape[0]
    tokens = keys.shape[0]
    x_pos, zb_pos = lax.axis_index("x"), lax.axis_index("zb")

    @pl.when(pl.program_id(0) == 0)
    def _():
        lower = lax.broadcasted_iota(jnp.int32, (rows, HD), 1) < HD // 2
        for k in range(tokens // rows):
            mine = kv_own[k, pl.ds(0, rows), :].astype(f32)
            other = kv_other[k, pl.ds(0, rows), :].astype(f32)
            first = jnp.where(zb_pos == 0, mine, other)
            second = jnp.where(zb_pos == 0, other, mine)
            tail = kv_own[k, pl.ds(rows, 16), :].astype(f32)
            block = pl.ds(k * rows, rows)
            key = jnp.where(lower, first, pltpu.roll(second, HD // 2, 1))
            keys[block, :] = rotate(key, table[block, :])
            values[block, :] = jnp.where(lower, pltpu.roll(first, HD // 2, 1), second)
            r = tail[0:1] + tail[1:2] + tail[2:3]
            r_all[:, block] = r
            docs_all[:, block] = tail[3:4]

            @pl.when(x_pos == k)
            def _():
                r_own[...] = column_of(r) * (1.0 / HD**0.5)
                docs_own[...] = column_of(tail[3:4])

    query = jnp.sum(q_in[...].astype(f32), axis=0)
    own = pl.ds(pl.multiple_of(x_pos * rows, rows), rows)
    query = rotate(query, table[own, :]) * r_own[...]
    scores = lax.dot_general(
        query, keys[...], (((1,), (1,)), ((), ())),
        preferred_element_type=f32, precision=lax.Precision.HIGHEST,
    )
    scores = scores * r_all[...]
    key_ids = lax.broadcasted_iota(jnp.int32, scores.shape, 1)
    own_ids = lax.broadcasted_iota(jnp.int32, scores.shape, 0) + x_pos * rows
    allowed = (key_ids <= own_ids) & (docs_all[...] == docs_own[...])
    scores = jnp.where(allowed, scores, f32(-1e30))
    peak = jnp.max(scores, axis=-1, keepdims=True)
    weights = jnp.where(allowed, jnp.exp(scores - peak), f32(0.0))
    total = jnp.sum(weights, axis=-1, keepdims=True)
    context = jnp.dot(
        weights * r_all[...], values[...],
        preferred_element_type=f32, precision=lax.Precision.HIGHEST,
    ) / total
    result = (resid[...].astype(f32) + context).astype(bf16)
    out[...] = result
    for copy in range(copies.shape[0]):
        copies[copy] = result


def attend(q_in, kv_own, kv_other, table, resid, after, copies):
    rows, feats = resid.shape
    heads, tokens = feats // HD, table.shape[0]
    return pl.pallas_call(
        attend_kernel,
        grid=(heads,),
        in_specs=[
            pl.BlockSpec((q_in.shape[0], rows, HD), lambda h: (0, h, 0)),
        ]
        + [fixed(kv_own.shape), fixed(kv_other.shape), fixed(table.shape)]
        + [pl.BlockSpec((rows, HD), lambda h: (0, h)), pl.BlockSpec(memory_space=pl.ANY)],
        out_specs=[
            pl.BlockSpec((copies, rows, HD), lambda h: (0, 0, h)),
            pl.BlockSpec((rows, HD), lambda h: (0, h)),
        ],
        out_shape=[
            pltpu.HBM((copies, rows, feats), bf16),
            pltpu.HBM((rows, feats), bf16),
        ],
        scratch_shapes=[
            pltpu.VMEM((tokens, HD), f32),
            pltpu.VMEM((tokens, HD), f32),
            pltpu.VMEM((1, tokens), f32),
            pltpu.VMEM((1, tokens), f32),
            pltpu.VMEM((rows, 1), f32),
            pltpu.VMEM((rows, 1), f32),
        ],
        compiler_params=params(),
        name="attend",
    )(q_in, kv_own, kv_other, table, resid, after)


def left_block(block, gain, r, scale):
    turned = (block.astype(f32) * gain).T
    return turned, r * r * scale


def attn_left_kernel(scale, own, one, two, three, gain, kv, out):
    rows = own.shape[0]
    blocks = kv.shape[0]
    seq_pos = lax.axis_index("seq")
    for away, ref in enumerate((own, one, two, three)):
        k = lax.rem(seq_pos + blocks - away, blocks)
        parts = kv[k, pl.ds(rows, 16), :].astype(f32)
        r = parts[0:1] + parts[1:2] + parts[2:3]
        turned, weight = left_block(ref[...], gain[...].astype(f32), r, scale)
        out[:, pl.ds(pl.multiple_of(k * rows, rows), rows)] = (turned * weight).astype(bf16)


def attn_left(scale, rows, gain, kv_all):
    feats = gain.shape[1]
    tokens = rows[0].shape[0] * kv_all.shape[0]
    arrays = (*rows, gain, kv_all)
    return pl.pallas_call(
        functools.partial(attn_left_kernel, scale),
        grid=(1,),
        in_specs=[fixed(a.shape) for a in arrays],
        out_specs=fixed((feats, tokens)),
        out_shape=jax.ShapeDtypeStruct((feats, tokens), bf16),
        compiler_params=params(),
        name="attn_left",
    )(*arrays)


def hessian_kernel(
    scale, place, left_a, cols_a, gain_a, ffn_rows, gain_row, r_ffn, cols_f, gain_f,
    out, diagonal, left_f, turned_f,
):
    blocks, rows, feats = cols_a.shape
    row, col = place[0], place[1] + pl.program_id(0)

    @pl.when(pl.program_id(0) == 0)
    def _():
        squares = jnp.zeros((rows, 1), f32)
        part = pl.multiple_of(lax.axis_index("seq") * rows, rows)
        for k in range(blocks):
            turned, weight = left_block(
                ffn_rows[k, pl.ds(0, rows), :], gain_row[...].astype(f32), r_ffn[k], scale
            )
            turned_f[...] = turned
            mine = turned_f[pl.ds(part, rows), :]
            squares += jnp.sum(mine * mine * weight, axis=1, keepdims=True)
            left_f[:, pl.ds(k * rows, rows)] = (turned * weight).astype(bf16)
        diagonal[...] = row_of(squares)

    def product(left, cols, gain):
        right = cols[...].reshape(blocks * rows, feats)
        return (jnp.dot(left[...], right, preferred_element_type=f32) * gain[...]).astype(bf16)

    @pl.when(row < col)
    def _():
        out[...] = product(left_a, cols_a, gain_a)

    @pl.when(row > col)
    def _():
        out[...] = product(left_f, cols_f, gain_f)

    @pl.when(row == col)
    def _():
        upper = product(left_a, cols_a, gain_a)
        lower = product(left_f, cols_f, gain_f)
        row_ids = lax.broadcasted_iota(jnp.int32, lower.shape, 0)
        col_ids = lax.broadcasted_iota(jnp.int32, lower.shape, 1)
        out[...] = jnp.where(row_ids <= col_ids, upper, lower)


def hessian(scale, place, left_a, cols_a, gain_a, ffn_rows, gain_row, r_ffn, cols_f, gain_f):
    blocks, parts, rows, feats = cols_a.shape
    tokens = blocks * rows

    def upper_at(z, at):
        return jnp.clip(jnp.maximum(z, at[0] - at[1]), 0, parts - 1)

    def lower_at(z, at):
        return jnp.clip(jnp.minimum(z, at[0] - at[1]), 0, parts - 1)

    def side(pick):
        return [
            pl.BlockSpec((blocks, None, rows, feats), lambda z, at: (0, pick(z, at), 0, 0)),
            pl.BlockSpec((None, 1, feats), lambda z, at: (z, 0, 0)),
        ]

    return pl.pallas_call(
        functools.partial(hessian_kernel, scale),
        grid_spec=pltpu.PrefetchScalarGridSpec(
            num_scalar_prefetch=1,
            grid=(parts,),
            in_specs=[fixed(left_a.shape)]
            + side(upper_at)
            + [fixed(ffn_rows.shape), fixed(gain_row.shape), fixed(r_ffn.shape)]
            + side(lower_at),
            out_specs=[
                pl.BlockSpec((feats, feats), lambda z, at: (0, z)),
                fixed((1, rows)),
            ],
            scratch_shapes=[pltpu.VMEM((feats, tokens), bf16), pltpu.VMEM((feats, rows), f32)],
        ),
        out_shape=[
            jax.ShapeDtypeStruct((feats, parts * feats), bf16),
            jax.ShapeDtypeStruct((1, rows), f32),
        ],
        compiler_params=params(),
        name="hessian",
    )(place, left_a, cols_a, gain_a, ffn_rows, gain_row, r_ffn, cols_f, gain_f)


def on_device(hidden, segment_ids, gain_attn, gain_ffn, w_query, w_key, w_value):
    x_pos = lax.axis_index("x")
    zl_pos = lax.axis_index(ZL)
    seq_pos = lax.axis_index("seq")
    nx, nz, ns = lax.axis_size("x"), lax.axis_size(ZL), lax.axis_size("seq")
    rows, feats = hidden.shape[1:]
    tokens = rows * ns
    width = feats * nx * nz
    scale = 2.0 / tokens
    place = jnp.stack([x_pos * nz + zl_pos, seq_pos * nz])
    place = place.astype(jnp.int32)

    def copied(value, count):
        return jnp.broadcast_to(value[None], (count,) + value.shape)

    def r_of(parts):
        return lax.rsqrt(jnp.sum(parts.astype(f32), axis=(0, 1)) / width + norm_eps)

    resid = swap_x_seq(hidden[0])
    docs = jnp.pad(segment_ids.astype(bf16), ((0, 13), (0, feats - rows)))
    extra = swap_x_seq(jnp.concatenate([gain_attn, gain_ffn, docs]))
    group = lax.all_to_all(copied(jnp.concatenate([resid, extra]), nz), ZL, 0, 0)
    copies, own_rows, sums, gain_a, gain_f = attn_copies(group, hidden[0], nx)
    attn_rows = [own_rows] + [to_upper(own_rows, d) for d in range(1, ns)]
    attn_cols = lax.all_to_all(copies, "x", 0, 0)

    message = project(attn_cols, gain_a, w_query, w_key, w_value, *attn_rows[1:3])
    message = lax.all_to_all(message, "x", 0, 0)
    kv = lax.all_to_all(kv_message(message, sums, attn_rows[3]), "seq", 0, 0)
    query = lax.all_to_all(take_after(message, rows * feats // HD, kv), "seq", 0, 0)
    kv_all = lax.all_gather(kv_sum(width, kv, extra), "x")
    kv_other = lax.ppermute(kv_all, "zb", [(0, 1), (1, 0)])
    left_a = attn_left(scale, attn_rows, gain_attn, kv_all)

    half = HD // 2
    freq = rope_base ** (-(jnp.arange(half, dtype=f32) * 2.0 / HD))
    angle = jnp.arange(tokens, dtype=f32)[:, None] * freq[None, :]
    table = jnp.concatenate([jnp.cos(angle), jnp.sin(angle)], 1)
    copies, section_out = attend(query, kv_all, kv_other, table, resid, left_a, nz)

    group = lax.all_to_all(copies, ZL, 0, 0)
    copies, message = ffn_copies(group, swap_x_seq(section_out), nx)
    ffn_cols = lax.all_to_all(copies, "x", 0, 0)
    ffn_rows = lax.all_gather(message, "seq")
    r_ffn = lax.all_gather(r_of(ffn_rows[:, rows : rows + 3, :rows])[None], "x")
    count = lax.axis_size("phase")
    passed = lax.dynamic_slice_in_dim(ffn_rows[:, :rows], seq_pos, 1, 0)
    passed = lax.ppermute(passed, "phase", [(p, (p + 1) % count) for p in range(count)])
    hessians, ffn_diagonal = hessian(
        scale, place, left_a, attn_cols, gain_a, ffn_rows, gain_ffn, r_ffn, ffn_cols, gain_f
    )
    return (passed, hessians[None], ffn_diagonal)


def solution(mesh):
    phase, tensor, seq = (mesh.shape[a] for a in ("phase", "tensor", "seq"))
    lines = Mesh(
        mesh.devices.reshape(phase, tensor // 4, 2, 2, seq), ("phase", "x", "za", "zb", "seq")
    )
    tiled = P("phase", "seq", TENSOR)
    return jax.shard_map(
        on_device,
        mesh=lines,
        in_specs=(
            tiled,
            P("phase", "seq"),
            P("phase", TENSOR),
            P("phase", TENSOR),
            tiled,
            tiled,
            tiled,
        ),
        out_specs=(tiled, P("phase", TENSOR, "seq"), P("phase", GROUP)),
        check_vma=False,
    )
```

```python
import functools

import jax
import jax.numpy as jnp
from jax import lax
from jax.experimental import pallas as pl
from jax.experimental.pallas import tpu as pltpu
from jax.sharding import Mesh, PartitionSpec as P

HD = 128
norm_eps = 1e-05
rope_base = 500000.0
ZL = ("za", "zb")
TENSOR = ("x", "za", "zb")
GROUP = TENSOR + ("seq",)
f32 = jnp.float32
bf16 = jnp.bfloat16
LIMIT = 24 * 1024 * 1024


def swap_x_seq(value):
    nx, nz, ns = lax.axis_size("x"), lax.axis_size(ZL), lax.axis_size("seq")
    pairs = [
        ((x * nz + z) * ns + s, (s * nz + z) * ns + x)
        for x in range(nx)
        for z in range(nz)
        for s in range(ns)
    ]
    return lax.ppermute(value, GROUP, pairs)


def project_kernel(cols, gain, wq, wk, wv, first, second, out, q_acc, kv_acc, squares):
    step = pl.program_id(0)
    blocks, rows, feats = cols.shape
    raw = cols[...].reshape(blocks * rows, feats).astype(f32)
    left = (raw * gain[...]).astype(bf16)
    part = jnp.sum(raw * raw, axis=1, keepdims=True)
    kv_w = jnp.concatenate([wk[...], wv[...]], 0)
    kv = lax.dot_general(left, kv_w, (((1,), (1,)), ((), ())), preferred_element_type=f32)
    q = jnp.dot(left, wq[...], preferred_element_type=f32)

    @pl.when(step == 0)
    def _():
        q_acc[...] = q
        kv_acc[...] = kv
        squares[...] = part

    @pl.when(step > 0)
    def _():
        q_acc[...] += q
        kv_acc[...] += kv
        squares[...] += part

    @pl.when(step == pl.num_programs(0) - 1)
    def _():
        heads = q_acc.shape[1] // HD
        for k in range(blocks):
            block = pl.ds(k * rows, rows)
            out[k, pl.ds(heads * rows, rows), :] = kv_acc[block, :].astype(bf16)
            sums = stacked(three_parts(row_of(squares[block, :])))
            out[k, pl.ds((heads + 1) * rows, 16), :] = sums
            for h in range(heads):
                out[k, pl.ds(h * rows, rows), :] = q_acc[block, pl.ds(h * HD, HD)].astype(bf16)


def project(cols, gain, w_query, w_key, w_value, *after):
    blocks, parts, rows, feats = cols.shape
    q_width, kv_width = w_query.shape[2], 2 * w_key.shape[2]
    heads = q_width // HD
    kv_spec = pl.BlockSpec((None, w_key.shape[2], feats), lambda z: (0, 0, z))
    return pl.pallas_call(
        project_kernel,
        grid=(parts,),
        in_specs=[
            pl.BlockSpec((blocks, None, rows, feats), lambda z: (0, z, 0, 0)),
            pl.BlockSpec((None, 1, feats), lambda z: (z, 0, 0)),
            pl.BlockSpec((None, feats, q_width), lambda z: (0, z, 0)),
            kv_spec,
            kv_spec,
        ]
        + [pl.BlockSpec(memory_space=pl.ANY)] * len(after),
        out_specs=fixed((blocks, (heads + 1) * rows + 16, HD)),
        out_shape=pltpu.HBM((blocks, (heads + 1) * rows + 16, HD), bf16),
        scratch_shapes=[
            pltpu.VMEM((blocks * rows, q_width), f32),
            pltpu.VMEM((blocks * rows, kv_width), f32),
            pltpu.VMEM((blocks * rows, 1), f32),
        ],
        compiler_params=params(),
        name="project",
    )(cols, gain, w_query, w_key.swapaxes(1, 2), w_value.swapaxes(1, 2), *after)


def fixed(shape):
    return pl.BlockSpec(shape, lambda *at: (0,) * len(shape))


def params():
    return pltpu.CompilerParams(vmem_limit_bytes=LIMIT)


def three_parts(value):
    parts = []
    for _ in range(3):
        part = value.astype(bf16)
        parts.append(part)
        value = value - part.astype(f32)
    return parts


def row_of(column):
    n = column.shape[0]
    same = lax.broadcasted_iota(jnp.int32, (n, n), 0) == lax.broadcasted_iota(jnp.int32, (n, n), 1)
    return jnp.sum(jnp.where(same, column, f32(0.0)), axis=0, keepdims=True)


def stacked(parts, more=()):
    rows = list(parts) + list(more)
    rows.append(jnp.zeros((16 - len(rows), rows[0].shape[1]), f32))
    return jnp.concatenate([row.astype(f32) for row in rows]).astype(bf16)


def add_squares(group, squares):
    rows = squares.shape[0]
    block = group[pl.ds(0, rows), :].astype(f32)
    part = jnp.sum(block * block, axis=1, keepdims=True)

    @pl.when(pl.program_id(0) == 0)
    def _():
        squares[...] = part

    @pl.when(pl.program_id(0) > 0)
    def _():
        squares[...] += part


def attn_copies_kernel(group, own, copies, kept, gain_a, gain_f):
    rows = own.shape[0]
    for k in range(copies.shape[0]):
        copies[k] = group[pl.ds(0, rows), :]
    gains = group[pl.ds(rows, 16), :].astype(f32)
    gain_a[...] = gains[0:1]
    gain_f[...] = gains[1:2]

    @pl.when(pl.program_id(0) == 0)
    def _():
        kept[...] = own[...]


def attn_copies(group, own, count):
    parts, tall, feats = group.shape
    rows = own.shape[0]
    gain = pl.BlockSpec((None, 1, feats), lambda z: (z, 0, 0))
    gain_shape = pltpu.HBM((parts, 1, feats), f32)
    return pl.pallas_call(
        attn_copies_kernel,
        grid=(parts,),
        in_specs=[pl.BlockSpec((None, tall, feats), lambda z: (z, 0, 0)), fixed(own.shape)],
        out_specs=[
            pl.BlockSpec((count, None, rows, feats), lambda z: (0, z, 0, 0)),
            fixed(own.shape),
            gain,
            gain,
        ],
        out_shape=[
            pltpu.HBM((count, parts, rows, feats), bf16),
            pltpu.HBM(own.shape, bf16),
            gain_shape,
            gain_shape,
        ],
        compiler_params=params(),
        name="attn_copies",
    )(group, own)


def ffn_copies_kernel(group, own, after, copies, message, squares):
    rows, feats = own.shape
    for k in range(copies.shape[0]):
        copies[k] = group[...]
    add_squares(group, squares)

    @pl.when(pl.program_id(0) == pl.num_programs(0) - 1)
    def _():
        message[pl.ds(0, rows), :] = own[...]
        sums = stacked(three_parts(row_of(squares[...])))
        message[pl.ds(rows, 16), :] = jnp.concatenate([sums] * (feats // rows), 1)


def ffn_copies(group, own, after, count):
    parts, rows, feats = group.shape
    return pl.pallas_call(
        ffn_copies_kernel,
        grid=(parts,),
        in_specs=[
            pl.BlockSpec((None, rows, feats), lambda z: (z, 0, 0)),
            fixed(own.shape),
            pl.BlockSpec(memory_space=pl.ANY),
        ],
        out_specs=[
            pl.BlockSpec((count, None, rows, feats), lambda z: (0, z, 0, 0)),
            fixed((rows + 16, feats)),
        ],
        out_shape=[
            pltpu.HBM((count, parts, rows, feats), bf16),
            jax.ShapeDtypeStruct((rows + 16, feats), bf16),
        ],
        scratch_shapes=[pltpu.VMEM((rows, 1), f32)],
        compiler_params=params(),
        name="ffn_copies",
    )(group, own, after)


def kv_sum_kernel(width, arrived, docs, out):
    rows = out.shape[1] - 16
    kv = jnp.sum(arrived[:, pl.ds(0, rows), :].astype(f32), axis=0).astype(bf16)
    sums = jnp.sum(arrived[:, pl.ds(rows, 16), :].astype(f32), axis=0)
    r = lax.rsqrt((sums[0:1] + sums[1:2] + sums[2:3]) / width + norm_eps)
    tail = stacked(three_parts(r), [docs[...].astype(f32)[2:3, :rows]])
    for copy in range(out.shape[0]):
        out[copy, pl.ds(0, rows), :] = kv
        out[copy, pl.ds(rows, 16), :] = tail


def kv_sum(width, arrived, docs, copies):
    blocks, tall, lanes = arrived.shape
    rows = HD
    last = tall - rows - 16
    return pl.pallas_call(
        functools.partial(kv_sum_kernel, width),
        grid=(1,),
        in_specs=[
            pl.BlockSpec(
                (pl.Element(blocks), pl.Element(rows + 16), pl.Element(lanes)),
                lambda i: (0, last, 0),
            ),
            fixed(docs.shape),
        ],
        out_specs=fixed((copies, rows + 16, lanes)),
        out_shape=pltpu.HBM((copies, rows + 16, lanes), bf16),
        compiler_params=params(),
        name="kv_sum",
    )(arrived, docs)


def rotate(values, table):
    lower = lax.broadcasted_iota(jnp.int32, table.shape, 1) < HD // 2
    swapped = pltpu.roll(table, HD // 2, 1)
    cosine = jnp.where(lower, table, swapped)
    sine = jnp.where(lower, -swapped, table)
    return values * cosine + pltpu.roll(values, HD // 2, 1) * sine


def column_of(row):
    n = row.shape[1]
    same = lax.broadcasted_iota(jnp.int32, (n, n), 0) == lax.broadcasted_iota(jnp.int32, (n, n), 1)
    return jnp.sum(jnp.where(same, row, f32(0.0)), axis=1, keepdims=True)


def attend_kernel(
    q_in, kv_in, table, resid, copies, out,
    keys, values, r_all, docs_all, r_own, docs_own,
):
    rows = out.shape[0]
    tokens = keys.shape[0]
    x_pos = lax.axis_index("x")

    @pl.when(pl.program_id(0) == 0)
    def _():
        lower = lax.broadcasted_iota(jnp.int32, (rows, HD), 1) < HD // 2
        for k in range(tokens // rows):
            first = kv_in[2 * k, pl.ds(0, rows), :].astype(f32)
            second = kv_in[2 * k + 1, pl.ds(0, rows), :].astype(f32)
            tail = kv_in[2 * k, pl.ds(rows, 16), :].astype(f32)
            block = pl.ds(k * rows, rows)
            key = jnp.where(lower, first, pltpu.roll(second, HD // 2, 1))
            keys[block, :] = rotate(key, table[block, :])
            values[block, :] = jnp.where(lower, pltpu.roll(first, HD // 2, 1), second)
            r = tail[0:1] + tail[1:2] + tail[2:3]
            r_all[:, block] = r
            docs_all[:, block] = tail[3:4]

            @pl.when(x_pos == k)
            def _():
                r_own[...] = column_of(r) * (1.0 / HD**0.5)
                docs_own[...] = column_of(tail[3:4])

    query = jnp.sum(q_in[...].astype(f32), axis=0)
    own = pl.ds(pl.multiple_of(x_pos * rows, rows), rows)
    query = rotate(query, table[own, :]) * r_own[...]
    scores = lax.dot_general(
        query, keys[...], (((1,), (1,)), ((), ())),
        preferred_element_type=f32, precision=lax.Precision.HIGHEST,
    )
    scores = scores * r_all[...]
    key_ids = lax.broadcasted_iota(jnp.int32, scores.shape, 1)
    own_ids = lax.broadcasted_iota(jnp.int32, scores.shape, 0) + x_pos * rows
    allowed = (key_ids <= own_ids) & (docs_all[...] == docs_own[...])
    scores = jnp.where(allowed, scores, f32(-1e30))
    peak = jnp.max(scores, axis=-1, keepdims=True)
    weights = jnp.where(allowed, jnp.exp(scores - peak), f32(0.0))
    total = jnp.sum(weights, axis=-1, keepdims=True)
    context = jnp.dot(
        weights * r_all[...], values[...],
        preferred_element_type=f32, precision=lax.Precision.HIGHEST,
    ) / total
    result = (resid[...].astype(f32) + context).astype(bf16)
    out[...] = result
    for copy in range(copies.shape[0]):
        copies[copy] = result


def attend(q_in, kv_in, table, resid, copies):
    rows, feats = resid.shape
    heads, tokens = feats // HD, table.shape[0]
    return pl.pallas_call(
        attend_kernel,
        grid=(heads,),
        in_specs=[
            pl.BlockSpec((q_in.shape[0], rows, HD), lambda h: (0, h, 0)),
        ]
        + [fixed(kv_in.shape), fixed(table.shape)]
        + [pl.BlockSpec((rows, HD), lambda h: (0, h))],
        out_specs=[
            pl.BlockSpec((copies, rows, HD), lambda h: (0, 0, h)),
            pl.BlockSpec((rows, HD), lambda h: (0, h)),
        ],
        out_shape=[
            pltpu.HBM((copies, rows, feats), bf16),
            pltpu.HBM((rows, feats), bf16),
        ],
        scratch_shapes=[
            pltpu.VMEM((tokens, HD), f32),
            pltpu.VMEM((tokens, HD), f32),
            pltpu.VMEM((1, tokens), f32),
            pltpu.VMEM((1, tokens), f32),
            pltpu.VMEM((rows, 1), f32),
            pltpu.VMEM((rows, 1), f32),
        ],
        compiler_params=params(),
        name="attend",
    )(q_in, kv_in, table, resid)


def left_block(block, gain, r, scale):
    turned = (block.astype(f32) * gain).T
    return turned, r * r * scale


def attn_left_kernel(scale, own_rows, gain, kv, out):
    blocks, rows, feats = own_rows.shape
    for k in range(blocks):
        parts = kv[2 * k, pl.ds(rows, 16), :].astype(f32)
        r = parts[0:1] + parts[1:2] + parts[2:3]
        turned, weight = left_block(own_rows[k], gain[...].astype(f32), r, scale)
        out[:, pl.ds(k * rows, rows)] = (turned * weight).astype(bf16)


def attn_left(scale, own_rows, gain, kv_all):
    blocks, rows, feats = own_rows.shape
    arrays = (own_rows, gain, kv_all)
    return pl.pallas_call(
        functools.partial(attn_left_kernel, scale),
        grid=(1,),
        in_specs=[fixed(a.shape) for a in arrays],
        out_specs=fixed((feats, blocks * rows)),
        out_shape=jax.ShapeDtypeStruct((feats, blocks * rows), bf16),
        compiler_params=params(),
        name="attn_left",
    )(*arrays)


def hessian_kernel(
    scale, place, left_a, cols_a, gain_a, ffn_rows, gain_row, r_ffn, cols_f, gain_f,
    out, diagonal, left_f, turned_f,
):
    blocks, rows, feats = cols_a.shape
    row, col = place[0], place[1] + pl.program_id(0)

    @pl.when(pl.program_id(0) == 0)
    def _():
        squares = jnp.zeros((rows, 1), f32)
        part = pl.multiple_of(lax.axis_index("seq") * rows, rows)
        for k in range(blocks):
            turned, weight = left_block(
                ffn_rows[k, pl.ds(0, rows), :], gain_row[...].astype(f32), r_ffn[k], scale
            )
            turned_f[...] = turned
            mine = turned_f[pl.ds(part, rows), :]
            squares += jnp.sum(mine * mine * weight, axis=1, keepdims=True)
            left_f[:, pl.ds(k * rows, rows)] = (turned * weight).astype(bf16)
        diagonal[...] = row_of(squares)

    def product(left, cols, gain):
        right = cols[...].reshape(blocks * rows, feats)
        return (jnp.dot(left[...], right, preferred_element_type=f32) * gain[...]).astype(bf16)

    @pl.when(row < col)
    def _():
        out[...] = product(left_a, cols_a, gain_a)

    @pl.when(row > col)
    def _():
        out[...] = product(left_f, cols_f, gain_f)

    @pl.when(row == col)
    def _():
        upper = product(left_a, cols_a, gain_a)
        lower = product(left_f, cols_f, gain_f)
        row_ids = lax.broadcasted_iota(jnp.int32, lower.shape, 0)
        col_ids = lax.broadcasted_iota(jnp.int32, lower.shape, 1)
        out[...] = jnp.where(row_ids <= col_ids, upper, lower)


def hessian(scale, place, left_a, cols_a, gain_a, ffn_rows, gain_row, r_ffn, cols_f, gain_f):
    blocks, parts, rows, feats = cols_a.shape
    tokens = blocks * rows

    def upper_at(z, at):
        return jnp.clip(jnp.maximum(z, at[0] - at[1]), 0, parts - 1)

    def lower_at(z, at):
        return jnp.clip(jnp.minimum(z, at[0] - at[1]), 0, parts - 1)

    def side(pick):
        return [
            pl.BlockSpec((blocks, None, rows, feats), lambda z, at: (0, pick(z, at), 0, 0)),
            pl.BlockSpec((None, 1, feats), lambda z, at: (z, 0, 0)),
        ]

    return pl.pallas_call(
        functools.partial(hessian_kernel, scale),
        grid_spec=pltpu.PrefetchScalarGridSpec(
            num_scalar_prefetch=1,
            grid=(parts,),
            in_specs=[fixed(left_a.shape)]
            + side(upper_at)
            + [fixed(ffn_rows.shape), fixed(gain_row.shape), fixed(r_ffn.shape)]
            + side(lower_at),
            out_specs=[
                pl.BlockSpec((feats, feats), lambda z, at: (0, z)),
                fixed((1, rows)),
            ],
            scratch_shapes=[pltpu.VMEM((feats, tokens), bf16), pltpu.VMEM((feats, rows), f32)],
        ),
        out_shape=[
            jax.ShapeDtypeStruct((feats, parts * feats), bf16),
            jax.ShapeDtypeStruct((1, rows), f32),
        ],
        compiler_params=params(),
        name="hessian",
    )(place, left_a, cols_a, gain_a, ffn_rows, gain_row, r_ffn, cols_f, gain_f)


def on_device(hidden, segment_ids, gain_attn, gain_ffn, w_query, w_key, w_value):
    x_pos = lax.axis_index("x")
    zl_pos = lax.axis_index(ZL)
    seq_pos = lax.axis_index("seq")
    nx, nz, ns = lax.axis_size("x"), lax.axis_size(ZL), lax.axis_size("seq")
    rows, feats = hidden.shape[1:]
    tokens = rows * ns
    width = feats * nx * nz
    scale = 2.0 / tokens
    place = jnp.stack([x_pos * nz + zl_pos, seq_pos * nz])
    place = place.astype(jnp.int32)

    def copied(value, count):
        return jnp.broadcast_to(value[None], (count,) + value.shape)

    def r_of(parts):
        return lax.rsqrt(jnp.sum(parts.astype(f32), axis=(0, 1)) / width + norm_eps)

    resid = swap_x_seq(hidden[0])
    docs = jnp.pad(segment_ids.astype(bf16), ((0, 13), (0, feats - rows)))
    extra = swap_x_seq(jnp.concatenate([gain_attn, gain_ffn, docs]))
    group = lax.all_to_all(copied(jnp.concatenate([resid, extra]), nz), ZL, 0, 0)
    copies, own_rows, gain_a, gain_f = attn_copies(group, hidden[0], nx)
    attn_rows = lax.all_gather(own_rows, "seq")
    attn_cols = lax.all_to_all(copies, "x", 0, 0)

    half = HD // 2
    freq = rope_base ** (-(jnp.arange(half, dtype=f32) * 2.0 / HD))
    angle = jnp.arange(tokens, dtype=f32)[:, None] * freq[None, :]
    table = jnp.concatenate([jnp.cos(angle), jnp.sin(angle)], 1)
    message = project(attn_cols, gain_a, w_query, w_key, w_value, attn_rows, table)
    arrived = lax.all_to_all(lax.all_to_all(message, "x", 0, 0), "seq", 0, 0)
    kv = lax.all_to_all(kv_sum(width, arrived, extra, 2 * nx), ("x", "zb"), 0, 0)
    copies, section_out = attend(arrived, kv, table, resid, nz)
    left_a = attn_left(scale, attn_rows, gain_attn, kv)

    group = lax.all_to_all(copies, ZL, 0, 0)
    copies, message = ffn_copies(group, swap_x_seq(section_out), left_a, nx)
    ffn_cols = lax.all_to_all(copies, "x", 0, 0)
    ffn_rows = lax.all_gather(message, "seq")
    r_ffn = lax.all_gather(r_of(ffn_rows[:, rows : rows + 3, :rows])[None], "x")
    count = lax.axis_size("phase")
    passed = lax.dynamic_slice_in_dim(ffn_rows[:, :rows], seq_pos, 1, 0)
    passed = lax.ppermute(passed, "phase", [(p, (p + 1) % count) for p in range(count)])
    hessians, ffn_diagonal = hessian(
        scale, place, left_a, attn_cols, gain_a, ffn_rows, gain_ffn, r_ffn, ffn_cols, gain_f
    )
    return (passed, hessians[None], ffn_diagonal)


def solution(mesh):
    phase, tensor, seq = (mesh.shape[a] for a in ("phase", "tensor", "seq"))
    lines = Mesh(
        mesh.devices.reshape(phase, tensor // 4, 2, 2, seq), ("phase", "x", "za", "zb", "seq")
    )
    tiled = P("phase", "seq", TENSOR)
    return jax.shard_map(
        on_device,
        mesh=lines,
        in_specs=(
            tiled,
            P("phase", "seq"),
            P("phase", TENSOR),
            P("phase", TENSOR),
            tiled,
            tiled,
            tiled,
        ),
        out_specs=(tiled, P("phase", TENSOR, "seq"), P("phase", GROUP)),
        check_vma=False,
    )
```

```python
import functools

import jax
import jax.numpy as jnp
from jax import lax
from jax.experimental import pallas as pl
from jax.experimental.pallas import tpu as pltpu
from jax.sharding import Mesh, PartitionSpec as P

HD = 128
norm_eps = 1e-05
rope_base = 500000.0
ZL = ("za", "zb")
TENSOR = ("x", "za", "zb")
GROUP = TENSOR + ("seq",)
f32 = jnp.float32
bf16 = jnp.bfloat16
LIMIT = 24 * 1024 * 1024
WIDE = 57 * 1024 * 1024


def swap_x_seq(value):
    nx, nz, ns = lax.axis_size("x"), lax.axis_size(ZL), lax.axis_size("seq")
    pairs = [
        ((x * nz + z) * ns + s, (s * nz + z) * ns + x)
        for x in range(nx)
        for z in range(nz)
        for s in range(ns)
    ]
    return lax.ppermute(value, GROUP, pairs)


def project_kernel(
    cols, gain, wq, wk, wv, first, second,
    out, q_acc, kv_acc, squares, gain_in, wq_in, wk_in, wv_in, done,
):
    step = pl.program_id(0)
    blocks, rows, feats = cols.shape

    def query_copy(z):
        part = pl.ds(pl.multiple_of(z * feats, feats), feats)
        return pltpu.make_async_copy(wq.at[0, part, :], wq_in.at[z], done.at[z])

    parts = wq_in.shape[0]
    others = [
        pltpu.make_async_copy(source, target, done.at[parts + i])
        for i, (source, target) in enumerate(
            [(gain, gain_in), (wk.at[0], wk_in), (wv.at[0], wv_in)]
        )
    ]

    @pl.when(step == 0)
    def _():
        for copy in others:
            copy.start()
        for z in range(parts):
            query_copy(z).start()
        for copy in others:
            copy.wait()

    query_copy(step).wait()
    raw = cols[...].reshape(blocks * rows, feats).astype(f32)
    left = (raw * gain_in[step]).astype(bf16)
    part = jnp.sum(raw * raw, axis=1, keepdims=True)
    here = pl.ds(pl.multiple_of(step * feats, feats), feats)
    kv_w = jnp.concatenate([wk_in[:, here], wv_in[:, here]], 0)
    kv = lax.dot_general(left, kv_w, (((1,), (1,)), ((), ())), preferred_element_type=f32)
    q = jnp.dot(left, wq_in[step], preferred_element_type=f32)

    @pl.when(step == 0)
    def _():
        q_acc[...] = q
        kv_acc[...] = kv
        squares[...] = part

    @pl.when(step > 0)
    def _():
        q_acc[...] += q
        kv_acc[...] += kv
        squares[...] += part

    @pl.when(step == pl.num_programs(0) - 1)
    def _():
        heads = q_acc.shape[1] // HD
        for k in range(blocks):
            block = pl.ds(k * rows, rows)
            out[k, pl.ds(heads * rows, rows), :] = kv_acc[block, :].astype(bf16)
            sums = stacked(three_parts(row_of(squares[block, :])))
            out[k, pl.ds((heads + 1) * rows, 16), :] = sums
            for h in range(heads):
                out[k, pl.ds(h * rows, rows), :] = q_acc[block, pl.ds(h * HD, HD)].astype(bf16)


def project(cols, gain, w_query, w_key, w_value, *after):
    blocks, parts, rows, feats = cols.shape
    q_width, kv_width = w_query.shape[2], 2 * w_key.shape[2]
    heads = q_width // HD
    kept = pl.BlockSpec(memory_space=pltpu.HBM)
    return pl.pallas_call(
        project_kernel,
        grid=(parts,),
        in_specs=[
            pl.BlockSpec((blocks, None, rows, feats), lambda z: (0, z, 0, 0)),
            kept,
            kept,
            kept,
            kept,
        ]
        + [pl.BlockSpec(memory_space=pl.ANY)] * len(after),
        out_specs=fixed((blocks, (heads + 1) * rows + 16, HD)),
        out_shape=pltpu.HBM((blocks, (heads + 1) * rows + 16, HD), bf16),
        scratch_shapes=[
            pltpu.VMEM((blocks * rows, q_width), f32),
            pltpu.VMEM((blocks * rows, kv_width), f32),
            pltpu.VMEM((blocks * rows, 1), f32),
            pltpu.VMEM(gain.shape, f32),
            pltpu.VMEM((parts, feats, q_width), bf16),
            pltpu.VMEM((w_key.shape[2], parts * feats), bf16),
            pltpu.VMEM((w_value.shape[2], parts * feats), bf16),
            pltpu.SemaphoreType.DMA((parts + 3,)),
        ],
        compiler_params=params(WIDE),
        name="project",
    )(cols, gain, w_query, w_key.swapaxes(1, 2), w_value.swapaxes(1, 2), *after)


def fixed(shape):
    return pl.BlockSpec(shape, lambda *at: (0,) * len(shape))


def params(limit=LIMIT):
    return pltpu.CompilerParams(vmem_limit_bytes=limit)


def three_parts(value):
    parts = []
    for _ in range(3):
        part = value.astype(bf16)
        parts.append(part)
        value = value - part.astype(f32)
    return parts


def row_of(column):
    n = column.shape[0]
    same = lax.broadcasted_iota(jnp.int32, (n, n), 0) == lax.broadcasted_iota(jnp.int32, (n, n), 1)
    return jnp.sum(jnp.where(same, column, f32(0.0)), axis=0, keepdims=True)


def stacked(parts, more=()):
    rows = list(parts) + list(more)
    rows.append(jnp.zeros((16 - len(rows), rows[0].shape[1]), f32))
    return jnp.concatenate([row.astype(f32) for row in rows]).astype(bf16)


def attn_copies_kernel(group, own, copies, kept, gain_a, gain_f):
    rows = own.shape[0]
    for k in range(copies.shape[0]):
        copies[k] = group[pl.ds(0, rows), :]
    gains = group[pl.ds(rows, 16), :].astype(f32)
    gain_a[...] = gains[0:1]
    gain_f[...] = gains[1:2]

    @pl.when(pl.program_id(0) == 0)
    def _():
        kept[...] = own[...]


def attn_copies(group, own, count):
    parts, tall, feats = group.shape
    rows = own.shape[0]
    gain = pl.BlockSpec((None, 1, feats), lambda z: (z, 0, 0))
    gain_shape = pltpu.HBM((parts, 1, feats), f32)
    return pl.pallas_call(
        attn_copies_kernel,
        grid=(parts,),
        in_specs=[pl.BlockSpec((None, tall, feats), lambda z: (z, 0, 0)), fixed(own.shape)],
        out_specs=[
            pl.BlockSpec((count, None, rows, feats), lambda z: (0, z, 0, 0)),
            fixed(own.shape),
            gain,
            gain,
        ],
        out_shape=[
            pltpu.HBM((count, parts, rows, feats), bf16),
            pltpu.HBM(own.shape, bf16),
            gain_shape,
            gain_shape,
        ],
        compiler_params=params(),
        name="attn_copies",
    )(group, own)


def ffn_copies_kernel(width, group, sums, own, after, copies, weight):
    step = pl.program_id(0)
    rows, feats = group.shape
    bottom = copies.shape[1] - 16

    @pl.when(step == 0)
    def _():
        r_sq = 1.0 / (jnp.sum(sums[...], axis=0) / width + norm_eps)
        weight[...] = column_of(r_sq)
        tail = jnp.concatenate([stacked(three_parts(r_sq))] * (feats // rows), 1)
        for k in range(copies.shape[0]):
            copies[k, pl.ds(bottom, 16), :] = tail

    block = (group[...].astype(f32) * weight[...]).astype(bf16)
    for k in range(copies.shape[0]):
        copies[k, pl.ds(pl.multiple_of(step * rows, rows), rows), :] = block


def ffn_copies(width, group, sums, count, *after):
    parts, rows, feats = group.shape
    shape = (count, parts * rows + 16, feats)
    return pl.pallas_call(
        functools.partial(ffn_copies_kernel, width),
        grid=(parts,),
        in_specs=[pl.BlockSpec((None, rows, feats), lambda z: (z, 0, 0)), fixed(sums.shape)]
        + [pl.BlockSpec(memory_space=pl.ANY)] * len(after),
        out_specs=fixed(shape),
        out_shape=pltpu.HBM(shape, bf16),
        scratch_shapes=[pltpu.VMEM((rows, 1), f32)],
        compiler_params=params(),
        name="ffn_copies",
    )(group, sums, *after)


def kv_sum_kernel(width, arrived, docs, out):
    rows = out.shape[1] - 16
    kv = jnp.sum(arrived[:, pl.ds(0, rows), :].astype(f32), axis=0).astype(bf16)
    sums = jnp.sum(arrived[:, pl.ds(rows, 16), :].astype(f32), axis=0)
    r = lax.rsqrt((sums[0:1] + sums[1:2] + sums[2:3]) / width + norm_eps)
    tail = stacked(three_parts(r), [docs[...].astype(f32)[2:3, :rows]])
    for copy in range(out.shape[0]):
        out[copy, pl.ds(0, rows), :] = kv
        out[copy, pl.ds(rows, 16), :] = tail


def kv_sum(width, arrived, docs, copies):
    blocks, tall, lanes = arrived.shape
    rows = HD
    last = tall - rows - 16
    return pl.pallas_call(
        functools.partial(kv_sum_kernel, width),
        grid=(1,),
        in_specs=[
            pl.BlockSpec(
                (pl.Element(blocks), pl.Element(rows + 16), pl.Element(lanes)),
                lambda i: (0, last, 0),
            ),
            fixed(docs.shape),
        ],
        out_specs=fixed((copies, rows + 16, lanes)),
        out_shape=pltpu.HBM((copies, rows + 16, lanes), bf16),
        compiler_params=params(),
        name="kv_sum",
    )(arrived, docs)


def rotate(values, table):
    lower = lax.broadcasted_iota(jnp.int32, table.shape, 1) < HD // 2
    swapped = pltpu.roll(table, HD // 2, 1)
    cosine = jnp.where(lower, table, swapped)
    sine = jnp.where(lower, -swapped, table)
    return values * cosine + pltpu.roll(values, HD // 2, 1) * sine


def column_of(row):
    n = row.shape[1]
    same = lax.broadcasted_iota(jnp.int32, (n, n), 0) == lax.broadcasted_iota(jnp.int32, (n, n), 1)
    return jnp.sum(jnp.where(same, row, f32(0.0)), axis=1, keepdims=True)


def attend_kernel(
    q_in, kv_in, table, resid, out, sums,
    keys, values, r_all, docs_all, r_own, docs_own, squares,
):
    rows = out.shape[0]
    tokens = keys.shape[0]
    x_pos = lax.axis_index("x")

    @pl.when(pl.program_id(0) == 0)
    def _():
        lower = lax.broadcasted_iota(jnp.int32, (rows, HD), 1) < HD // 2
        for k in range(tokens // rows):
            first = kv_in[2 * k, pl.ds(0, rows), :].astype(f32)
            second = kv_in[2 * k + 1, pl.ds(0, rows), :].astype(f32)
            tail = kv_in[2 * k, pl.ds(rows, 16), :].astype(f32)
            block = pl.ds(k * rows, rows)
            key = jnp.where(lower, first, pltpu.roll(second, HD // 2, 1))
            keys[block, :] = rotate(key, table[block, :])
            values[block, :] = jnp.where(lower, pltpu.roll(first, HD // 2, 1), second)
            r = tail[0:1] + tail[1:2] + tail[2:3]
            r_all[:, block] = r
            docs_all[:, block] = tail[3:4]

            @pl.when(x_pos == k)
            def _():
                r_own[...] = column_of(r) * (1.0 / HD**0.5)
                docs_own[...] = column_of(tail[3:4])

    query = jnp.sum(q_in[...].astype(f32), axis=0)
    own = pl.ds(pl.multiple_of(x_pos * rows, rows), rows)
    query = rotate(query, table[own, :]) * r_own[...]
    scores = lax.dot_general(
        query, keys[...], (((1,), (1,)), ((), ())),
        preferred_element_type=f32, precision=lax.Precision.HIGHEST,
    )
    scores = scores * r_all[...]
    key_ids = lax.broadcasted_iota(jnp.int32, scores.shape, 1)
    own_ids = lax.broadcasted_iota(jnp.int32, scores.shape, 0) + x_pos * rows
    allowed = (key_ids <= own_ids) & (docs_all[...] == docs_own[...])
    scores = jnp.where(allowed, scores, f32(-1e30))
    peak = jnp.max(scores, axis=-1, keepdims=True)
    weights = jnp.where(allowed, jnp.exp(scores - peak), f32(0.0))
    total = jnp.sum(weights, axis=-1, keepdims=True)
    context = jnp.dot(
        weights * r_all[...], values[...],
        preferred_element_type=f32, precision=lax.Precision.HIGHEST,
    ) / total
    result = (resid[...].astype(f32) + context).astype(bf16)
    out[...] = result
    result = result.astype(f32)
    part = jnp.sum(result * result, axis=1, keepdims=True)

    @pl.when(pl.program_id(0) == 0)
    def _():
        squares[...] = part

    @pl.when(pl.program_id(0) > 0)
    def _():
        squares[...] += part

    @pl.when(pl.program_id(0) == pl.num_programs(0) - 1)
    def _():
        sums[...] = jnp.broadcast_to(row_of(squares[...])[None], sums.shape)


def attend(q_in, kv_in, table, resid, copies):
    rows, feats = resid.shape
    heads, tokens = feats // HD, table.shape[0]
    return pl.pallas_call(
        attend_kernel,
        grid=(heads,),
        in_specs=[
            pl.BlockSpec((q_in.shape[0], rows, HD), lambda h: (0, h, 0)),
        ]
        + [fixed(kv_in.shape), fixed(table.shape)]
        + [pl.BlockSpec((rows, HD), lambda h: (0, h))],
        out_specs=[
            pl.BlockSpec((rows, HD), lambda h: (0, h)),
            fixed((copies, 1, rows)),
        ],
        out_shape=[
            pltpu.HBM((rows, feats), bf16),
            pltpu.HBM((copies, 1, rows), f32),
        ],
        scratch_shapes=[
            pltpu.VMEM((tokens, HD), f32),
            pltpu.VMEM((tokens, HD), f32),
            pltpu.VMEM((1, tokens), f32),
            pltpu.VMEM((1, tokens), f32),
            pltpu.VMEM((rows, 1), f32),
            pltpu.VMEM((rows, 1), f32),
            pltpu.VMEM((rows, 1), f32),
        ],
        compiler_params=params(),
        name="attend",
    )(q_in, kv_in, table, resid)


def attn_left_kernel(scale, own_rows, gain, kv, out):
    blocks, rows, feats = own_rows.shape
    for k in range(blocks):
        parts = kv[2 * k, pl.ds(rows, 16), :].astype(f32)
        r = parts[0:1] + parts[1:2] + parts[2:3]
        turned = (own_rows[k].astype(f32) * gain[...].astype(f32)).T
        out[:, pl.ds(k * rows, rows)] = (turned * (r * r * scale)).astype(bf16)


def attn_left(scale, own_rows, gain, kv_all):
    blocks, rows, feats = own_rows.shape
    arrays = (own_rows, gain, kv_all)
    return pl.pallas_call(
        functools.partial(attn_left_kernel, scale),
        grid=(1,),
        in_specs=[fixed(a.shape) for a in arrays],
        out_specs=fixed((feats, blocks * rows)),
        out_shape=jax.ShapeDtypeStruct((feats, blocks * rows), bf16),
        compiler_params=params(),
        name="attn_left",
    )(*arrays)


def hessian_kernel(
    scale, place, left_a, cols_a, gain_a, ffn_rows, gain_row, r_sq, cols_f, gain_f,
    out, diagonal, left_f, turned_f,
):
    blocks, rows, feats = cols_a.shape
    row, col = place[0], place[1] + pl.program_id(0)

    @pl.when(pl.program_id(0) == 0)
    def _():
        squares = jnp.zeros((rows, 1), f32)
        part = pl.multiple_of(lax.axis_index("seq") * rows, rows)
        for k in range(blocks):
            turned = (ffn_rows[k].astype(f32) * gain_row[...].astype(f32)).T * scale
            parts = r_sq[k].astype(f32)[:, :rows]
            weight = (parts[0:1] + parts[1:2] + parts[2:3]) / scale
            turned_f[...] = turned
            mine = turned_f[pl.ds(part, rows), :]
            squares += jnp.sum(mine * mine * weight, axis=1, keepdims=True)
            left_f[:, pl.ds(k * rows, rows)] = turned.astype(bf16)
        diagonal[...] = row_of(squares)

    def product(left, cols, gain):
        right = cols[...].reshape(blocks * rows, feats)
        return (jnp.dot(left[...], right, preferred_element_type=f32) * gain[...]).astype(bf16)

    @pl.when(row < col)
    def _():
        out[...] = product(left_a, cols_a, gain_a)

    @pl.when(row > col)
    def _():
        out[...] = product(left_f, cols_f, gain_f)

    @pl.when(row == col)
    def _():
        upper = product(left_a, cols_a, gain_a)
        lower = product(left_f, cols_f, gain_f)
        row_ids = lax.broadcasted_iota(jnp.int32, lower.shape, 0)
        col_ids = lax.broadcasted_iota(jnp.int32, lower.shape, 1)
        out[...] = jnp.where(row_ids <= col_ids, upper, lower)


def hessian(scale, place, left_a, cols_a, gain_a, ffn_rows, gain_row, cols_f, gain_f):
    blocks, parts, rows, feats = cols_a.shape
    tokens = blocks * rows

    def upper_at(z, at):
        return jnp.clip(jnp.maximum(z, at[0] - at[1]), 0, parts - 1)

    def lower_at(z, at):
        return jnp.clip(jnp.minimum(z, at[0] - at[1]), 0, parts - 1)

    gain = pl.BlockSpec((None, 1, feats), lambda z, at: (z, 0, 0))
    return pl.pallas_call(
        functools.partial(hessian_kernel, scale),
        grid_spec=pltpu.PrefetchScalarGridSpec(
            num_scalar_prefetch=1,
            grid=(parts,),
            in_specs=[
                fixed(left_a.shape),
                pl.BlockSpec((blocks, None, rows, feats), lambda z, at: (0, upper_at(z, at), 0, 0)),
                gain,
                fixed(ffn_rows.shape),
                fixed(gain_row.shape),
                pl.BlockSpec((blocks, 16, feats), lambda z, at: (0, parts * rows // 16, 0)),
                pl.BlockSpec((blocks, rows, feats), lambda z, at: (0, lower_at(z, at), 0)),
                gain,
            ],
            out_specs=[
                pl.BlockSpec((feats, feats), lambda z, at: (0, z)),
                fixed((1, rows)),
            ],
            scratch_shapes=[pltpu.VMEM((feats, tokens), bf16), pltpu.VMEM((feats, rows), f32)],
        ),
        out_shape=[
            jax.ShapeDtypeStruct((feats, parts * feats), bf16),
            jax.ShapeDtypeStruct((1, rows), f32),
        ],
        compiler_params=params(WIDE),
        name="hessian",
    )(place, left_a, cols_a, gain_a, ffn_rows, gain_row, cols_f, cols_f, gain_f)


def on_device(hidden, segment_ids, gain_attn, gain_ffn, w_query, w_key, w_value):
    x_pos = lax.axis_index("x")
    zl_pos = lax.axis_index(ZL)
    seq_pos = lax.axis_index("seq")
    nx, nz, ns = lax.axis_size("x"), lax.axis_size(ZL), lax.axis_size("seq")
    rows, feats = hidden.shape[1:]
    tokens = rows * ns
    width = feats * nx * nz
    scale = 2.0 / tokens
    place = jnp.stack([x_pos * nz + zl_pos, seq_pos * nz])
    place = place.astype(jnp.int32)

    resid = swap_x_seq(hidden[0])
    docs = jnp.pad(segment_ids.astype(bf16), ((0, 13), (0, feats - rows)))
    extra = swap_x_seq(jnp.concatenate([gain_attn, gain_ffn, docs]))
    group = lax.all_gather(jnp.concatenate([resid, extra]), ZL)
    copies, own_rows, gain_a, gain_f = attn_copies(group, hidden[0], nx)
    attn_rows = lax.all_gather(own_rows, "seq")
    attn_cols = lax.all_to_all(copies, "x", 0, 0)

    half = HD // 2
    freq = rope_base ** (-(jnp.arange(half, dtype=f32) * 2.0 / HD))
    angle = jnp.arange(tokens, dtype=f32)[:, None] * freq[None, :]
    table = jnp.concatenate([jnp.cos(angle), jnp.sin(angle)], 1)
    message = project(attn_cols, gain_a, w_query, w_key, w_value, attn_rows, table)
    arrived = lax.all_to_all(lax.all_to_all(message, "x", 0, 0), "seq", 0, 0)
    kv = lax.all_to_all(kv_sum(width, arrived, extra, 2 * nx), ("x", "zb"), 0, 0)
    ring = ZL + ("seq",)
    section_out, sums = attend(arrived, kv, table, resid, lax.axis_size(ring))
    left_a = attn_left(scale, attn_rows, gain_attn, kv)

    sums = lax.all_to_all(sums, ring, 0, 0)
    out_rows = swap_x_seq(section_out)
    group = lax.all_gather(section_out, ZL)
    copies = ffn_copies(width, group, sums, nx, out_rows, left_a)
    ffn_cols = lax.all_to_all(copies, "x", 0, 0)
    ffn_rows = lax.all_gather(out_rows, "seq")
    count = lax.axis_size("phase")
    passed = lax.dynamic_slice_in_dim(ffn_rows, seq_pos, 1, 0)
    passed = lax.ppermute(passed, "phase", [(p, (p + 1) % count) for p in range(count)])
    hessians, ffn_diagonal = hessian(
        scale, place, left_a, attn_cols, gain_a, ffn_rows, gain_ffn, ffn_cols, gain_f
    )
    return (passed, hessians[None], ffn_diagonal)


def solution(mesh):
    phase, tensor, seq = (mesh.shape[a] for a in ("phase", "tensor", "seq"))
    lines = Mesh(
        mesh.devices.reshape(phase, tensor // 4, 2, 2, seq), ("phase", "x", "za", "zb", "seq")
    )
    tiled = P("phase", "seq", TENSOR)
    return jax.shard_map(
        on_device,
        mesh=lines,
        in_specs=(
            tiled,
            P("phase", "seq"),
            P("phase", TENSOR),
            P("phase", TENSOR),
            tiled,
            tiled,
            tiled,
        ),
        out_specs=(tiled, P("phase", TENSOR, "seq"), P("phase", GROUP)),
        check_vma=False,
    )
```

```python
import functools

import jax
import jax.numpy as jnp
from jax import lax
from jax.experimental import pallas as pl
from jax.experimental.pallas import tpu as pltpu
from jax.sharding import Mesh, PartitionSpec as P

HD = 128
norm_eps = 1e-05
rope_base = 500000.0
ZL = ("za", "zb")
TENSOR = ("x", "za", "zb")
GROUP = TENSOR + ("seq",)
f32 = jnp.float32
bf16 = jnp.bfloat16
LIMIT = 24 * 1024 * 1024
WIDE = 57 * 1024 * 1024
PROJECT = 55 * 1024 * 1024


def swap_x_seq(value):
    nx, nz, ns = lax.axis_size("x"), lax.axis_size(ZL), lax.axis_size("seq")
    pairs = [
        ((x * nz + z) * ns + s, (s * nz + z) * ns + x)
        for x in range(nx)
        for z in range(nz)
        for s in range(ns)
    ]
    return lax.ppermute(value, GROUP, pairs)


def project_kernel(cols, gain, wq, wk, wv, after, out, q_acc, kv_acc, squares):
    step = pl.program_id(0)
    blocks, rows, feats = cols.shape
    raw = cols[...].reshape(blocks * rows, feats).astype(f32)
    left = (raw * gain[...]).astype(bf16)
    part = jnp.sum(raw * raw, axis=1, keepdims=True)
    kv_w = jnp.concatenate([wk[...], wv[...]], 0)
    kv = lax.dot_general(left, kv_w, (((1,), (1,)), ((), ())), preferred_element_type=f32)
    q = jnp.dot(left, wq[...], preferred_element_type=f32)

    @pl.when(step == 0)
    def _():
        q_acc[...] = q
        kv_acc[...] = kv
        squares[...] = part

    @pl.when(step > 0)
    def _():
        q_acc[...] += q
        kv_acc[...] += kv
        squares[...] += part

    @pl.when(step == pl.num_programs(0) - 1)
    def _():
        heads = q_acc.shape[1] // HD
        for k in range(blocks):
            block = pl.ds(k * rows, rows)
            out[k, pl.ds(heads * rows, rows), :] = kv_acc[block, :].astype(bf16)
            sums = stacked(three_parts(row_of(squares[block, :])))
            out[k, pl.ds((heads + 1) * rows, 16), :] = sums
            for h in range(heads):
                out[k, pl.ds(h * rows, rows), :] = q_acc[block, pl.ds(h * HD, HD)].astype(bf16)


def project(cols, gain, w_query, w_key, w_value, after):
    blocks, parts, rows, feats = cols.shape
    q_width, kv_width = w_query.shape[2], 2 * w_key.shape[2]
    heads = q_width // HD
    kv_spec = pl.BlockSpec((None, w_key.shape[2], feats), lambda z: (0, 0, z))
    return pl.pallas_call(
        project_kernel,
        grid=(parts,),
        in_specs=[
            pl.BlockSpec((blocks, None, rows, feats), lambda z: (0, z, 0, 0)),
            pl.BlockSpec((None, 1, feats), lambda z: (z, 0, 0)),
            pl.BlockSpec((None, feats, q_width), lambda z: (0, z, 0)),
            kv_spec,
            kv_spec,
            pl.BlockSpec(memory_space=pl.ANY),
        ],
        out_specs=fixed((blocks, (heads + 1) * rows + 16, HD)),
        out_shape=pltpu.HBM((blocks, (heads + 1) * rows + 16, HD), bf16),
        scratch_shapes=[
            pltpu.VMEM((blocks * rows, q_width), f32),
            pltpu.VMEM((blocks * rows, kv_width), f32),
            pltpu.VMEM((blocks * rows, 1), f32),
        ],
        compiler_params=params(PROJECT),
        name="project",
    )(cols, gain, w_query, w_key.swapaxes(1, 2), w_value.swapaxes(1, 2), after)


def fixed(shape):
    return pl.BlockSpec(shape, lambda *at: (0,) * len(shape))


def params(limit=LIMIT):
    return pltpu.CompilerParams(vmem_limit_bytes=limit)


def three_parts(value):
    parts = []
    for _ in range(3):
        part = value.astype(bf16)
        parts.append(part)
        value = value - part.astype(f32)
    return parts


def row_of(column):
    n = column.shape[0]
    same = lax.broadcasted_iota(jnp.int32, (n, n), 0) == lax.broadcasted_iota(jnp.int32, (n, n), 1)
    return jnp.sum(jnp.where(same, column, f32(0.0)), axis=0, keepdims=True)


def stacked(parts, more=()):
    rows = list(parts) + list(more)
    rows.append(jnp.zeros((16 - len(rows), rows[0].shape[1]), f32))
    return jnp.concatenate([row.astype(f32) for row in rows]).astype(bf16)


def attn_copies_kernel(group, copies, gain_a, gain_f):
    rows = copies.shape[1]
    for k in range(copies.shape[0]):
        copies[k] = group[pl.ds(0, rows), :]
    gains = group[pl.ds(rows, 16), :].astype(f32)
    gain_a[...] = gains[0:1]
    gain_f[...] = gains[1:2]


def attn_copies(group, count):
    parts, tall, feats = group.shape
    rows = tall - 16
    gain = pl.BlockSpec((None, 1, feats), lambda z: (z, 0, 0))
    gain_shape = pltpu.HBM((parts, 1, feats), f32)
    return pl.pallas_call(
        attn_copies_kernel,
        grid=(parts,),
        in_specs=[pl.BlockSpec((None, tall, feats), lambda z: (z, 0, 0))],
        out_specs=[
            pl.BlockSpec((count, None, rows, feats), lambda z: (0, z, 0, 0)),
            gain,
            gain,
        ],
        out_shape=[
            pltpu.HBM((count, parts, rows, feats), bf16),
            gain_shape,
            gain_shape,
        ],
        compiler_params=params(),
        name="attn_copies",
    )(group)


def take_kernel(value, after, out):
    out[...] = value[...]


def take_after(value, after):
    return pl.pallas_call(
        take_kernel,
        grid=(1,),
        in_specs=[fixed(value.shape), pl.BlockSpec(memory_space=pl.ANY)],
        out_specs=fixed(value.shape),
        out_shape=pltpu.HBM(value.shape, value.dtype),
        compiler_params=params(),
        name="take_after",
    )(value, after)


def pile_kernel(top, bottom, after, out):
    rows = top.shape[0]
    out[pl.ds(0, rows), :] = top[...]
    out[pl.ds(rows, bottom.shape[0]), :] = bottom[...]


def pile(top, bottom, after):
    shape = (top.shape[0] + bottom.shape[0], top.shape[1])
    return pl.pallas_call(
        pile_kernel,
        grid=(1,),
        in_specs=[fixed(top.shape), fixed(bottom.shape), pl.BlockSpec(memory_space=pl.ANY)],
        out_specs=fixed(shape),
        out_shape=jax.ShapeDtypeStruct(shape, top.dtype),
        compiler_params=params(),
        name="pile",
    )(top, bottom, after)


def ffn_copies_kernel(width, group, sums, own, after, copies, weight):
    step = pl.program_id(0)
    rows, feats = group.shape
    bottom = copies.shape[1] - 16

    @pl.when(step == 0)
    def _():
        r_sq = 1.0 / (jnp.sum(sums[...], axis=0) / width + norm_eps)
        weight[...] = column_of(r_sq)
        tail = jnp.concatenate([stacked(three_parts(r_sq))] * (feats // rows), 1)
        for k in range(copies.shape[0]):
            copies[k, pl.ds(bottom, 16), :] = tail

    block = (group[...].astype(f32) * weight[...]).astype(bf16)
    for k in range(copies.shape[0]):
        copies[k, pl.ds(pl.multiple_of(step * rows, rows), rows), :] = block


def ffn_copies(width, group, sums, count, *after):
    parts, rows, feats = group.shape
    shape = (count, parts * rows + 16, feats)
    return pl.pallas_call(
        functools.partial(ffn_copies_kernel, width),
        grid=(parts,),
        in_specs=[pl.BlockSpec((None, rows, feats), lambda z: (z, 0, 0)), fixed(sums.shape)]
        + [pl.BlockSpec(memory_space=pl.ANY)] * len(after),
        out_specs=fixed(shape),
        out_shape=pltpu.HBM(shape, bf16),
        scratch_shapes=[pltpu.VMEM((rows, 1), f32)],
        compiler_params=params(),
        name="ffn_copies",
    )(group, sums, *after)


def kv_sum_kernel(width, arrived, docs, out):
    rows = out.shape[1] - 16
    kv = jnp.sum(arrived[:, pl.ds(0, rows), :].astype(f32), axis=0).astype(bf16)
    sums = jnp.sum(arrived[:, pl.ds(rows, 16), :].astype(f32), axis=0)
    r = lax.rsqrt((sums[0:1] + sums[1:2] + sums[2:3]) / width + norm_eps)
    tail = stacked(three_parts(r), [docs[...].astype(f32)[2:3, :rows]])
    for copy in range(out.shape[0]):
        out[copy, pl.ds(0, rows), :] = kv
        out[copy, pl.ds(rows, 16), :] = tail


def kv_sum(width, arrived, docs, copies):
    blocks, tall, lanes = arrived.shape
    rows = HD
    last = tall - rows - 16
    return pl.pallas_call(
        functools.partial(kv_sum_kernel, width),
        grid=(1,),
        in_specs=[
            pl.BlockSpec(
                (pl.Element(blocks), pl.Element(rows + 16), pl.Element(lanes)),
                lambda i: (0, last, 0),
            ),
            fixed(docs.shape),
        ],
        out_specs=fixed((copies, rows + 16, lanes)),
        out_shape=pltpu.HBM((copies, rows + 16, lanes), bf16),
        compiler_params=params(),
        name="kv_sum",
    )(arrived, docs)


def rotate(values, table):
    lower = lax.broadcasted_iota(jnp.int32, table.shape, 1) < HD // 2
    swapped = pltpu.roll(table, HD // 2, 1)
    cosine = jnp.where(lower, table, swapped)
    sine = jnp.where(lower, -swapped, table)
    return values * cosine + pltpu.roll(values, HD // 2, 1) * sine


def column_of(row):
    n = row.shape[1]
    same = lax.broadcasted_iota(jnp.int32, (n, n), 0) == lax.broadcasted_iota(jnp.int32, (n, n), 1)
    return jnp.sum(jnp.where(same, row, f32(0.0)), axis=1, keepdims=True)


def attend_kernel(
    q_in, kv_in, table, resid, out, sums,
    keys, values, r_all, docs_all, r_own, docs_own, squares,
):
    rows = out.shape[0]
    tokens = keys.shape[0]
    x_pos = lax.axis_index("x")

    @pl.when(pl.program_id(0) == 0)
    def _():
        lower = lax.broadcasted_iota(jnp.int32, (rows, HD), 1) < HD // 2
        for k in range(tokens // rows):
            first = kv_in[2 * k, pl.ds(0, rows), :].astype(f32)
            second = kv_in[2 * k + 1, pl.ds(0, rows), :].astype(f32)
            tail = kv_in[2 * k, pl.ds(rows, 16), :].astype(f32)
            block = pl.ds(k * rows, rows)
            key = jnp.where(lower, first, pltpu.roll(second, HD // 2, 1))
            keys[block, :] = rotate(key, table[block, :])
            values[block, :] = jnp.where(lower, pltpu.roll(first, HD // 2, 1), second)
            r = tail[0:1] + tail[1:2] + tail[2:3]
            r_all[:, block] = r
            docs_all[:, block] = tail[3:4]

            @pl.when(x_pos == k)
            def _():
                r_own[...] = column_of(r) * (1.0 / HD**0.5)
                docs_own[...] = column_of(tail[3:4])

    query = jnp.sum(q_in[...].astype(f32), axis=0)
    own = pl.ds(pl.multiple_of(x_pos * rows, rows), rows)
    query = rotate(query, table[own, :]) * r_own[...]
    scores = lax.dot_general(
        query, keys[...], (((1,), (1,)), ((), ())),
        preferred_element_type=f32, precision=lax.Precision.HIGHEST,
    )
    scores = scores * r_all[...]
    key_ids = lax.broadcasted_iota(jnp.int32, scores.shape, 1)
    own_ids = lax.broadcasted_iota(jnp.int32, scores.shape, 0) + x_pos * rows
    allowed = (key_ids <= own_ids) & (docs_all[...] == docs_own[...])
    scores = jnp.where(allowed, scores, f32(-1e30))
    peak = jnp.max(scores, axis=-1, keepdims=True)
    weights = jnp.where(allowed, jnp.exp(scores - peak), f32(0.0))
    total = jnp.sum(weights, axis=-1, keepdims=True)
    context = jnp.dot(
        weights * r_all[...], values[...],
        preferred_element_type=f32, precision=lax.Precision.HIGHEST,
    ) / total
    result = (resid[...].astype(f32) + context).astype(bf16)
    out[...] = result
    result = result.astype(f32)
    part = jnp.sum(result * result, axis=1, keepdims=True)

    @pl.when(pl.program_id(0) == 0)
    def _():
        squares[...] = part

    @pl.when(pl.program_id(0) > 0)
    def _():
        squares[...] += part

    @pl.when(pl.program_id(0) == pl.num_programs(0) - 1)
    def _():
        sums[...] = jnp.broadcast_to(row_of(squares[...])[None], sums.shape)


def attend(q_in, kv_in, table, resid, copies):
    rows, feats = resid.shape
    heads, tokens = feats // HD, table.shape[0]
    return pl.pallas_call(
        attend_kernel,
        grid=(heads,),
        in_specs=[
            pl.BlockSpec((q_in.shape[0], rows, HD), lambda h: (0, h, 0)),
        ]
        + [fixed(kv_in.shape), fixed(table.shape)]
        + [pl.BlockSpec((rows, HD), lambda h: (0, h))],
        out_specs=[
            pl.BlockSpec((rows, HD), lambda h: (0, h)),
            fixed((copies, 1, rows)),
        ],
        out_shape=[
            pltpu.HBM((rows, feats), bf16),
            pltpu.HBM((copies, 1, rows), f32),
        ],
        scratch_shapes=[
            pltpu.VMEM((tokens, HD), f32),
            pltpu.VMEM((tokens, HD), f32),
            pltpu.VMEM((1, tokens), f32),
            pltpu.VMEM((1, tokens), f32),
            pltpu.VMEM((rows, 1), f32),
            pltpu.VMEM((rows, 1), f32),
            pltpu.VMEM((rows, 1), f32),
        ],
        compiler_params=params(),
        name="attend",
    )(q_in, kv_in, table, resid)


def attn_left_kernel(scale, own_rows, gain, kv, out):
    blocks, rows, feats = own_rows.shape
    for k in range(blocks):
        parts = kv[2 * k, pl.ds(rows, 16), :].astype(f32)
        r = parts[0:1] + parts[1:2] + parts[2:3]
        turned = (own_rows[k].astype(f32) * gain[...].astype(f32)).T
        out[:, pl.ds(k * rows, rows)] = (turned * (r * r * scale)).astype(bf16)


def attn_left(scale, own_rows, gain, kv_all):
    blocks, rows, feats = own_rows.shape
    arrays = (own_rows, gain, kv_all)
    return pl.pallas_call(
        functools.partial(attn_left_kernel, scale),
        grid=(1,),
        in_specs=[fixed(a.shape) for a in arrays],
        out_specs=fixed((feats, blocks * rows)),
        out_shape=jax.ShapeDtypeStruct((feats, blocks * rows), bf16),
        compiler_params=params(),
        name="attn_left",
    )(*arrays)


def hessian_kernel(
    scale, place, left_a, cols_a, gain_a, ffn_rows, gain_row, r_sq, cols_f, gain_f,
    out, diagonal, left_f, turned_f,
):
    blocks, rows, feats = cols_a.shape
    row, col = place[0], place[1] + pl.program_id(0)

    @pl.when(pl.program_id(0) == 0)
    def _():
        squares = jnp.zeros((rows, 1), f32)
        part = pl.multiple_of(lax.axis_index("seq") * rows, rows)
        for k in range(blocks):
            turned = (ffn_rows[k].astype(f32) * gain_row[...].astype(f32)).T * scale
            parts = r_sq[k].astype(f32)[:, :rows]
            weight = (parts[0:1] + parts[1:2] + parts[2:3]) / scale
            turned_f[...] = turned
            mine = turned_f[pl.ds(part, rows), :]
            squares += jnp.sum(mine * mine * weight, axis=1, keepdims=True)
            left_f[:, pl.ds(k * rows, rows)] = turned.astype(bf16)
        diagonal[...] = row_of(squares)

    def product(left, cols, gain):
        right = cols[...].reshape(blocks * rows, feats)
        return (jnp.dot(left[...], right, preferred_element_type=f32) * gain[...]).astype(bf16)

    @pl.when(row < col)
    def _():
        out[...] = product(left_a, cols_a, gain_a)

    @pl.when(row > col)
    def _():
        out[...] = product(left_f, cols_f, gain_f)

    @pl.when(row == col)
    def _():
        upper = product(left_a, cols_a, gain_a)
        lower = product(left_f, cols_f, gain_f)
        row_ids = lax.broadcasted_iota(jnp.int32, lower.shape, 0)
        col_ids = lax.broadcasted_iota(jnp.int32, lower.shape, 1)
        out[...] = jnp.where(row_ids <= col_ids, upper, lower)


def hessian(scale, place, left_a, cols_a, gain_a, ffn_rows, gain_row, cols_f, gain_f):
    blocks, parts, rows, feats = cols_a.shape
    tokens = blocks * rows

    def upper_at(z, at):
        return jnp.clip(jnp.maximum(z, at[0] - at[1]), 0, parts - 1)

    def lower_at(z, at):
        return jnp.clip(jnp.minimum(z, at[0] - at[1]), 0, parts - 1)

    gain = pl.BlockSpec((None, 1, feats), lambda z, at: (z, 0, 0))
    return pl.pallas_call(
        functools.partial(hessian_kernel, scale),
        grid_spec=pltpu.PrefetchScalarGridSpec(
            num_scalar_prefetch=1,
            grid=(parts,),
            in_specs=[
                fixed(left_a.shape),
                pl.BlockSpec((blocks, None, rows, feats), lambda z, at: (0, upper_at(z, at), 0, 0)),
                gain,
                fixed(ffn_rows.shape),
                fixed(gain_row.shape),
                pl.BlockSpec((blocks, 16, feats), lambda z, at: (0, parts * rows // 16, 0)),
                pl.BlockSpec((blocks, rows, feats), lambda z, at: (0, lower_at(z, at), 0)),
                gain,
            ],
            out_specs=[
                pl.BlockSpec((feats, feats), lambda z, at: (0, z)),
                fixed((1, rows)),
            ],
            scratch_shapes=[pltpu.VMEM((feats, tokens), bf16), pltpu.VMEM((feats, rows), f32)],
        ),
        out_shape=[
            jax.ShapeDtypeStruct((feats, parts * feats), bf16),
            jax.ShapeDtypeStruct((1, rows), f32),
        ],
        compiler_params=params(WIDE),
        name="hessian",
    )(place, left_a, cols_a, gain_a, ffn_rows, gain_row, cols_f, cols_f, gain_f)


def on_device(hidden, segment_ids, gain_attn, gain_ffn, w_query, w_key, w_value):
    x_pos = lax.axis_index("x")
    zl_pos = lax.axis_index(ZL)
    seq_pos = lax.axis_index("seq")
    nx, nz, ns = lax.axis_size("x"), lax.axis_size(ZL), lax.axis_size("seq")
    rows, feats = hidden.shape[1:]
    tokens = rows * ns
    width = feats * nx * nz
    scale = 2.0 / tokens
    place = jnp.stack([x_pos * nz + zl_pos, seq_pos * nz])
    place = place.astype(jnp.int32)

    resid = swap_x_seq(hidden[0])
    docs = jnp.pad(segment_ids.astype(bf16), ((0, 13), (0, feats - rows)))
    extra = swap_x_seq(jnp.concatenate([gain_attn, gain_ffn, docs]))
    half = HD // 2
    freq = rope_base ** (-(jnp.arange(half, dtype=f32) * 2.0 / HD))
    angle = jnp.arange(tokens, dtype=f32)[:, None] * freq[None, :]
    table = jnp.concatenate([jnp.cos(angle), jnp.sin(angle)], 1)
    group = lax.all_gather(pile(resid, extra, table), ZL)
    copies, gain_a, gain_f = attn_copies(group, nx)
    attn_rows = lax.all_gather(take_after(hidden[0], gain_a), "seq")
    attn_cols = lax.all_to_all(copies, "x", 0, 0)

    message = project(attn_cols, gain_a, w_query, w_key, w_value, attn_rows)
    arrived = lax.all_to_all(lax.all_to_all(message, "x", 0, 0), "seq", 0, 0)
    kv = lax.all_to_all(kv_sum(width, arrived, extra, 2 * nx), ("x", "zb"), 0, 0)
    ring = ZL + ("seq",)
    section_out, sums = attend(arrived, kv, table, resid, lax.axis_size(ring))
    left_a = attn_left(scale, attn_rows, gain_attn, kv)

    sums = lax.all_to_all(sums, ring, 0, 0)
    out_rows = swap_x_seq(section_out)
    group = lax.all_gather(section_out, ZL)
    copies = ffn_copies(width, group, sums, nx, out_rows, left_a)
    ffn_cols = lax.all_to_all(copies, "x", 0, 0)
    ffn_rows = lax.all_gather(out_rows, "seq")
    count = lax.axis_size("phase")
    passed = lax.ppermute(out_rows, "phase", [(p, (p + 1) % count) for p in range(count)])[None]
    hessians, ffn_diagonal = hessian(
        scale, place, left_a, attn_cols, gain_a, ffn_rows, gain_ffn, ffn_cols, gain_f
    )
    return (passed, hessians[None], ffn_diagonal)


def solution(mesh):
    phase, tensor, seq = (mesh.shape[a] for a in ("phase", "tensor", "seq"))
    lines = Mesh(
        mesh.devices.reshape(phase, tensor // 4, 2, 2, seq), ("phase", "x", "za", "zb", "seq")
    )
    tiled = P("phase", "seq", TENSOR)
    return jax.shard_map(
        on_device,
        mesh=lines,
        in_specs=(
            tiled,
            P("phase", "seq"),
            P("phase", TENSOR),
            P("phase", TENSOR),
            tiled,
            tiled,
            tiled,
        ),
        out_specs=(tiled, P("phase", TENSOR, "seq"), P("phase", GROUP)),
        check_vma=False,
    )
```

```python
import functools

import jax
import jax.numpy as jnp
from jax import lax
from jax.experimental import pallas as pl
from jax.experimental.pallas import tpu as pltpu
from jax.sharding import Mesh, PartitionSpec as P

HD = 128
norm_eps = 1e-05
rope_base = 500000.0
ZL = ("za", "zb")
TENSOR = ("x", "za", "zb")
GROUP = TENSOR + ("seq",)
f32 = jnp.float32
bf16 = jnp.bfloat16
LIMIT = 24 * 1024 * 1024
WIDE = 57 * 1024 * 1024
PROJECT = 55 * 1024 * 1024


def swap_x_seq(value):
    nx, nz, ns = lax.axis_size("x"), lax.axis_size(ZL), lax.axis_size("seq")
    pairs = [
        ((x * nz + z) * ns + s, (s * nz + z) * ns + x)
        for x in range(nx)
        for z in range(nz)
        for s in range(ns)
    ]
    return lax.ppermute(value, GROUP, pairs)


def project_kernel(cols, gain, wq, wk, wv, after, out, q_acc, kv_acc, squares):
    step = pl.program_id(0)
    blocks, rows, feats = cols.shape
    raw = cols[...].reshape(blocks * rows, feats).astype(f32)
    left = (raw * gain[...]).astype(bf16)
    part = jnp.sum(raw * raw, axis=1, keepdims=True)
    kv_w = jnp.concatenate([wk[...], wv[...]], 0)
    kv = lax.dot_general(left, kv_w, (((1,), (1,)), ((), ())), preferred_element_type=f32)
    q = jnp.dot(left, wq[...], preferred_element_type=f32)

    @pl.when(step == 0)
    def _():
        q_acc[...] = q
        kv_acc[...] = kv
        squares[...] = part

    @pl.when(step > 0)
    def _():
        q_acc[...] += q
        kv_acc[...] += kv
        squares[...] += part

    @pl.when(step == pl.num_programs(0) - 1)
    def _():
        heads = q_acc.shape[1] // HD
        for k in range(blocks):
            block = pl.ds(k * rows, rows)
            out[k, pl.ds(heads * rows, rows), :] = kv_acc[block, :].astype(bf16)
            sums = stacked(three_parts(row_of(squares[block, :])))
            out[k, pl.ds((heads + 1) * rows, 16), :] = sums
            for h in range(heads):
                out[k, pl.ds(h * rows, rows), :] = q_acc[block, pl.ds(h * HD, HD)].astype(bf16)


def project(cols, gain, w_query, w_key, w_value, after):
    blocks, parts, rows, feats = cols.shape
    q_width, kv_width = w_query.shape[2], 2 * w_key.shape[2]
    heads = q_width // HD
    kv_spec = pl.BlockSpec((None, w_key.shape[2], feats), lambda z: (0, 0, z))
    return pl.pallas_call(
        project_kernel,
        grid=(parts,),
        in_specs=[
            pl.BlockSpec((blocks, None, rows, feats), lambda z: (0, z, 0, 0)),
            pl.BlockSpec((None, 1, feats), lambda z: (z, 0, 0)),
            pl.BlockSpec((None, feats, q_width), lambda z: (0, z, 0)),
            kv_spec,
            kv_spec,
            pl.BlockSpec(memory_space=pl.ANY),
        ],
        out_specs=fixed((blocks, (heads + 1) * rows + 16, HD)),
        out_shape=pltpu.HBM((blocks, (heads + 1) * rows + 16, HD), bf16),
        scratch_shapes=[
            pltpu.VMEM((blocks * rows, q_width), f32),
            pltpu.VMEM((blocks * rows, kv_width), f32),
            pltpu.VMEM((blocks * rows, 1), f32),
        ],
        compiler_params=params(PROJECT),
        name="project",
    )(cols, gain, w_query, w_key.swapaxes(1, 2), w_value.swapaxes(1, 2), after)


def fixed(shape):
    return pl.BlockSpec(shape, lambda *at: (0,) * len(shape))


def params(limit=LIMIT):
    return pltpu.CompilerParams(vmem_limit_bytes=limit)


def three_parts(value):
    parts = []
    for _ in range(3):
        part = value.astype(bf16)
        parts.append(part)
        value = value - part.astype(f32)
    return parts


def row_of(column):
    n = column.shape[0]
    same = lax.broadcasted_iota(jnp.int32, (n, n), 0) == lax.broadcasted_iota(jnp.int32, (n, n), 1)
    return jnp.sum(jnp.where(same, column, f32(0.0)), axis=0, keepdims=True)


def stacked(parts, more=()):
    rows = list(parts) + list(more)
    rows.append(jnp.zeros((16 - len(rows), rows[0].shape[1]), f32))
    return jnp.concatenate([row.astype(f32) for row in rows]).astype(bf16)


def attn_copies_kernel(group, copies, gain_a, gain_f):
    rows = copies.shape[1]
    for k in range(copies.shape[0]):
        copies[k] = group[pl.ds(0, rows), :]
    gains = group[pl.ds(rows, 16), :].astype(f32)
    gain_a[...] = gains[0:1]
    gain_f[...] = gains[1:2]


def attn_copies(group, count):
    parts, tall, feats = group.shape
    rows = tall - 16
    gain = pl.BlockSpec((None, 1, feats), lambda z: (z, 0, 0))
    gain_shape = pltpu.HBM((parts, 1, feats), f32)
    return pl.pallas_call(
        attn_copies_kernel,
        grid=(parts,),
        in_specs=[pl.BlockSpec((None, tall, feats), lambda z: (z, 0, 0))],
        out_specs=[
            pl.BlockSpec((count, None, rows, feats), lambda z: (0, z, 0, 0)),
            gain,
            gain,
        ],
        out_shape=[
            pltpu.HBM((count, parts, rows, feats), bf16),
            gain_shape,
            gain_shape,
        ],
        compiler_params=params(),
        name="attn_copies",
    )(group)


def take_kernel(value, after, out):
    out[...] = value[...]


def take_after(value, after):
    return pl.pallas_call(
        take_kernel,
        grid=(1,),
        in_specs=[fixed(value.shape), pl.BlockSpec(memory_space=pl.ANY)],
        out_specs=fixed(value.shape),
        out_shape=pltpu.HBM(value.shape, value.dtype),
        compiler_params=params(),
        name="take_after",
    )(value, after)


def pile_kernel(top, bottom, after, out):
    rows = top.shape[0]
    out[pl.ds(0, rows), :] = top[...]
    out[pl.ds(rows, bottom.shape[0]), :] = bottom[...]


def pile(top, bottom, after):
    shape = (top.shape[0] + bottom.shape[0], top.shape[1])
    return pl.pallas_call(
        pile_kernel,
        grid=(1,),
        in_specs=[fixed(top.shape), fixed(bottom.shape), pl.BlockSpec(memory_space=pl.ANY)],
        out_specs=fixed(shape),
        out_shape=jax.ShapeDtypeStruct(shape, top.dtype),
        compiler_params=params(),
        name="pile",
    )(top, bottom, after)


def total_of(parts):
    parts = parts.astype(f32)
    return parts[0:1] + parts[1:2] + parts[2:3]


def below(row, feats):
    return jnp.concatenate([stacked(three_parts(row))] * (feats // row.shape[1]), 1)


def ffn_copies_kernel(group, own, after, copies, message, sums):
    step = pl.program_id(0)
    rows, feats = own.shape
    for k in range(copies.shape[0]):
        copies[k] = group[pl.ds(0, rows), :]
    part = total_of(group[pl.ds(rows, 16), :])[:, :rows]

    @pl.when(step == 0)
    def _():
        message[pl.ds(0, rows), :] = own[...]
        sums[...] = part

    @pl.when(step > 0)
    def _():
        sums[...] += part

    @pl.when(step == pl.num_programs(0) - 1)
    def _():
        message[pl.ds(rows, 16), :] = below(sums[...], feats)


def ffn_copies(group, own, count, after):
    parts, tall, feats = group.shape
    rows = own.shape[0]
    return pl.pallas_call(
        ffn_copies_kernel,
        grid=(parts,),
        in_specs=[
            pl.BlockSpec((None, tall, feats), lambda z: (z, 0, 0)),
            fixed(own.shape),
            pl.BlockSpec(memory_space=pl.ANY),
        ],
        out_specs=[
            pl.BlockSpec((count, None, rows, feats), lambda z: (0, z, 0, 0)),
            fixed((tall, feats)),
        ],
        out_shape=[
            pltpu.HBM((count, parts, rows, feats), bf16),
            pltpu.HBM((tall, feats), bf16),
        ],
        scratch_shapes=[pltpu.VMEM((1, rows), f32)],
        compiler_params=params(),
        name="ffn_copies",
    )(group, own, after)


def kv_sum_kernel(width, arrived, docs, out):
    rows = out.shape[1] - 16
    kv = jnp.sum(arrived[:, pl.ds(0, rows), :].astype(f32), axis=0).astype(bf16)
    sums = jnp.sum(arrived[:, pl.ds(rows, 16), :].astype(f32), axis=0)
    r = lax.rsqrt((sums[0:1] + sums[1:2] + sums[2:3]) / width + norm_eps)
    tail = stacked(three_parts(r), [docs[...].astype(f32)[2:3, :rows]])
    for copy in range(out.shape[0]):
        out[copy, pl.ds(0, rows), :] = kv
        out[copy, pl.ds(rows, 16), :] = tail


def kv_sum(width, arrived, docs, copies):
    blocks, tall, lanes = arrived.shape
    rows = HD
    last = tall - rows - 16
    return pl.pallas_call(
        functools.partial(kv_sum_kernel, width),
        grid=(1,),
        in_specs=[
            pl.BlockSpec(
                (pl.Element(blocks), pl.Element(rows + 16), pl.Element(lanes)),
                lambda i: (0, last, 0),
            ),
            fixed(docs.shape),
        ],
        out_specs=fixed((copies, rows + 16, lanes)),
        out_shape=pltpu.HBM((copies, rows + 16, lanes), bf16),
        compiler_params=params(),
        name="kv_sum",
    )(arrived, docs)


def rotate(values, table):
    lower = lax.broadcasted_iota(jnp.int32, table.shape, 1) < HD // 2
    swapped = pltpu.roll(table, HD // 2, 1)
    cosine = jnp.where(lower, table, swapped)
    sine = jnp.where(lower, -swapped, table)
    return values * cosine + pltpu.roll(values, HD // 2, 1) * sine


def column_of(row):
    n = row.shape[1]
    same = lax.broadcasted_iota(jnp.int32, (n, n), 0) == lax.broadcasted_iota(jnp.int32, (n, n), 1)
    return jnp.sum(jnp.where(same, row, f32(0.0)), axis=1, keepdims=True)


def halves(value):
    high = value.astype(bf16)
    return high, (value - high.astype(f32)).astype(bf16)


def attend_kernel(q_in, kv_in, table, resid, copies, out, keys, values, r_all, docs_all):
    rows, feats = out.shape
    heads = feats // HD
    tokens = keys.shape[0]
    x_pos = lax.axis_index("x")
    lower = lax.broadcasted_iota(jnp.int32, (rows, HD), 1) < HD // 2
    for k in range(tokens // rows):
        first = kv_in[2 * k, pl.ds(0, rows), :].astype(f32)
        second = kv_in[2 * k + 1, pl.ds(0, rows), :].astype(f32)
        tail = kv_in[2 * k, pl.ds(rows, 16), :].astype(f32)
        block = pl.ds(k * rows, rows)
        key = jnp.where(lower, first, pltpu.roll(second, HD // 2, 1))
        high, low = halves(rotate(key, table[block, :]))
        keys[block, :] = jnp.concatenate([high, high, low], 1)
        value = jnp.where(lower, pltpu.roll(first, HD // 2, 1), second).astype(bf16)
        values[block, :] = value
        values[pl.ds(tokens + k * rows, rows), :] = value
        r_all[:, block] = total_of(tail)
        docs_all[:, block] = tail[3:4]

    own = pl.ds(pl.multiple_of(x_pos * rows, rows), rows)
    r_own = column_of(r_all[:, own]) * (1.0 / HD**0.5)
    key_ids = lax.broadcasted_iota(jnp.int32, (rows, tokens), 1)
    own_ids = lax.broadcasted_iota(jnp.int32, (rows, tokens), 0) + x_pos * rows
    allowed = (key_ids <= own_ids) & (docs_all[...] == column_of(docs_all[:, own]))
    squares = jnp.zeros((rows, 1), f32)
    for h in range(heads):
        query = jnp.sum(q_in[:, pl.ds(h * rows, rows), :].astype(f32), axis=0)
        high, low = halves(rotate(query, table[own, :]) * r_own)
        scores = lax.dot_general(
            jnp.concatenate([high, low, high], 1), keys[...], (((1,), (1,)), ((), ())),
            preferred_element_type=f32,
        )
        scores = jnp.where(allowed, scores * r_all[...], f32(-1e30))
        peak = jnp.max(scores, axis=-1, keepdims=True)
        weights = jnp.where(allowed, jnp.exp(scores - peak), f32(0.0))
        total = jnp.sum(weights, axis=-1, keepdims=True)
        weights = jnp.concatenate(halves(weights * r_all[...]), 1)
        context = jnp.dot(weights, values[...], preferred_element_type=f32) / total
        lanes = pl.ds(h * HD, HD)
        result = (resid[:, lanes].astype(f32) + context).astype(bf16)
        out[:, lanes] = result
        for copy in range(copies.shape[0]):
            copies[copy, pl.ds(0, rows), lanes] = result
        result = result.astype(f32)
        squares += jnp.sum(result * result, axis=1, keepdims=True)
    tail = below(row_of(squares), feats)
    for copy in range(copies.shape[0]):
        copies[copy, pl.ds(rows, 16), :] = tail


def attend(q_in, kv_in, table, resid, copies):
    rows, feats = resid.shape
    heads, tokens = feats // HD, table.shape[0]
    shape = (copies, rows + 16, feats)
    return pl.pallas_call(
        attend_kernel,
        grid=(1,),
        in_specs=[
            fixed((q_in.shape[0], heads * rows, HD)),
            fixed(kv_in.shape),
            fixed(table.shape),
            fixed(resid.shape),
        ],
        out_specs=[fixed(shape), fixed(resid.shape)],
        out_shape=[pltpu.HBM(shape, bf16), pltpu.HBM(resid.shape, bf16)],
        scratch_shapes=[
            pltpu.VMEM((tokens, 3 * HD), bf16),
            pltpu.VMEM((2 * tokens, HD), bf16),
            pltpu.VMEM((1, tokens), f32),
            pltpu.VMEM((1, tokens), f32),
        ],
        compiler_params=params(),
        name="attend",
    )(q_in, kv_in, table, resid)


def attn_left_kernel(scale, own_rows, gain, kv, out):
    blocks, rows, feats = own_rows.shape
    for k in range(blocks):
        parts = kv[2 * k, pl.ds(rows, 16), :].astype(f32)
        r = parts[0:1] + parts[1:2] + parts[2:3]
        turned = (own_rows[k].astype(f32) * gain[...].astype(f32)).T
        out[:, pl.ds(k * rows, rows)] = (turned * (r * r * scale)).astype(bf16)


def attn_left(scale, own_rows, gain, kv_all):
    blocks, rows, feats = own_rows.shape
    arrays = (own_rows, gain, kv_all)
    return pl.pallas_call(
        functools.partial(attn_left_kernel, scale),
        grid=(1,),
        in_specs=[fixed(a.shape) for a in arrays],
        out_specs=fixed((feats, blocks * rows)),
        out_shape=jax.ShapeDtypeStruct((feats, blocks * rows), bf16),
        compiler_params=params(),
        name="attn_left",
    )(*arrays)


def hessian_kernel(
    scale, width, place, left_a, cols_a, gain_a, ffn_rows, gain_row, total, cols_f, gain_f,
    out, diagonal, left_f,
):
    blocks, rows, feats = cols_a.shape
    row, col = place[0], place[1] + pl.program_id(0)

    @pl.when(pl.program_id(0) == 0)
    def _():
        part = pl.ds(pl.multiple_of(lax.axis_index("seq") * rows, rows), rows)
        squares = jnp.zeros((1, rows), f32)
        for k in range(blocks):
            weight = column_of(scale / (total[k] / width + norm_eps))
            block = ffn_rows[k, pl.ds(0, rows), :].astype(f32) * gain_row[...].astype(f32)
            left_f[:, pl.ds(k * rows, rows)] = (block * weight).astype(bf16).T
            mine = ffn_rows[k, pl.ds(0, rows), part].astype(f32) * gain_row[:, part].astype(f32)
            squares += jnp.sum(mine * mine * weight, axis=0, keepdims=True)
        diagonal[...] = squares

    def product(left, cols, gain):
        right = cols[...].reshape(blocks * rows, feats)
        return (jnp.dot(left[...], right, preferred_element_type=f32) * gain[...]).astype(bf16)

    @pl.when(row < col)
    def _():
        out[...] = product(left_a, cols_a, gain_a)

    @pl.when(row > col)
    def _():
        out[...] = product(left_f, cols_f, gain_f)

    @pl.when(row == col)
    def _():
        upper = product(left_a, cols_a, gain_a)
        lower = product(left_f, cols_f, gain_f)
        row_ids = lax.broadcasted_iota(jnp.int32, lower.shape, 0)
        col_ids = lax.broadcasted_iota(jnp.int32, lower.shape, 1)
        out[...] = jnp.where(row_ids <= col_ids, upper, lower)


def hessian(
    scale, width, place, left_a, cols_a, gain_a, ffn_rows, gain_row, total, cols_f, gain_f
):
    blocks, parts, rows, feats = cols_a.shape
    tokens = blocks * rows

    def upper_at(z, at):
        return jnp.clip(jnp.maximum(z, at[0] - at[1]), 0, parts - 1)

    def lower_at(z, at):
        return jnp.clip(jnp.minimum(z, at[0] - at[1]), 0, parts - 1)

    gain = pl.BlockSpec((None, 1, feats), lambda z, at: (z, 0, 0))
    return pl.pallas_call(
        functools.partial(hessian_kernel, scale, width),
        grid_spec=pltpu.PrefetchScalarGridSpec(
            num_scalar_prefetch=1,
            grid=(parts,),
            in_specs=[
                fixed(left_a.shape),
                pl.BlockSpec((blocks, None, rows, feats), lambda z, at: (0, upper_at(z, at), 0, 0)),
                gain,
                fixed(ffn_rows.shape),
                fixed(gain_row.shape),
                fixed(total.shape),
                pl.BlockSpec((blocks, None, rows, feats), lambda z, at: (0, lower_at(z, at), 0, 0)),
                gain,
            ],
            out_specs=[
                pl.BlockSpec((feats, feats), lambda z, at: (0, z)),
                fixed((1, rows)),
            ],
            scratch_shapes=[pltpu.VMEM((feats, tokens), bf16)],
        ),
        out_shape=[
            jax.ShapeDtypeStruct((feats, parts * feats), bf16),
            jax.ShapeDtypeStruct((1, rows), f32),
        ],
        compiler_params=params(WIDE),
        name="hessian",
    )(place, left_a, cols_a, gain_a, ffn_rows, gain_row, total, cols_f, gain_f)


def on_device(hidden, segment_ids, gain_attn, gain_ffn, w_query, w_key, w_value):
    x_pos = lax.axis_index("x")
    zl_pos = lax.axis_index(ZL)
    seq_pos = lax.axis_index("seq")
    nx, nz, ns = lax.axis_size("x"), lax.axis_size(ZL), lax.axis_size("seq")
    rows, feats = hidden.shape[1:]
    tokens = rows * ns
    width = feats * nx * nz
    scale = 2.0 / tokens
    place = jnp.stack([x_pos * nz + zl_pos, seq_pos * nz])
    place = place.astype(jnp.int32)

    resid = swap_x_seq(hidden[0])
    docs = jnp.pad(segment_ids.astype(bf16), ((0, 13), (0, feats - rows)))
    extra = swap_x_seq(jnp.concatenate([gain_attn, gain_ffn, docs]))
    half = HD // 2
    freq = rope_base ** (-(jnp.arange(half, dtype=f32) * 2.0 / HD))
    angle = jnp.arange(tokens, dtype=f32)[:, None] * freq[None, :]
    table = jnp.concatenate([jnp.cos(angle), jnp.sin(angle)], 1)
    group = lax.all_gather(pile(resid, extra, table), ZL)
    copies, gain_a, gain_f = attn_copies(group, nx)
    attn_rows = lax.all_gather(take_after(hidden[0], gain_a), "seq")
    attn_cols = lax.all_to_all(copies, "x", 0, 0)

    message = project(attn_cols, gain_a, w_query, w_key, w_value, attn_rows)
    arrived = lax.all_to_all(lax.all_to_all(message, "x", 0, 0), "seq", 0, 0)
    kv = lax.all_to_all(kv_sum(width, arrived, extra, 2 * nx), ("x", "zb"), 0, 0)
    copies, section_out = attend(arrived, kv, table, resid, nz)
    left_a = attn_left(scale, attn_rows, gain_attn, kv)

    out_rows = swap_x_seq(section_out)
    group = lax.all_to_all(copies, ZL, 0, 0)
    copies, message = ffn_copies(group, out_rows, nx, left_a)
    ffn_cols = lax.all_to_all(copies, "x", 0, 0)
    ffn_rows = lax.all_gather(message, "seq")
    total = jnp.sum(ffn_rows[:, rows : rows + 3, :rows].astype(f32), axis=(0, 1))
    total = lax.all_gather(total[None], "x")
    count = lax.axis_size("phase")
    passed = lax.dynamic_slice_in_dim(ffn_rows[:, :rows], seq_pos, 1, 0)
    passed = lax.ppermute(passed, "phase", [(p, (p + 1) % count) for p in range(count)])
    hessians, ffn_diagonal = hessian(
        scale, width, place, left_a, attn_cols, gain_a, ffn_rows, gain_ffn, total, ffn_cols, gain_f
    )
    return (passed, hessians[None], ffn_diagonal)


def solution(mesh):
    phase, tensor, seq = (mesh.shape[a] for a in ("phase", "tensor", "seq"))
    lines = Mesh(
        mesh.devices.reshape(phase, tensor // 4, 2, 2, seq), ("phase", "x", "za", "zb", "seq")
    )
    tiled = P("phase", "seq", TENSOR)
    return jax.shard_map(
        on_device,
        mesh=lines,
        in_specs=(
            tiled,
            P("phase", "seq"),
            P("phase", TENSOR),
            P("phase", TENSOR),
            tiled,
            tiled,
            tiled,
        ),
        out_specs=(tiled, P("phase", TENSOR, "seq"), P("phase", GROUP)),
        check_vma=False,
    )
```

```python
import functools

import jax
import jax.numpy as jnp
from jax import lax
from jax.experimental import pallas as pl
from jax.experimental.pallas import tpu as pltpu
from jax.sharding import Mesh, PartitionSpec as P

HD = 128
norm_eps = 1e-05
rope_base = 500000.0
ZL = ("za", "zb")
TENSOR = ("x", "za", "zb")
GROUP = TENSOR + ("seq",)
f32 = jnp.float32
bf16 = jnp.bfloat16
LIMIT = 24 * 1024 * 1024
WIDE = 57 * 1024 * 1024
PROJECT = 55 * 1024 * 1024


def swap_x_seq(value):
    nx, nz, ns = lax.axis_size("x"), lax.axis_size(ZL), lax.axis_size("seq")
    pairs = [
        ((x * nz + z) * ns + s, (s * nz + z) * ns + x)
        for x in range(nx)
        for z in range(nz)
        for s in range(ns)
    ]
    return lax.ppermute(value, GROUP, pairs)


def project_kernel(cols, gain, wq, wk, wv, after, out, q_acc, kv_acc, squares):
    step = pl.program_id(0)
    blocks, rows, feats = cols.shape
    raw = cols[...].reshape(blocks * rows, feats).astype(f32)
    left = (raw * gain[...]).astype(bf16)
    part = jnp.sum(raw * raw, axis=1, keepdims=True)
    kv_w = jnp.concatenate([wk[...], wv[...]], 0)
    kv = lax.dot_general(left, kv_w, (((1,), (1,)), ((), ())), preferred_element_type=f32)
    q = jnp.dot(left, wq[...], preferred_element_type=f32)

    @pl.when(step == 0)
    def _():
        q_acc[...] = q
        kv_acc[...] = kv
        squares[...] = part

    @pl.when(step > 0)
    def _():
        q_acc[...] += q
        kv_acc[...] += kv
        squares[...] += part

    @pl.when(step == pl.num_programs(0) - 1)
    def _():
        heads = q_acc.shape[1] // HD
        for k in range(blocks):
            block = pl.ds(k * rows, rows)
            out[k, pl.ds(heads * rows, rows), :] = kv_acc[block, :].astype(bf16)
            sums = stacked(three_parts(row_of(squares[block, :])))
            out[k, pl.ds((heads + 1) * rows, 16), :] = sums
            for h in range(heads):
                out[k, pl.ds(h * rows, rows), :] = q_acc[block, pl.ds(h * HD, HD)].astype(bf16)


def project(cols, gain, w_query, w_key, w_value, after):
    blocks, parts, rows, feats = cols.shape
    q_width, kv_width = w_query.shape[2], 2 * w_key.shape[2]
    heads = q_width // HD
    kv_spec = pl.BlockSpec((None, w_key.shape[2], feats), lambda z: (0, 0, z))
    return pl.pallas_call(
        project_kernel,
        grid=(parts,),
        in_specs=[
            pl.BlockSpec((blocks, None, rows, feats), lambda z: (0, z, 0, 0)),
            pl.BlockSpec((None, 1, feats), lambda z: (z, 0, 0)),
            pl.BlockSpec((None, feats, q_width), lambda z: (0, z, 0)),
            kv_spec,
            kv_spec,
            pl.BlockSpec(memory_space=pl.ANY),
        ],
        out_specs=fixed((blocks, (heads + 1) * rows + 16, HD)),
        out_shape=pltpu.HBM((blocks, (heads + 1) * rows + 16, HD), bf16),
        scratch_shapes=[
            pltpu.VMEM((blocks * rows, q_width), f32),
            pltpu.VMEM((blocks * rows, kv_width), f32),
            pltpu.VMEM((blocks * rows, 1), f32),
        ],
        compiler_params=params(PROJECT),
        name="project",
    )(cols, gain, w_query, w_key.swapaxes(1, 2), w_value.swapaxes(1, 2), after)


def fixed(shape):
    return pl.BlockSpec(shape, lambda *at: (0,) * len(shape))


def params(limit=LIMIT):
    return pltpu.CompilerParams(vmem_limit_bytes=limit)


def three_parts(value):
    parts = []
    for _ in range(3):
        part = value.astype(bf16)
        parts.append(part)
        value = value - part.astype(f32)
    return parts


def row_of(column):
    n = column.shape[0]
    same = lax.broadcasted_iota(jnp.int32, (n, n), 0) == lax.broadcasted_iota(jnp.int32, (n, n), 1)
    return jnp.sum(jnp.where(same, column, f32(0.0)), axis=0, keepdims=True)


def stacked(parts, more=()):
    rows = list(parts) + list(more)
    rows.append(jnp.zeros((16 - len(rows), rows[0].shape[1]), f32))
    return jnp.concatenate([row.astype(f32) for row in rows]).astype(bf16)


def attn_copies_kernel(group, table, place, copies, gain_a, gain_f):
    rows = copies.shape[1]
    for k in range(copies.shape[0]):
        copies[k] = group[pl.ds(0, rows), :]
    gains = group[pl.ds(rows, 16), :].astype(f32)
    gain_a[...] = gains[0:1]
    gain_f[...] = gains[1:2]


def attn_copies(group, count, *after):
    parts, tall, feats = group.shape
    rows = tall - 16
    gain = pl.BlockSpec((None, 1, feats), lambda z: (z, 0, 0))
    gain_shape = pltpu.HBM((parts, 1, feats), f32)
    return pl.pallas_call(
        attn_copies_kernel,
        grid=(parts,),
        in_specs=[pl.BlockSpec((None, tall, feats), lambda z: (z, 0, 0))]
        + [pl.BlockSpec(memory_space=pl.ANY)] * len(after),
        out_specs=[
            pl.BlockSpec((count, None, rows, feats), lambda z: (0, z, 0, 0)),
            gain,
            gain,
        ],
        out_shape=[
            pltpu.HBM((count, parts, rows, feats), bf16),
            gain_shape,
            gain_shape,
        ],
        compiler_params=params(),
        name="attn_copies",
    )(group, *after)


def take_kernel(value, after, out):
    out[...] = value[...]


def take_after(value, after):
    return pl.pallas_call(
        take_kernel,
        grid=(1,),
        in_specs=[fixed(value.shape), pl.BlockSpec(memory_space=pl.ANY)],
        out_specs=fixed(value.shape),
        out_shape=pltpu.HBM(value.shape, value.dtype),
        compiler_params=params(WIDE),
        name="take_after",
    )(value, after)


def first_message_kernel(hidden, gain_a, gain_f, ids, out):
    rows, feats = hidden.shape
    out[pl.ds(0, rows), :] = hidden[...]
    docs = jnp.concatenate([ids[...].astype(f32)] * (feats // rows), 1)
    out[pl.ds(rows, 16), :] = stacked([gain_a[...], gain_f[...], docs])


def first_message(hidden, gain_a, gain_f, ids):
    shape = (hidden.shape[0] + 16, hidden.shape[1])
    arrays = (hidden, gain_a, gain_f, ids)
    return pl.pallas_call(
        first_message_kernel,
        grid=(1,),
        in_specs=[fixed(a.shape) for a in arrays],
        out_specs=fixed(shape),
        out_shape=pltpu.HBM(shape, bf16),
        compiler_params=params(WIDE),
        name="first_message",
    )(*arrays)


def total_of(parts):
    parts = parts.astype(f32)
    return parts[0:1] + parts[1:2] + parts[2:3]


def below(row, feats):
    return jnp.concatenate([stacked(three_parts(row))] * (feats // row.shape[1]), 1)


def ffn_copies_kernel(group, own, after, copies, message, sums):
    step = pl.program_id(0)
    rows, feats = own.shape
    for k in range(copies.shape[0]):
        copies[k] = group[pl.ds(0, rows), :]
    part = total_of(group[pl.ds(rows, 16), :])[:, :rows]

    @pl.when(step == 0)
    def _():
        message[pl.ds(0, rows), :] = own[...]
        sums[...] = part

    @pl.when(step > 0)
    def _():
        sums[...] += part

    @pl.when(step == pl.num_programs(0) - 1)
    def _():
        message[pl.ds(rows, 16), :] = below(sums[...], feats)


def ffn_copies(group, own, count, after):
    parts, tall, feats = group.shape
    rows = own.shape[0]
    return pl.pallas_call(
        ffn_copies_kernel,
        grid=(parts,),
        in_specs=[
            pl.BlockSpec((None, tall, feats), lambda z: (z, 0, 0)),
            fixed(own.shape),
            pl.BlockSpec(memory_space=pl.ANY),
        ],
        out_specs=[
            pl.BlockSpec((count, None, rows, feats), lambda z: (0, z, 0, 0)),
            fixed((tall, feats)),
        ],
        out_shape=[
            pltpu.HBM((count, parts, rows, feats), bf16),
            pltpu.HBM((tall, feats), bf16),
        ],
        scratch_shapes=[pltpu.VMEM((1, rows), f32)],
        compiler_params=params(),
        name="ffn_copies",
    )(group, own, after)


def kv_sum_kernel(width, arrived, docs, out):
    rows = out.shape[1] - 16
    kv = jnp.sum(arrived[:, pl.ds(0, rows), :].astype(f32), axis=0).astype(bf16)
    sums = jnp.sum(arrived[:, pl.ds(rows, 16), :].astype(f32), axis=0)
    r = lax.rsqrt((sums[0:1] + sums[1:2] + sums[2:3]) / width + norm_eps)
    tail = stacked(three_parts(r), [docs[...].astype(f32)[2:3, :rows]])
    for copy in range(out.shape[0]):
        out[copy, pl.ds(0, rows), :] = kv
        out[copy, pl.ds(rows, 16), :] = tail


def kv_sum(width, arrived, docs, copies):
    blocks, tall, lanes = arrived.shape
    rows = HD
    last = tall - rows - 16
    return pl.pallas_call(
        functools.partial(kv_sum_kernel, width),
        grid=(1,),
        in_specs=[
            pl.BlockSpec(
                (pl.Element(blocks), pl.Element(rows + 16), pl.Element(lanes)),
                lambda i: (0, last, 0),
            ),
            pl.BlockSpec((16, docs.shape[1]), lambda i: (rows // 16, 0)),
        ],
        out_specs=fixed((copies, rows + 16, lanes)),
        out_shape=pltpu.HBM((copies, rows + 16, lanes), bf16),
        compiler_params=params(),
        name="kv_sum",
    )(arrived, docs)


def rotate(values, table):
    lower = lax.broadcasted_iota(jnp.int32, table.shape, 1) < HD // 2
    swapped = pltpu.roll(table, HD // 2, 1)
    cosine = jnp.where(lower, table, swapped)
    sine = jnp.where(lower, -swapped, table)
    return values * cosine + pltpu.roll(values, HD // 2, 1) * sine


def column_of(row):
    n = row.shape[1]
    same = lax.broadcasted_iota(jnp.int32, (n, n), 0) == lax.broadcasted_iota(jnp.int32, (n, n), 1)
    return jnp.sum(jnp.where(same, row, f32(0.0)), axis=1, keepdims=True)


def halves(value):
    high = value.astype(bf16)
    return high, (value - high.astype(f32)).astype(bf16)


def attend_kernel(q_in, kv_in, table, resid, copies, out, keys, values, r_all, docs_all):
    rows, feats = out.shape
    heads = feats // HD
    tokens = keys.shape[0]
    x_pos = lax.axis_index("x")
    lower = lax.broadcasted_iota(jnp.int32, (rows, HD), 1) < HD // 2
    for k in range(tokens // rows):
        first = kv_in[2 * k, pl.ds(0, rows), :].astype(f32)
        second = kv_in[2 * k + 1, pl.ds(0, rows), :].astype(f32)
        tail = kv_in[2 * k, pl.ds(rows, 16), :].astype(f32)
        block = pl.ds(k * rows, rows)
        key = jnp.where(lower, first, pltpu.roll(second, HD // 2, 1))
        high, low = halves(rotate(key, table[block, :]))
        keys[block, :] = jnp.concatenate([high, high, low], 1)
        value = jnp.where(lower, pltpu.roll(first, HD // 2, 1), second).astype(bf16)
        values[block, :] = value
        values[pl.ds(tokens + k * rows, rows), :] = value
        r_all[:, block] = total_of(tail)
        docs_all[:, block] = tail[3:4]

    own = pl.ds(pl.multiple_of(x_pos * rows, rows), rows)
    r_own = column_of(r_all[:, own]) * (1.0 / HD**0.5)
    key_ids = lax.broadcasted_iota(jnp.int32, (rows, tokens), 1)
    own_ids = lax.broadcasted_iota(jnp.int32, (rows, tokens), 0) + x_pos * rows
    allowed = (key_ids <= own_ids) & (docs_all[...] == column_of(docs_all[:, own]))
    squares = jnp.zeros((rows, 1), f32)
    for h in range(heads):
        query = jnp.sum(q_in[:, pl.ds(h * rows, rows), :].astype(f32), axis=0)
        high, low = halves(rotate(query, table[own, :]) * r_own)
        scores = lax.dot_general(
            jnp.concatenate([high, low, high], 1), keys[...], (((1,), (1,)), ((), ())),
            preferred_element_type=f32,
        )
        scores = jnp.where(allowed, scores * r_all[...], f32(-1e30))
        peak = jnp.max(scores, axis=-1, keepdims=True)
        weights = jnp.where(allowed, jnp.exp(scores - peak), f32(0.0))
        total = jnp.sum(weights, axis=-1, keepdims=True)
        weights = jnp.concatenate(halves(weights * r_all[...]), 1)
        context = jnp.dot(weights, values[...], preferred_element_type=f32) / total
        lanes = pl.ds(h * HD, HD)
        result = (resid[:, lanes].astype(f32) + context).astype(bf16)
        out[:, lanes] = result
        for copy in range(copies.shape[0]):
            copies[copy, pl.ds(0, rows), lanes] = result
        result = result.astype(f32)
        squares += jnp.sum(result * result, axis=1, keepdims=True)
    tail = below(row_of(squares), feats)
    for copy in range(copies.shape[0]):
        copies[copy, pl.ds(rows, 16), :] = tail


def attend(q_in, kv_in, table, swapped, copies):
    rows, feats = swapped.shape[0] - 16, swapped.shape[1]
    heads, tokens = feats // HD, table.shape[0]
    shape = (copies, rows + 16, feats)
    return pl.pallas_call(
        attend_kernel,
        grid=(1,),
        in_specs=[
            fixed((q_in.shape[0], heads * rows, HD)),
            fixed(kv_in.shape),
            fixed(table.shape),
            fixed((rows, feats)),
        ],
        out_specs=[fixed(shape), fixed((rows, feats))],
        out_shape=[pltpu.HBM(shape, bf16), pltpu.HBM((rows, feats), bf16)],
        scratch_shapes=[
            pltpu.VMEM((tokens, 3 * HD), bf16),
            pltpu.VMEM((2 * tokens, HD), bf16),
            pltpu.VMEM((1, tokens), f32),
            pltpu.VMEM((1, tokens), f32),
        ],
        compiler_params=params(),
        name="attend",
    )(q_in, kv_in, table, swapped)


def attn_left_kernel(scale, own_rows, gain, kv, out):
    blocks, rows, feats = own_rows.shape
    for k in range(blocks):
        parts = kv[2 * k, pl.ds(rows, 16), :].astype(f32)
        r = parts[0:1] + parts[1:2] + parts[2:3]
        turned = (own_rows[k].astype(f32) * gain[...].astype(f32)).T
        out[:, pl.ds(k * rows, rows)] = (turned * (r * r * scale)).astype(bf16)


def attn_left(scale, own_rows, gain, kv_all):
    blocks, rows, feats = own_rows.shape
    arrays = (own_rows, gain, kv_all)
    return pl.pallas_call(
        functools.partial(attn_left_kernel, scale),
        grid=(1,),
        in_specs=[fixed(a.shape) for a in arrays],
        out_specs=fixed((feats, blocks * rows)),
        out_shape=jax.ShapeDtypeStruct((feats, blocks * rows), bf16),
        compiler_params=params(),
        name="attn_left",
    )(*arrays)


def hessian_kernel(
    scale, width, place, left_a, cols_a, gain_a, ffn_rows, gain_row, total, cols_f, gain_f,
    out, diagonal, left_f,
):
    blocks, rows, feats = cols_a.shape
    row, col = place[0], place[1] + pl.program_id(0)

    @pl.when(pl.program_id(0) == 0)
    def _():
        part = pl.ds(pl.multiple_of(lax.axis_index("seq") * rows, rows), rows)
        squares = jnp.zeros((1, rows), f32)
        for k in range(blocks):
            weight = column_of(scale / (total[k] / width + norm_eps))
            block = ffn_rows[k, pl.ds(0, rows), :].astype(f32) * gain_row[...].astype(f32)
            left_f[:, pl.ds(k * rows, rows)] = (block * weight).astype(bf16).T
            mine = ffn_rows[k, pl.ds(0, rows), part].astype(f32) * gain_row[:, part].astype(f32)
            squares += jnp.sum(mine * mine * weight, axis=0, keepdims=True)
        diagonal[...] = squares

    def product(left, cols, gain):
        right = cols[...].reshape(blocks * rows, feats)
        return (jnp.dot(left[...], right, preferred_element_type=f32) * gain[...]).astype(bf16)

    @pl.when(row < col)
    def _():
        out[...] = product(left_a, cols_a, gain_a)

    @pl.when(row > col)
    def _():
        out[...] = product(left_f, cols_f, gain_f)

    @pl.when(row == col)
    def _():
        upper = product(left_a, cols_a, gain_a)
        lower = product(left_f, cols_f, gain_f)
        row_ids = lax.broadcasted_iota(jnp.int32, lower.shape, 0)
        col_ids = lax.broadcasted_iota(jnp.int32, lower.shape, 1)
        out[...] = jnp.where(row_ids <= col_ids, upper, lower)


def hessian(
    scale, width, place, left_a, cols_a, gain_a, ffn_rows, gain_row, total, cols_f, gain_f
):
    blocks, parts, rows, feats = cols_a.shape
    tokens = blocks * rows

    def upper_at(z, at):
        return jnp.clip(jnp.maximum(z, at[0] - at[1]), 0, parts - 1)

    def lower_at(z, at):
        return jnp.clip(jnp.minimum(z, at[0] - at[1]), 0, parts - 1)

    gain = pl.BlockSpec((None, 1, feats), lambda z, at: (z, 0, 0))
    return pl.pallas_call(
        functools.partial(hessian_kernel, scale, width),
        grid_spec=pltpu.PrefetchScalarGridSpec(
            num_scalar_prefetch=1,
            grid=(parts,),
            in_specs=[
                fixed(left_a.shape),
                pl.BlockSpec((blocks, None, rows, feats), lambda z, at: (0, upper_at(z, at), 0, 0)),
                gain,
                fixed(ffn_rows.shape),
                fixed(gain_row.shape),
                fixed(total.shape),
                pl.BlockSpec((blocks, None, rows, feats), lambda z, at: (0, lower_at(z, at), 0, 0)),
                gain,
            ],
            out_specs=[
                pl.BlockSpec((feats, feats), lambda z, at: (0, z)),
                fixed((1, rows)),
            ],
            scratch_shapes=[pltpu.VMEM((feats, tokens), bf16)],
        ),
        out_shape=[
            jax.ShapeDtypeStruct((feats, parts * feats), bf16),
            jax.ShapeDtypeStruct((1, rows), f32),
        ],
        compiler_params=params(),
        name="hessian",
    )(place, left_a, cols_a, gain_a, ffn_rows, gain_row, total, cols_f, gain_f)


def on_device(hidden, segment_ids, gain_attn, gain_ffn, w_query, w_key, w_value):
    x_pos = lax.axis_index("x")
    zl_pos = lax.axis_index(ZL)
    seq_pos = lax.axis_index("seq")
    nx, nz, ns = lax.axis_size("x"), lax.axis_size(ZL), lax.axis_size("seq")
    rows, feats = hidden.shape[1:]
    tokens = rows * ns
    width = feats * nx * nz
    scale = 2.0 / tokens
    place = jnp.stack([x_pos * nz + zl_pos, seq_pos * nz])
    place = place.astype(jnp.int32)

    swapped = swap_x_seq(first_message(hidden[0], gain_attn, gain_ffn, segment_ids))
    half = HD // 2
    freq = rope_base ** (-(jnp.arange(half, dtype=f32) * 2.0 / HD))
    angle = jnp.arange(tokens, dtype=f32)[:, None] * freq[None, :]
    table = jnp.concatenate([jnp.cos(angle), jnp.sin(angle)], 1)
    group = lax.all_gather(swapped, ZL)
    copies, gain_a, gain_f = attn_copies(group, nx, table, place)
    attn_rows = lax.all_gather(take_after(hidden[0], gain_a), "seq")
    attn_cols = lax.all_to_all(copies, "x", 0, 0)

    message = project(attn_cols, gain_a, w_query, w_key, w_value, attn_rows)
    arrived = lax.all_to_all(lax.all_to_all(message, "x", 0, 0), "seq", 0, 0)
    kv = lax.all_to_all(kv_sum(width, arrived, swapped, 2 * nx), ("x", "zb"), 0, 0)
    copies, section_out = attend(arrived, kv, table, swapped, nz)
    left_a = attn_left(scale, attn_rows, gain_attn, kv)

    out_rows = swap_x_seq(section_out)
    group = lax.all_to_all(copies, ZL, 0, 0)
    copies, message = ffn_copies(group, out_rows, nx, left_a)
    ffn_cols = lax.all_to_all(copies, "x", 0, 0)
    ffn_rows = lax.all_gather(message, "seq")
    total = jnp.sum(ffn_rows[:, rows : rows + 3, :rows].astype(f32), axis=(0, 1))
    total = lax.all_gather(total[None], "x")
    count = lax.axis_size("phase")
    passed = lax.dynamic_slice_in_dim(ffn_rows[:, :rows], seq_pos, 1, 0)
    passed = lax.ppermute(passed, "phase", [(p, (p + 1) % count) for p in range(count)])
    hessians, ffn_diagonal = hessian(
        scale, width, place, left_a, attn_cols, gain_a, ffn_rows, gain_ffn, total, ffn_cols, gain_f
    )
    return (passed, hessians[None], ffn_diagonal)


def solution(mesh):
    phase, tensor, seq = (mesh.shape[a] for a in ("phase", "tensor", "seq"))
    lines = Mesh(
        mesh.devices.reshape(phase, tensor // 4, 2, 2, seq), ("phase", "x", "za", "zb", "seq")
    )
    tiled = P("phase", "seq", TENSOR)
    return jax.shard_map(
        on_device,
        mesh=lines,
        in_specs=(
            tiled,
            P("phase", "seq"),
            P("phase", TENSOR),
            P("phase", TENSOR),
            tiled,
            tiled,
            tiled,
        ),
        out_specs=(tiled, P("phase", TENSOR, "seq"), P("phase", GROUP)),
        check_vma=False,
    )
```

```python
import functools

import jax
import jax.numpy as jnp
from jax import lax
from jax.experimental import pallas as pl
from jax.experimental.pallas import tpu as pltpu
from jax.sharding import Mesh, PartitionSpec as P

HD = 128
norm_eps = 1e-05
rope_base = 500000.0
ZL = ("za", "zb")
TENSOR = ("x", "za", "zb")
GROUP = TENSOR + ("seq",)
f32 = jnp.float32
bf16 = jnp.bfloat16
LIMIT = 24 * 1024 * 1024
WIDE = 57 * 1024 * 1024
PROJECT = 57 * 1024 * 1024


def swap_x_seq(value):
    nx, nz, ns = lax.axis_size("x"), lax.axis_size(ZL), lax.axis_size("seq")
    pairs = [
        ((x * nz + z) * ns + s, (s * nz + z) * ns + x)
        for x in range(nx)
        for z in range(nz)
        for s in range(ns)
    ]
    return lax.ppermute(value, GROUP, pairs)


def project_kernel(cols, gain, wq, wk, wv, after, out, q_acc, kv_acc, squares, left):
    step = pl.program_id(0)
    blocks, parts, rows, feats = cols.shape
    part = jnp.zeros((blocks * rows, 1), f32)
    for z in range(parts):
        raw = cols[:, z].reshape(blocks * rows, feats).astype(f32)
        left[:, pl.ds(z * feats, feats)] = (raw * gain[z]).astype(bf16)
        part += jnp.sum(raw * raw, axis=1, keepdims=True)
    kv_w = jnp.concatenate([wk[...], wv[...]], 0)
    kv = lax.dot_general(left[...], kv_w, (((1,), (1,)), ((), ())), preferred_element_type=f32)
    q = jnp.dot(left[...], wq[...], preferred_element_type=f32)

    @pl.when(step == 0)
    def _():
        q_acc[...] = q
        kv_acc[...] = kv
        squares[...] = part

    @pl.when(step > 0)
    def _():
        q_acc[...] += q
        kv_acc[...] += kv
        squares[...] += part

    @pl.when(step == pl.num_programs(0) - 1)
    def _():
        heads = q_acc.shape[1] // HD
        for k in range(blocks):
            block = pl.ds(k * rows, rows)
            out[k, pl.ds(heads * rows, rows), :] = kv_acc[block, :].astype(bf16)
            sums = stacked(three_parts(row_of(squares[block, :])))
            out[k, pl.ds((heads + 1) * rows, 16), :] = sums
            for h in range(heads):
                out[k, pl.ds(h * rows, rows), :] = q_acc[block, pl.ds(h * HD, HD)].astype(bf16)


def project(cols, gain, w_query, w_key, w_value, after):
    blocks, parts, rows, feats = cols.shape
    q_width, kv_width = w_query.shape[2], 2 * w_key.shape[2]
    heads = q_width // HD
    pair = 2
    kv_spec = pl.BlockSpec((None, w_key.shape[2], pair * feats), lambda z: (0, 0, z))
    return pl.pallas_call(
        project_kernel,
        grid=(parts // pair,),
        in_specs=[
            pl.BlockSpec((blocks, pair, rows, feats), lambda z: (0, z, 0, 0)),
            pl.BlockSpec((pair, 1, feats), lambda z: (z, 0, 0)),
            pl.BlockSpec((None, pair * feats, q_width), lambda z: (0, z, 0)),
            kv_spec,
            kv_spec,
            pl.BlockSpec(memory_space=pl.ANY),
        ],
        out_specs=fixed((blocks, (heads + 1) * rows + 16, HD)),
        out_shape=pltpu.HBM((blocks, (heads + 1) * rows + 16, HD), bf16),
        scratch_shapes=[
            pltpu.VMEM((blocks * rows, q_width), f32),
            pltpu.VMEM((blocks * rows, kv_width), f32),
            pltpu.VMEM((blocks * rows, 1), f32),
            pltpu.VMEM((blocks * rows, pair * feats), bf16),
        ],
        compiler_params=params(PROJECT),
        name="project",
    )(cols, gain, w_query, w_key.swapaxes(1, 2), w_value.swapaxes(1, 2), after)


def fixed(shape):
    return pl.BlockSpec(shape, lambda *at: (0,) * len(shape))


def params(limit=LIMIT):
    return pltpu.CompilerParams(vmem_limit_bytes=limit)


def three_parts(value):
    parts = []
    for _ in range(3):
        part = value.astype(bf16)
        parts.append(part)
        value = value - part.astype(f32)
    return parts


def row_of(column):
    n = column.shape[0]
    same = lax.broadcasted_iota(jnp.int32, (n, n), 0) == lax.broadcasted_iota(jnp.int32, (n, n), 1)
    return jnp.sum(jnp.where(same, column, f32(0.0)), axis=0, keepdims=True)


def stacked(parts, more=()):
    rows = list(parts) + list(more)
    rows.append(jnp.zeros((16 - len(rows), rows[0].shape[1]), f32))
    return jnp.concatenate([row.astype(f32) for row in rows]).astype(bf16)


def attn_copies_kernel(group, table, place, copies, gain_a, gain_f):
    rows = copies.shape[1]
    for k in range(copies.shape[0]):
        copies[k] = group[pl.ds(0, rows), :]
    gains = group[pl.ds(rows, 16), :].astype(f32)
    gain_a[...] = gains[0:1]
    gain_f[...] = gains[1:2]


def attn_copies(group, count, *after):
    parts, tall, feats = group.shape
    rows = tall - 16
    gain = pl.BlockSpec((None, 1, feats), lambda z: (z, 0, 0))
    gain_shape = pltpu.HBM((parts, 1, feats), f32)
    return pl.pallas_call(
        attn_copies_kernel,
        grid=(parts,),
        in_specs=[pl.BlockSpec((None, tall, feats), lambda z: (z, 0, 0))]
        + [pl.BlockSpec(memory_space=pl.ANY)] * len(after),
        out_specs=[
            pl.BlockSpec((count, None, rows, feats), lambda z: (0, z, 0, 0)),
            gain,
            gain,
        ],
        out_shape=[
            pltpu.HBM((count, parts, rows, feats), bf16),
            gain_shape,
            gain_shape,
        ],
        compiler_params=params(),
        name="attn_copies",
    )(group, *after)


def take_kernel(value, after, out):
    out[...] = value[...]


def take_after(value, after):
    return pl.pallas_call(
        take_kernel,
        grid=(1,),
        in_specs=[fixed(value.shape), pl.BlockSpec(memory_space=pl.ANY)],
        out_specs=fixed(value.shape),
        out_shape=pltpu.HBM(value.shape, value.dtype),
        compiler_params=params(),
        name="take_after",
    )(value, after)


def first_message_kernel(hidden, gain_a, gain_f, ids, out):
    rows, feats = hidden.shape
    out[pl.ds(0, rows), :] = hidden[...]
    docs = jnp.concatenate([ids[...].astype(f32)] * (feats // rows), 1)
    out[pl.ds(rows, 16), :] = stacked([gain_a[...], gain_f[...], docs])


def first_message(hidden, gain_a, gain_f, ids):
    shape = (hidden.shape[0] + 16, hidden.shape[1])
    arrays = (hidden, gain_a, gain_f, ids)
    return pl.pallas_call(
        first_message_kernel,
        grid=(1,),
        in_specs=[fixed(a.shape) for a in arrays],
        out_specs=fixed(shape),
        out_shape=pltpu.HBM(shape, bf16),
        compiler_params=params(WIDE),
        name="first_message",
    )(*arrays)


def total_of(parts):
    parts = parts.astype(f32)
    return parts[0:1] + parts[1:2] + parts[2:3]


def below(row, feats):
    return jnp.concatenate([stacked(three_parts(row))] * (feats // row.shape[1]), 1)


def ffn_copies_kernel(group, own, after, copies, message, sums):
    step = pl.program_id(0)
    rows, feats = own.shape
    for k in range(copies.shape[0]):
        copies[k] = group[pl.ds(0, rows), :]
    part = total_of(group[pl.ds(rows, 16), :])[:, :rows]

    @pl.when(step == 0)
    def _():
        message[pl.ds(0, rows), :] = own[...]
        sums[...] = part

    @pl.when(step > 0)
    def _():
        sums[...] += part

    @pl.when(step == pl.num_programs(0) - 1)
    def _():
        message[pl.ds(rows, 16), :] = below(sums[...], feats)


def ffn_copies(group, own, count, after):
    parts, tall, feats = group.shape
    rows = own.shape[0]
    return pl.pallas_call(
        ffn_copies_kernel,
        grid=(parts,),
        in_specs=[
            pl.BlockSpec((None, tall, feats), lambda z: (z, 0, 0)),
            fixed(own.shape),
            pl.BlockSpec(memory_space=pl.ANY),
        ],
        out_specs=[
            pl.BlockSpec((count, None, rows, feats), lambda z: (0, z, 0, 0)),
            fixed((tall, feats)),
        ],
        out_shape=[
            pltpu.HBM((count, parts, rows, feats), bf16),
            pltpu.HBM((tall, feats), bf16),
        ],
        scratch_shapes=[pltpu.VMEM((1, rows), f32)],
        compiler_params=params(),
        name="ffn_copies",
    )(group, own, after)


def kv_sum_kernel(width, arrived, docs, out):
    rows = out.shape[1] - 16
    kv = jnp.sum(arrived[:, pl.ds(0, rows), :].astype(f32), axis=0).astype(bf16)
    sums = jnp.sum(arrived[:, pl.ds(rows, 16), :].astype(f32), axis=0)
    r = lax.rsqrt((sums[0:1] + sums[1:2] + sums[2:3]) / width + norm_eps)
    tail = stacked(three_parts(r), [docs[...].astype(f32)[2:3, :rows]])
    for copy in range(out.shape[0]):
        out[copy, pl.ds(0, rows), :] = kv
        out[copy, pl.ds(rows, 16), :] = tail


def kv_sum(width, arrived, docs, copies):
    blocks, tall, lanes = arrived.shape
    rows = HD
    last = tall - rows - 16
    return pl.pallas_call(
        functools.partial(kv_sum_kernel, width),
        grid=(1,),
        in_specs=[
            pl.BlockSpec(
                (pl.Element(blocks), pl.Element(rows + 16), pl.Element(lanes)),
                lambda i: (0, last, 0),
            ),
            pl.BlockSpec((16, docs.shape[1]), lambda i: (rows // 16, 0)),
        ],
        out_specs=fixed((copies, rows + 16, lanes)),
        out_shape=pltpu.HBM((copies, rows + 16, lanes), bf16),
        compiler_params=params(),
        name="kv_sum",
    )(arrived, docs)


def rotate(values, table):
    lower = lax.broadcasted_iota(jnp.int32, table.shape, 1) < HD // 2
    swapped = pltpu.roll(table, HD // 2, 1)
    cosine = jnp.where(lower, table, swapped)
    sine = jnp.where(lower, -swapped, table)
    return values * cosine + pltpu.roll(values, HD // 2, 1) * sine


def column_of(row):
    n = row.shape[1]
    same = lax.broadcasted_iota(jnp.int32, (n, n), 0) == lax.broadcasted_iota(jnp.int32, (n, n), 1)
    return jnp.sum(jnp.where(same, row, f32(0.0)), axis=1, keepdims=True)


def halves(value):
    high = value.astype(bf16)
    return high, (value - high.astype(f32)).astype(bf16)


def attend_kernel(q_in, kv_in, table, resid, copies, out, keys, values, r_all, docs_all):
    rows, feats = out.shape
    heads = feats // HD
    tokens = keys.shape[0]
    x_pos = lax.axis_index("x")
    lower = lax.broadcasted_iota(jnp.int32, (rows, HD), 1) < HD // 2
    for k in range(tokens // rows):
        first = kv_in[2 * k, pl.ds(0, rows), :].astype(f32)
        second = kv_in[2 * k + 1, pl.ds(0, rows), :].astype(f32)
        tail = kv_in[2 * k, pl.ds(rows, 16), :].astype(f32)
        block = pl.ds(k * rows, rows)
        key = jnp.where(lower, first, pltpu.roll(second, HD // 2, 1))
        high, low = halves(rotate(key, table[block, :]))
        keys[block, :] = jnp.concatenate([high, high, low], 1)
        value = jnp.where(lower, pltpu.roll(first, HD // 2, 1), second).astype(bf16)
        values[block, :] = value
        values[pl.ds(tokens + k * rows, rows), :] = value
        r_all[:, block] = total_of(tail)
        docs_all[:, block] = tail[3:4]

    own = pl.ds(pl.multiple_of(x_pos * rows, rows), rows)
    r_own = column_of(r_all[:, own]) * (1.0 / HD**0.5)
    key_ids = lax.broadcasted_iota(jnp.int32, (rows, tokens), 1)
    own_ids = lax.broadcasted_iota(jnp.int32, (rows, tokens), 0) + x_pos * rows
    allowed = (key_ids <= own_ids) & (docs_all[...] == column_of(docs_all[:, own]))
    squares = jnp.zeros((rows, 1), f32)
    for h in range(heads):
        query = jnp.sum(q_in[:, pl.ds(h * rows, rows), :].astype(f32), axis=0)
        high, low = halves(rotate(query, table[own, :]) * r_own)
        scores = lax.dot_general(
            jnp.concatenate([high, low, high], 1), keys[...], (((1,), (1,)), ((), ())),
            preferred_element_type=f32,
        )
        scores = jnp.where(allowed, scores * r_all[...], f32(-1e30))
        peak = jnp.max(scores, axis=-1, keepdims=True)
        weights = jnp.where(allowed, jnp.exp(scores - peak), f32(0.0))
        total = jnp.sum(weights, axis=-1, keepdims=True)
        weights = jnp.concatenate(halves(weights * r_all[...]), 1)
        context = jnp.dot(weights, values[...], preferred_element_type=f32) / total
        lanes = pl.ds(h * HD, HD)
        result = (resid[:, lanes].astype(f32) + context).astype(bf16)
        out[:, lanes] = result
        for copy in range(copies.shape[0]):
            copies[copy, pl.ds(0, rows), lanes] = result
        result = result.astype(f32)
        squares += jnp.sum(result * result, axis=1, keepdims=True)
    tail = below(row_of(squares), feats)
    for copy in range(copies.shape[0]):
        copies[copy, pl.ds(rows, 16), :] = tail


def attend(q_in, kv_in, table, swapped, copies):
    rows, feats = swapped.shape[0] - 16, swapped.shape[1]
    heads, tokens = feats // HD, table.shape[0]
    shape = (copies, rows + 16, feats)
    return pl.pallas_call(
        attend_kernel,
        grid=(1,),
        in_specs=[
            fixed((q_in.shape[0], heads * rows, HD)),
            fixed(kv_in.shape),
            fixed(table.shape),
            fixed((rows, feats)),
        ],
        out_specs=[fixed(shape), fixed((rows, feats))],
        out_shape=[pltpu.HBM(shape, bf16), pltpu.HBM((rows, feats), bf16)],
        scratch_shapes=[
            pltpu.VMEM((tokens, 3 * HD), bf16),
            pltpu.VMEM((2 * tokens, HD), bf16),
            pltpu.VMEM((1, tokens), f32),
            pltpu.VMEM((1, tokens), f32),
        ],
        compiler_params=params(),
        name="attend",
    )(q_in, kv_in, table, swapped)


def attn_left_kernel(scale, own_rows, gain, kv, out):
    blocks, rows, feats = own_rows.shape
    for k in range(blocks):
        parts = kv[2 * k, pl.ds(rows, 16), :].astype(f32)
        r = parts[0:1] + parts[1:2] + parts[2:3]
        turned = (own_rows[k].astype(f32) * gain[...].astype(f32)).T
        out[:, pl.ds(k * rows, rows)] = (turned * (r * r * scale)).astype(bf16)


def attn_left(scale, own_rows, gain, kv_all):
    blocks, rows, feats = own_rows.shape
    arrays = (own_rows, gain, kv_all)
    return pl.pallas_call(
        functools.partial(attn_left_kernel, scale),
        grid=(1,),
        in_specs=[fixed(a.shape) for a in arrays],
        out_specs=fixed((feats, blocks * rows)),
        out_shape=jax.ShapeDtypeStruct((feats, blocks * rows), bf16),
        compiler_params=params(),
        name="attn_left",
    )(*arrays)


def hessian_kernel(
    scale, width, place, left_a, cols_a, gain_a, ffn_rows, gain_row, total, cols_f, gain_f,
    passed, out, diagonal, passed_out, left_f,
):
    blocks, rows, feats = cols_a.shape
    row, col = place[0], place[1] + pl.program_id(0)

    @pl.when(pl.program_id(0) == 0)
    def _():
        part = pl.ds(pl.multiple_of(lax.axis_index("seq") * rows, rows), rows)
        squares = jnp.zeros((1, rows), f32)
        for k in range(blocks):
            weight = column_of(scale / (total[k] / width + norm_eps))
            block = ffn_rows[k, pl.ds(0, rows), :].astype(f32) * gain_row[...].astype(f32)
            left_f[:, pl.ds(k * rows, rows)] = (block * weight).astype(bf16).T
            mine = ffn_rows[k, pl.ds(0, rows), part].astype(f32) * gain_row[:, part].astype(f32)
            squares += jnp.sum(mine * mine * weight, axis=0, keepdims=True)
        diagonal[...] = squares
        passed_out[...] = passed[...]

    def product(left, cols, gain):
        right = cols[...].reshape(blocks * rows, feats)
        return (jnp.dot(left[...], right, preferred_element_type=f32) * gain[...]).astype(bf16)

    @pl.when(row < col)
    def _():
        out[...] = product(left_a, cols_a, gain_a)

    @pl.when(row > col)
    def _():
        out[...] = product(left_f, cols_f, gain_f)

    @pl.when(row == col)
    def _():
        upper = product(left_a, cols_a, gain_a)
        lower = product(left_f, cols_f, gain_f)
        row_ids = lax.broadcasted_iota(jnp.int32, lower.shape, 0)
        col_ids = lax.broadcasted_iota(jnp.int32, lower.shape, 1)
        out[...] = jnp.where(row_ids <= col_ids, upper, lower)


def hessian(
    scale, width, place, left_a, cols_a, gain_a, ffn_rows, gain_row, total, cols_f, gain_f, passed
):
    blocks, parts, rows, feats = cols_a.shape
    tokens = blocks * rows

    def upper_at(z, at):
        return jnp.clip(jnp.maximum(z, at[0] - at[1]), 0, parts - 1)

    def lower_at(z, at):
        return jnp.clip(jnp.minimum(z, at[0] - at[1]), 0, parts - 1)

    gain = pl.BlockSpec((None, 1, feats), lambda z, at: (z, 0, 0))
    return pl.pallas_call(
        functools.partial(hessian_kernel, scale, width),
        grid_spec=pltpu.PrefetchScalarGridSpec(
            num_scalar_prefetch=1,
            grid=(parts,),
            in_specs=[
                fixed(left_a.shape),
                pl.BlockSpec((blocks, None, rows, feats), lambda z, at: (0, upper_at(z, at), 0, 0)),
                gain,
                fixed(ffn_rows.shape),
                fixed(gain_row.shape),
                fixed(total.shape),
                pl.BlockSpec((blocks, None, rows, feats), lambda z, at: (0, lower_at(z, at), 0, 0)),
                gain,
                fixed(passed.shape),
            ],
            out_specs=[
                pl.BlockSpec((feats, feats), lambda z, at: (0, z)),
                fixed((1, rows)),
                fixed(passed.shape),
            ],
            scratch_shapes=[pltpu.VMEM((feats, tokens), bf16)],
        ),
        out_shape=[
            jax.ShapeDtypeStruct((feats, parts * feats), bf16),
            jax.ShapeDtypeStruct((1, rows), f32),
            jax.ShapeDtypeStruct(passed.shape, bf16),
        ],
        compiler_params=params(),
        name="hessian",
    )(place, left_a, cols_a, gain_a, ffn_rows, gain_row, total, cols_f, gain_f, passed)


def on_device(hidden, segment_ids, gain_attn, gain_ffn, w_query, w_key, w_value):
    x_pos = lax.axis_index("x")
    zl_pos = lax.axis_index(ZL)
    seq_pos = lax.axis_index("seq")
    nx, nz, ns = lax.axis_size("x"), lax.axis_size(ZL), lax.axis_size("seq")
    rows, feats = hidden.shape[1:]
    tokens = rows * ns
    width = feats * nx * nz
    scale = 2.0 / tokens
    place = jnp.stack([x_pos * nz + zl_pos, seq_pos * nz])
    place = place.astype(jnp.int32)

    swapped = swap_x_seq(first_message(hidden[0], gain_attn, gain_ffn, segment_ids))
    half = HD // 2
    freq = rope_base ** (-(jnp.arange(half, dtype=f32) * 2.0 / HD))
    angle = jnp.arange(tokens, dtype=f32)[:, None] * freq[None, :]
    table = jnp.concatenate([jnp.cos(angle), jnp.sin(angle)], 1)
    group = lax.all_gather(swapped, ZL)
    copies, gain_a, gain_f = attn_copies(group, nx, table, place)
    attn_rows = lax.all_gather(take_after(hidden[0], gain_a), "seq")
    attn_cols = lax.all_to_all(copies, "x", 0, 0)

    message = project(attn_cols, gain_a, w_query, w_key, w_value, attn_rows)
    arrived = lax.all_to_all(lax.all_to_all(message, "x", 0, 0), "seq", 0, 0)
    kv = lax.all_to_all(kv_sum(width, arrived, swapped, 2 * nx), ("x", "zb"), 0, 0)
    copies, section_out = attend(arrived, kv, table, swapped, nz)
    left_a = attn_left(scale, attn_rows, gain_attn, kv)

    out_rows = swap_x_seq(section_out)
    group = lax.all_to_all(copies, ZL, 0, 0)
    copies, message = ffn_copies(group, out_rows, nx, left_a)
    ffn_cols = lax.all_to_all(copies, "x", 0, 0)
    ffn_rows = lax.all_gather(message, "seq")
    total = jnp.sum(ffn_rows[:, rows : rows + 3, :rows].astype(f32), axis=(0, 1))
    total = lax.all_gather(total[None], "x")
    count = lax.axis_size("phase")
    passed = lax.dynamic_slice_in_dim(ffn_rows[:, :rows], seq_pos, 1, 0)
    passed = lax.ppermute(passed, "phase", [(p, (p + 1) % count) for p in range(count)])
    hessians, ffn_diagonal, passed = hessian(
        scale,
        width,
        place,
        left_a,
        attn_cols,
        gain_a,
        ffn_rows,
        gain_ffn,
        total,
        ffn_cols,
        gain_f,
        passed,
    )
    return (passed, hessians[None], ffn_diagonal)


def solution(mesh):
    phase, tensor, seq = (mesh.shape[a] for a in ("phase", "tensor", "seq"))
    lines = Mesh(
        mesh.devices.reshape(phase, tensor // 4, 2, 2, seq), ("phase", "x", "za", "zb", "seq")
    )
    tiled = P("phase", "seq", TENSOR)
    return jax.shard_map(
        on_device,
        mesh=lines,
        in_specs=(
            tiled,
            P("phase", "seq"),
            P("phase", TENSOR),
            P("phase", TENSOR),
            tiled,
            tiled,
            tiled,
        ),
        out_specs=(tiled, P("phase", TENSOR, "seq"), P("phase", GROUP)),
        check_vma=False,
    )
```

```python
import functools

import jax
import jax.numpy as jnp
from jax import lax
from jax.experimental import pallas as pl
from jax.experimental.pallas import tpu as pltpu
from jax.sharding import Mesh, PartitionSpec as P

HD = 128
norm_eps = 1e-05
rope_base = 500000.0
ZL = ("za", "zb")
TENSOR = ("x", "za", "zb")
GROUP = TENSOR + ("seq",)
f32 = jnp.float32
bf16 = jnp.bfloat16
LIMIT = 24 * 1024 * 1024
WIDE = 57 * 1024 * 1024
PROJECT = 57 * 1024 * 1024


def swap_x_seq(value):
    nx, nz, ns = lax.axis_size("x"), lax.axis_size(ZL), lax.axis_size("seq")
    pairs = [
        ((x * nz + z) * ns + s, (s * nz + z) * ns + x)
        for x in range(nx)
        for z in range(nz)
        for s in range(ns)
    ]
    return lax.ppermute(value, GROUP, pairs)


def project_kernel(cols, gain, wq, wk, wv, out, q_acc, kv_acc, squares, left):
    step = pl.program_id(0)
    blocks, parts, rows, feats = cols.shape
    part = jnp.zeros((blocks * rows, 1), f32)
    for z in range(parts):
        raw = cols[:, z].reshape(blocks * rows, feats).astype(f32)
        left[:, pl.ds(z * feats, feats)] = (raw * gain[z]).astype(bf16)
        part += jnp.sum(raw * raw, axis=1, keepdims=True)
    kv_w = jnp.concatenate([wk[...], wv[...]], 0)
    kv = lax.dot_general(left[...], kv_w, (((1,), (1,)), ((), ())), preferred_element_type=f32)
    q = jnp.dot(left[...], wq[...], preferred_element_type=f32)

    @pl.when(step == 0)
    def _():
        q_acc[...] = q
        kv_acc[...] = kv
        squares[...] = part

    @pl.when(step > 0)
    def _():
        q_acc[...] += q
        kv_acc[...] += kv
        squares[...] += part

    @pl.when(step == pl.num_programs(0) - 1)
    def _():
        heads = q_acc.shape[1] // HD
        for k in range(blocks):
            block = pl.ds(k * rows, rows)
            out[k, pl.ds(heads * rows, rows), :] = kv_acc[block, :].astype(bf16)
            sums = stacked(three_parts(row_of(squares[block, :])))
            out[k, pl.ds((heads + 1) * rows, 16), :] = sums
            for h in range(heads):
                out[k, pl.ds(h * rows, rows), :] = q_acc[block, pl.ds(h * HD, HD)].astype(bf16)


def project(cols, gain, w_query, w_key, w_value):
    blocks, parts, rows, feats = cols.shape
    q_width, kv_width = w_query.shape[2], 2 * w_key.shape[2]
    heads = q_width // HD
    pair = 2
    kv_spec = pl.BlockSpec((None, w_key.shape[2], pair * feats), lambda z: (0, 0, z))
    return pl.pallas_call(
        project_kernel,
        grid=(parts // pair,),
        in_specs=[
            pl.BlockSpec((blocks, pair, rows, feats), lambda z: (0, z, 0, 0)),
            pl.BlockSpec((pair, 1, feats), lambda z: (z, 0, 0)),
            pl.BlockSpec((None, pair * feats, q_width), lambda z: (0, z, 0)),
            kv_spec,
            kv_spec,
        ],
        out_specs=fixed((blocks, (heads + 1) * rows + 16, HD)),
        out_shape=pltpu.HBM((blocks, (heads + 1) * rows + 16, HD), bf16),
        scratch_shapes=[
            pltpu.VMEM((blocks * rows, q_width), f32),
            pltpu.VMEM((blocks * rows, kv_width), f32),
            pltpu.VMEM((blocks * rows, 1), f32),
            pltpu.VMEM((blocks * rows, pair * feats), bf16),
        ],
        compiler_params=params(PROJECT),
        name="project",
    )(cols, gain, w_query, w_key.swapaxes(1, 2), w_value.swapaxes(1, 2))


def fixed(shape):
    return pl.BlockSpec(shape, lambda *at: (0,) * len(shape))


def params(limit=LIMIT):
    return pltpu.CompilerParams(vmem_limit_bytes=limit)


def three_parts(value):
    parts = []
    for _ in range(3):
        part = value.astype(bf16)
        parts.append(part)
        value = value - part.astype(f32)
    return parts


def row_of(column):
    n = column.shape[0]
    same = lax.broadcasted_iota(jnp.int32, (n, n), 0) == lax.broadcasted_iota(jnp.int32, (n, n), 1)
    return jnp.sum(jnp.where(same, column, f32(0.0)), axis=0, keepdims=True)


def stacked(parts, more=()):
    rows = list(parts) + list(more)
    rows.append(jnp.zeros((16 - len(rows), rows[0].shape[1]), f32))
    return jnp.concatenate([row.astype(f32) for row in rows]).astype(bf16)


def attn_copies_kernel(group, own_rows, copies, gain_a, gain_f):
    rows = copies.shape[1]
    for k in range(copies.shape[0]):
        copies[k] = group[pl.ds(0, rows), :]
    gains = group[pl.ds(rows, 16), :].astype(f32)
    gain_a[...] = gains[0:1]
    gain_f[...] = gains[1:2]


def attn_copies(group, count, *after):
    parts, tall, feats = group.shape
    rows = tall - 16
    gain = pl.BlockSpec((None, 1, feats), lambda z: (z, 0, 0))
    gain_shape = pltpu.HBM((parts, 1, feats), f32)
    return pl.pallas_call(
        attn_copies_kernel,
        grid=(parts,),
        in_specs=[pl.BlockSpec((None, tall, feats), lambda z: (z, 0, 0))]
        + [pl.BlockSpec(memory_space=pl.ANY)] * len(after),
        out_specs=[
            pl.BlockSpec((count, None, rows, feats), lambda z: (0, z, 0, 0)),
            gain,
            gain,
        ],
        out_shape=[
            pltpu.HBM((count, parts, rows, feats), bf16),
            gain_shape,
            gain_shape,
        ],
        compiler_params=params(),
        name="attn_copies",
    )(group, *after)


def first_message_kernel(hidden, gain_a, gain_f, ids, out):
    rows, feats = hidden.shape
    out[pl.ds(0, rows), :] = hidden[...]
    docs = jnp.concatenate([ids[...].astype(f32)] * (feats // rows), 1)
    out[pl.ds(rows, 16), :] = stacked([gain_a[...], gain_f[...], docs])


def first_message(hidden, gain_a, gain_f, ids):
    shape = (hidden.shape[0] + 16, hidden.shape[1])
    arrays = (hidden, gain_a, gain_f, ids)
    return pl.pallas_call(
        first_message_kernel,
        grid=(1,),
        in_specs=[fixed(a.shape) for a in arrays],
        out_specs=fixed(shape),
        out_shape=pltpu.HBM(shape, bf16),
        compiler_params=params(WIDE),
        name="first_message",
    )(*arrays)


def total_of(parts):
    parts = parts.astype(f32)
    return parts[0:1] + parts[1:2] + parts[2:3]


def below(row, feats):
    return jnp.concatenate([stacked(three_parts(row))] * (feats // row.shape[1]), 1)


def ffn_copies_kernel(group, own, after, copies, message, sums):
    step = pl.program_id(0)
    rows, feats = own.shape
    for k in range(copies.shape[0]):
        copies[k] = group[pl.ds(0, rows), :]
    part = total_of(group[pl.ds(rows, 16), :])[:, :rows]

    @pl.when(step == 0)
    def _():
        message[pl.ds(0, rows), :] = own[...]
        sums[...] = part

    @pl.when(step > 0)
    def _():
        sums[...] += part

    @pl.when(step == pl.num_programs(0) - 1)
    def _():
        message[pl.ds(rows, 16), :] = below(sums[...], feats)


def ffn_copies(group, own, count, after):
    parts, tall, feats = group.shape
    rows = own.shape[0]
    return pl.pallas_call(
        ffn_copies_kernel,
        grid=(parts,),
        in_specs=[
            pl.BlockSpec((None, tall, feats), lambda z: (z, 0, 0)),
            fixed(own.shape),
            pl.BlockSpec(memory_space=pl.ANY),
        ],
        out_specs=[
            pl.BlockSpec((count, None, rows, feats), lambda z: (0, z, 0, 0)),
            fixed((tall, feats)),
        ],
        out_shape=[
            pltpu.HBM((count, parts, rows, feats), bf16),
            pltpu.HBM((tall, feats), bf16),
        ],
        scratch_shapes=[pltpu.VMEM((1, rows), f32)],
        compiler_params=params(),
        name="ffn_copies",
    )(group, own, after)


def kv_sum_kernel(width, arrived, docs, table, place, out):
    rows = out.shape[1] - 16
    kv = jnp.sum(arrived[:, pl.ds(0, rows), :].astype(f32), axis=0).astype(bf16)
    sums = jnp.sum(arrived[:, pl.ds(rows, 16), :].astype(f32), axis=0)
    r = lax.rsqrt((sums[0:1] + sums[1:2] + sums[2:3]) / width + norm_eps)
    tail = stacked(three_parts(r), [docs[...].astype(f32)[2:3, :rows]])
    for copy in range(out.shape[0]):
        out[copy, pl.ds(0, rows), :] = kv
        out[copy, pl.ds(rows, 16), :] = tail


def kv_sum(width, arrived, docs, copies, *after):
    blocks, tall, lanes = arrived.shape
    rows = HD
    last = tall - rows - 16
    return pl.pallas_call(
        functools.partial(kv_sum_kernel, width),
        grid=(1,),
        in_specs=[
            pl.BlockSpec(
                (pl.Element(blocks), pl.Element(rows + 16), pl.Element(lanes)),
                lambda i: (0, last, 0),
            ),
            pl.BlockSpec((16, docs.shape[1]), lambda i: (rows // 16, 0)),
        ]
        + [pl.BlockSpec(memory_space=pl.ANY)] * len(after),
        out_specs=fixed((copies, rows + 16, lanes)),
        out_shape=pltpu.HBM((copies, rows + 16, lanes), bf16),
        compiler_params=params(),
        name="kv_sum",
    )(arrived, docs, *after)


def rotate(values, table):
    lower = lax.broadcasted_iota(jnp.int32, table.shape, 1) < HD // 2
    swapped = pltpu.roll(table, HD // 2, 1)
    cosine = jnp.where(lower, table, swapped)
    sine = jnp.where(lower, -swapped, table)
    return values * cosine + pltpu.roll(values, HD // 2, 1) * sine


def column_of(row):
    n = row.shape[1]
    same = lax.broadcasted_iota(jnp.int32, (n, n), 0) == lax.broadcasted_iota(jnp.int32, (n, n), 1)
    return jnp.sum(jnp.where(same, row, f32(0.0)), axis=1, keepdims=True)


def halves(value):
    high = value.astype(bf16)
    return high, (value - high.astype(f32)).astype(bf16)


def attend_kernel(q_in, kv_in, table, resid, copies, out, keys, values, r_all, docs_all):
    rows, feats = out.shape
    heads = feats // HD
    tokens = keys.shape[0]
    x_pos = lax.axis_index("x")
    lower = lax.broadcasted_iota(jnp.int32, (rows, HD), 1) < HD // 2
    for k in range(tokens // rows):
        first = kv_in[2 * k, pl.ds(0, rows), :].astype(f32)
        second = kv_in[2 * k + 1, pl.ds(0, rows), :].astype(f32)
        tail = kv_in[2 * k, pl.ds(rows, 16), :].astype(f32)
        block = pl.ds(k * rows, rows)
        key = jnp.where(lower, first, pltpu.roll(second, HD // 2, 1))
        high, low = halves(rotate(key, table[block, :]))
        keys[block, :] = jnp.concatenate([high, high, low], 1)
        value = jnp.where(lower, pltpu.roll(first, HD // 2, 1), second).astype(bf16)
        values[block, :] = value
        values[pl.ds(tokens + k * rows, rows), :] = value
        r_all[:, block] = total_of(tail)
        docs_all[:, block] = tail[3:4]

    own = pl.ds(pl.multiple_of(x_pos * rows, rows), rows)
    r_own = column_of(r_all[:, own]) * (1.0 / HD**0.5)
    key_ids = lax.broadcasted_iota(jnp.int32, (rows, tokens), 1)
    own_ids = lax.broadcasted_iota(jnp.int32, (rows, tokens), 0) + x_pos * rows
    allowed = (key_ids <= own_ids) & (docs_all[...] == column_of(docs_all[:, own]))
    squares = jnp.zeros((rows, 1), f32)
    for h in range(heads):
        query = jnp.sum(q_in[:, pl.ds(h * rows, rows), :].astype(f32), axis=0)
        high, low = halves(rotate(query, table[own, :]) * r_own)
        scores = lax.dot_general(
            jnp.concatenate([high, low, high], 1), keys[...], (((1,), (1,)), ((), ())),
            preferred_element_type=f32,
        )
        scores = jnp.where(allowed, scores * r_all[...], f32(-1e30))
        peak = jnp.max(scores, axis=-1, keepdims=True)
        weights = jnp.where(allowed, jnp.exp(scores - peak), f32(0.0))
        total = jnp.sum(weights, axis=-1, keepdims=True)
        weights = jnp.concatenate(halves(weights * r_all[...]), 1)
        context = jnp.dot(weights, values[...], preferred_element_type=f32) / total
        lanes = pl.ds(h * HD, HD)
        result = (resid[:, lanes].astype(f32) + context).astype(bf16)
        out[:, lanes] = result
        for copy in range(copies.shape[0]):
            copies[copy, pl.ds(0, rows), lanes] = result
        result = result.astype(f32)
        squares += jnp.sum(result * result, axis=1, keepdims=True)
    tail = below(row_of(squares), feats)
    for copy in range(copies.shape[0]):
        copies[copy, pl.ds(rows, 16), :] = tail


def attend(q_in, kv_in, table, swapped, copies):
    rows, feats = swapped.shape[0] - 16, swapped.shape[1]
    heads, tokens = feats // HD, table.shape[0]
    shape = (copies, rows + 16, feats)
    return pl.pallas_call(
        attend_kernel,
        grid=(1,),
        in_specs=[
            fixed((q_in.shape[0], heads * rows, HD)),
            fixed(kv_in.shape),
            fixed(table.shape),
            fixed((rows, feats)),
        ],
        out_specs=[fixed(shape), fixed((rows, feats))],
        out_shape=[pltpu.HBM(shape, bf16), pltpu.HBM((rows, feats), bf16)],
        scratch_shapes=[
            pltpu.VMEM((tokens, 3 * HD), bf16),
            pltpu.VMEM((2 * tokens, HD), bf16),
            pltpu.VMEM((1, tokens), f32),
            pltpu.VMEM((1, tokens), f32),
        ],
        compiler_params=params(),
        name="attend",
    )(q_in, kv_in, table, swapped)


def attn_left_kernel(scale, own_rows, gain, kv, out):
    blocks, rows, feats = own_rows.shape
    for k in range(blocks):
        parts = kv[2 * k, pl.ds(rows, 16), :].astype(f32)
        r = parts[0:1] + parts[1:2] + parts[2:3]
        turned = (own_rows[k].astype(f32) * gain[...].astype(f32)).T
        out[:, pl.ds(k * rows, rows)] = (turned * (r * r * scale)).astype(bf16)


def attn_left(scale, own_rows, gain, kv_all):
    blocks, rows, feats = own_rows.shape
    arrays = (own_rows, gain, kv_all)
    return pl.pallas_call(
        functools.partial(attn_left_kernel, scale),
        grid=(1,),
        in_specs=[fixed(a.shape) for a in arrays],
        out_specs=fixed((feats, blocks * rows)),
        out_shape=jax.ShapeDtypeStruct((feats, blocks * rows), bf16),
        compiler_params=params(),
        name="attn_left",
    )(*arrays)


def hessian_kernel(
    scale, width, place, left_a, cols_a, gain_a, ffn_rows, gain_row, total, cols_f, gain_f,
    passed, out, diagonal, passed_out, left_f,
):
    blocks, rows, feats = cols_a.shape
    row, col = place[0], place[1] + pl.program_id(0)

    @pl.when(pl.program_id(0) == 0)
    def _():
        part = pl.ds(pl.multiple_of(lax.axis_index("seq") * rows, rows), rows)
        squares = jnp.zeros((1, rows), f32)
        for k in range(blocks):
            weight = column_of(scale / (total[k] / width + norm_eps))
            block = ffn_rows[k, pl.ds(0, rows), :].astype(f32) * gain_row[...].astype(f32)
            left_f[:, pl.ds(k * rows, rows)] = (block * weight).astype(bf16).T
            mine = ffn_rows[k, pl.ds(0, rows), part].astype(f32) * gain_row[:, part].astype(f32)
            squares += jnp.sum(mine * mine * weight, axis=0, keepdims=True)
        diagonal[...] = squares
        passed_out[...] = passed[...]

    def product(left, cols, gain):
        right = cols[...].reshape(blocks * rows, feats)
        return (jnp.dot(left[...], right, preferred_element_type=f32) * gain[...]).astype(bf16)

    @pl.when(row < col)
    def _():
        out[...] = product(left_a, cols_a, gain_a)

    @pl.when(row > col)
    def _():
        out[...] = product(left_f, cols_f, gain_f)

    @pl.when(row == col)
    def _():
        upper = product(left_a, cols_a, gain_a)
        lower = product(left_f, cols_f, gain_f)
        row_ids = lax.broadcasted_iota(jnp.int32, lower.shape, 0)
        col_ids = lax.broadcasted_iota(jnp.int32, lower.shape, 1)
        out[...] = jnp.where(row_ids <= col_ids, upper, lower)


def hessian(
    scale, width, place, left_a, cols_a, gain_a, ffn_rows, gain_row, total, cols_f, gain_f, passed
):
    blocks, parts, rows, feats = cols_a.shape
    tokens = blocks * rows

    def upper_at(z, at):
        return jnp.clip(jnp.maximum(z, at[0] - at[1]), 0, parts - 1)

    def lower_at(z, at):
        return jnp.clip(jnp.minimum(z, at[0] - at[1]), 0, parts - 1)

    gain = pl.BlockSpec((None, 1, feats), lambda z, at: (z, 0, 0))
    return pl.pallas_call(
        functools.partial(hessian_kernel, scale, width),
        grid_spec=pltpu.PrefetchScalarGridSpec(
            num_scalar_prefetch=1,
            grid=(parts,),
            in_specs=[
                fixed(left_a.shape),
                pl.BlockSpec((blocks, None, rows, feats), lambda z, at: (0, upper_at(z, at), 0, 0)),
                gain,
                fixed(ffn_rows.shape),
                fixed(gain_row.shape),
                fixed(total.shape),
                pl.BlockSpec((blocks, None, rows, feats), lambda z, at: (0, lower_at(z, at), 0, 0)),
                gain,
                fixed(passed.shape),
            ],
            out_specs=[
                pl.BlockSpec((feats, feats), lambda z, at: (0, z)),
                fixed((1, rows)),
                fixed(passed.shape),
            ],
            scratch_shapes=[pltpu.VMEM((feats, tokens), bf16)],
        ),
        out_shape=[
            jax.ShapeDtypeStruct((feats, parts * feats), bf16),
            jax.ShapeDtypeStruct((1, rows), f32),
            jax.ShapeDtypeStruct(passed.shape, bf16),
        ],
        compiler_params=params(),
        name="hessian",
    )(place, left_a, cols_a, gain_a, ffn_rows, gain_row, total, cols_f, gain_f, passed)


def on_device(hidden, segment_ids, gain_attn, gain_ffn, w_query, w_key, w_value):
    x_pos = lax.axis_index("x")
    zl_pos = lax.axis_index(ZL)
    seq_pos = lax.axis_index("seq")
    nx, nz, ns = lax.axis_size("x"), lax.axis_size(ZL), lax.axis_size("seq")
    rows, feats = hidden.shape[1:]
    tokens = rows * ns
    width = feats * nx * nz
    scale = 2.0 / tokens
    place = jnp.stack([x_pos * nz + zl_pos, seq_pos * nz])
    place = place.astype(jnp.int32)

    swapped = swap_x_seq(first_message(hidden[0], gain_attn, gain_ffn, segment_ids))
    half = HD // 2
    freq = rope_base ** (-(jnp.arange(half, dtype=f32) * 2.0 / HD))
    angle = jnp.arange(tokens, dtype=f32)[:, None] * freq[None, :]
    table = jnp.concatenate([jnp.cos(angle), jnp.sin(angle)], 1)
    group = lax.all_gather(swapped, ZL)
    attn_rows = lax.all_gather(hidden[0], "seq")
    copies, gain_a, gain_f = attn_copies(group, nx, attn_rows)
    attn_cols = lax.all_to_all(copies, "x", 0, 0)

    message = project(attn_cols, gain_a, w_query, w_key, w_value)
    arrived = lax.all_to_all(lax.all_to_all(message, "x", 0, 0), "seq", 0, 0)
    kv = lax.all_to_all(kv_sum(width, arrived, swapped, 2 * nx, table, place), ("x", "zb"), 0, 0)
    copies, section_out = attend(arrived, kv, table, swapped, nz)
    left_a = attn_left(scale, attn_rows, gain_attn, kv)

    out_rows = swap_x_seq(section_out)
    group = lax.all_to_all(copies, ZL, 0, 0)
    copies, message = ffn_copies(group, out_rows, nx, left_a)
    ffn_cols = lax.all_to_all(copies, "x", 0, 0)
    ffn_rows = lax.all_gather(message, "seq")
    total = jnp.sum(ffn_rows[:, rows : rows + 3, :rows].astype(f32), axis=(0, 1))
    total = lax.all_gather(total[None], "x")
    count = lax.axis_size("phase")
    passed = lax.dynamic_slice_in_dim(ffn_rows[:, :rows], seq_pos, 1, 0)
    passed = lax.ppermute(passed, "phase", [(p, (p + 1) % count) for p in range(count)])
    hessians, ffn_diagonal, passed = hessian(
        scale,
        width,
        place,
        left_a,
        attn_cols,
        gain_a,
        ffn_rows,
        gain_ffn,
        total,
        ffn_cols,
        gain_f,
        passed,
    )
    return (passed, hessians[None], ffn_diagonal)


def solution(mesh):
    phase, tensor, seq = (mesh.shape[a] for a in ("phase", "tensor", "seq"))
    lines = Mesh(
        mesh.devices.reshape(phase, tensor // 4, 2, 2, seq), ("phase", "x", "za", "zb", "seq")
    )
    tiled = P("phase", "seq", TENSOR)
    return jax.shard_map(
        on_device,
        mesh=lines,
        in_specs=(
            tiled,
            P("phase", "seq"),
            P("phase", TENSOR),
            P("phase", TENSOR),
            tiled,
            tiled,
            tiled,
        ),
        out_specs=(tiled, P("phase", TENSOR, "seq"), P("phase", GROUP)),
        check_vma=False,
    )
```

```python
import functools

import jax
import jax.numpy as jnp
from jax import lax
from jax.experimental import pallas as pl
from jax.experimental.pallas import tpu as pltpu
from jax.sharding import Mesh, PartitionSpec as P

HD = 128
norm_eps = 1e-05
rope_base = 500000.0
ZL = ("za", "zb")
TENSOR = ("x", "za", "zb")
GROUP = TENSOR + ("seq",)
f32 = jnp.float32
bf16 = jnp.bfloat16
LIMIT = 24 * 1024 * 1024
WIDE = 57 * 1024 * 1024
PROJECT = 57 * 1024 * 1024


def swap_x_seq(value):
    nx, nz, ns = lax.axis_size("x"), lax.axis_size(ZL), lax.axis_size("seq")
    pairs = [
        ((x * nz + z) * ns + s, (s * nz + z) * ns + x)
        for x in range(nx)
        for z in range(nz)
        for s in range(ns)
    ]
    return lax.ppermute(value, GROUP, pairs)


def project_kernel(cols, gain, wq, wk, wv, after, out, q_acc, kv_acc, squares, left):
    step = pl.program_id(0)
    blocks, parts, rows, feats = cols.shape
    part = jnp.zeros((blocks * rows, 1), f32)
    for z in range(parts):
        raw = cols[:, z].reshape(blocks * rows, feats).astype(f32)
        left[:, pl.ds(z * feats, feats)] = (raw * gain[z]).astype(bf16)
        part += jnp.sum(raw * raw, axis=1, keepdims=True)
    kv_w = jnp.concatenate([wk[...], wv[...]], 0)
    kv = lax.dot_general(left[...], kv_w, (((1,), (1,)), ((), ())), preferred_element_type=f32)
    q = jnp.dot(left[...], wq[...], preferred_element_type=f32)

    @pl.when(step == 0)
    def _():
        q_acc[...] = q
        kv_acc[...] = kv
        squares[...] = part

    @pl.when(step > 0)
    def _():
        q_acc[...] += q
        kv_acc[...] += kv
        squares[...] += part

    @pl.when(step == pl.num_programs(0) - 1)
    def _():
        heads = q_acc.shape[1] // HD
        for k in range(blocks):
            block = pl.ds(k * rows, rows)
            out[k, pl.ds(heads * rows, rows), :] = kv_acc[block, :].astype(bf16)
            sums = stacked(three_parts(row_of(squares[block, :])))
            out[k, pl.ds((heads + 1) * rows, 16), :] = sums
            for h in range(heads):
                out[k, pl.ds(h * rows, rows), :] = q_acc[block, pl.ds(h * HD, HD)].astype(bf16)


def project(cols, gain, w_query, w_key, w_value, after):
    blocks, parts, rows, feats = cols.shape
    q_width, kv_width = w_query.shape[2], 2 * w_key.shape[2]
    heads = q_width // HD
    pair = 2
    kv_spec = pl.BlockSpec((None, w_key.shape[2], pair * feats), lambda z: (0, 0, z))
    return pl.pallas_call(
        project_kernel,
        grid=(parts // pair,),
        in_specs=[
            pl.BlockSpec((blocks, pair, rows, feats), lambda z: (0, z, 0, 0)),
            pl.BlockSpec((pair, 1, feats), lambda z: (z, 0, 0)),
            pl.BlockSpec((None, pair * feats, q_width), lambda z: (0, z, 0)),
            kv_spec,
            kv_spec,
            pl.BlockSpec(memory_space=pl.ANY),
        ],
        out_specs=fixed((blocks, (heads + 1) * rows + 16, HD)),
        out_shape=pltpu.HBM((blocks, (heads + 1) * rows + 16, HD), bf16),
        scratch_shapes=[
            pltpu.VMEM((blocks * rows, q_width), f32),
            pltpu.VMEM((blocks * rows, kv_width), f32),
            pltpu.VMEM((blocks * rows, 1), f32),
            pltpu.VMEM((blocks * rows, pair * feats), bf16),
        ],
        compiler_params=params(PROJECT),
        name="project",
    )(cols, gain, w_query, w_key.swapaxes(1, 2), w_value.swapaxes(1, 2), after)


def fixed(shape):
    return pl.BlockSpec(shape, lambda *at: (0,) * len(shape))


def params(limit=LIMIT):
    return pltpu.CompilerParams(vmem_limit_bytes=limit)


def three_parts(value):
    parts = []
    for _ in range(3):
        part = value.astype(bf16)
        parts.append(part)
        value = value - part.astype(f32)
    return parts


def row_of(column):
    n = column.shape[0]
    same = lax.broadcasted_iota(jnp.int32, (n, n), 0) == lax.broadcasted_iota(jnp.int32, (n, n), 1)
    return jnp.sum(jnp.where(same, column, f32(0.0)), axis=0, keepdims=True)


def stacked(parts, more=()):
    rows = list(parts) + list(more)
    rows.append(jnp.zeros((16 - len(rows), rows[0].shape[1]), f32))
    return jnp.concatenate([row.astype(f32) for row in rows]).astype(bf16)


def attn_copies_kernel(group, copies, gain_a, gain_f):
    rows = copies.shape[1]
    for k in range(copies.shape[0]):
        copies[k] = group[pl.ds(0, rows), :]
    gains = group[pl.ds(rows, 16), :].astype(f32)
    gain_a[...] = gains[0:1]
    gain_f[...] = gains[1:2]


def attn_copies(group, count):
    parts, tall, feats = group.shape
    rows = tall - 16
    gain = pl.BlockSpec((None, 1, feats), lambda z: (z, 0, 0))
    gain_shape = pltpu.HBM((parts, 1, feats), f32)
    return pl.pallas_call(
        attn_copies_kernel,
        grid=(parts,),
        in_specs=[pl.BlockSpec((None, tall, feats), lambda z: (z, 0, 0))],
        out_specs=[
            pl.BlockSpec((count, None, rows, feats), lambda z: (0, z, 0, 0)),
            gain,
            gain,
        ],
        out_shape=[
            pltpu.HBM((count, parts, rows, feats), bf16),
            gain_shape,
            gain_shape,
        ],
        compiler_params=params(),
        name="attn_copies",
    )(group)


def first_message_kernel(hidden, gain_a, gain_f, ids, out):
    rows, feats = hidden.shape
    out[pl.ds(0, rows), :] = hidden[...]
    docs = jnp.concatenate([ids[...].astype(f32)] * (feats // rows), 1)
    out[pl.ds(rows, 16), :] = stacked([gain_a[...], gain_f[...], docs])


def first_message(hidden, gain_a, gain_f, ids):
    shape = (hidden.shape[0] + 16, hidden.shape[1])
    arrays = (hidden, gain_a, gain_f, ids)
    return pl.pallas_call(
        first_message_kernel,
        grid=(1,),
        in_specs=[fixed(a.shape) for a in arrays],
        out_specs=fixed(shape),
        out_shape=pltpu.HBM(shape, bf16),
        compiler_params=params(WIDE),
        name="first_message",
    )(*arrays)


def total_of(parts):
    parts = parts.astype(f32)
    return parts[0:1] + parts[1:2] + parts[2:3]


def below(row, feats):
    return jnp.concatenate([stacked(three_parts(row))] * (feats // row.shape[1]), 1)


def ffn_copies_kernel(group, own, after, copies, message, sums):
    step = pl.program_id(0)
    rows, feats = own.shape
    for k in range(copies.shape[0]):
        copies[k] = group[pl.ds(0, rows), :]
    part = total_of(group[pl.ds(rows, 16), :])[:, :rows]

    @pl.when(step == 0)
    def _():
        message[pl.ds(0, rows), :] = own[...]
        sums[...] = part

    @pl.when(step > 0)
    def _():
        sums[...] += part

    @pl.when(step == pl.num_programs(0) - 1)
    def _():
        message[pl.ds(rows, 16), :] = below(sums[...], feats)


def ffn_copies(group, own, count, after):
    parts, tall, feats = group.shape
    rows = own.shape[0]
    return pl.pallas_call(
        ffn_copies_kernel,
        grid=(parts,),
        in_specs=[
            pl.BlockSpec((None, tall, feats), lambda z: (z, 0, 0)),
            fixed(own.shape),
            pl.BlockSpec(memory_space=pl.ANY),
        ],
        out_specs=[
            pl.BlockSpec((count, None, rows, feats), lambda z: (0, z, 0, 0)),
            fixed((tall, feats)),
        ],
        out_shape=[
            pltpu.HBM((count, parts, rows, feats), bf16),
            pltpu.HBM((tall, feats), bf16),
        ],
        scratch_shapes=[pltpu.VMEM((1, rows), f32)],
        compiler_params=params(),
        name="ffn_copies",
    )(group, own, after)


def kv_sum_kernel(width, arrived, docs, table, place, out):
    rows = out.shape[1] - 16
    kv = jnp.sum(arrived[:, pl.ds(0, rows), :].astype(f32), axis=0).astype(bf16)
    sums = jnp.sum(arrived[:, pl.ds(rows, 16), :].astype(f32), axis=0)
    r = lax.rsqrt((sums[0:1] + sums[1:2] + sums[2:3]) / width + norm_eps)
    tail = stacked(three_parts(r), [docs[...].astype(f32)[2:3, :rows]])
    for copy in range(out.shape[0]):
        out[copy, pl.ds(0, rows), :] = kv
        out[copy, pl.ds(rows, 16), :] = tail


def kv_sum(width, arrived, docs, copies, *after):
    blocks, tall, lanes = arrived.shape
    rows = HD
    last = tall - rows - 16
    return pl.pallas_call(
        functools.partial(kv_sum_kernel, width),
        grid=(1,),
        in_specs=[
            pl.BlockSpec(
                (pl.Element(blocks), pl.Element(rows + 16), pl.Element(lanes)),
                lambda i: (0, last, 0),
            ),
            pl.BlockSpec((16, docs.shape[1]), lambda i: (rows // 16, 0)),
        ]
        + [pl.BlockSpec(memory_space=pl.ANY)] * len(after),
        out_specs=fixed((copies, rows + 16, lanes)),
        out_shape=pltpu.HBM((copies, rows + 16, lanes), bf16),
        compiler_params=params(),
        name="kv_sum",
    )(arrived, docs, *after)


def rotate(values, table):
    lower = lax.broadcasted_iota(jnp.int32, table.shape, 1) < HD // 2
    swapped = pltpu.roll(table, HD // 2, 1)
    cosine = jnp.where(lower, table, swapped)
    sine = jnp.where(lower, -swapped, table)
    return values * cosine + pltpu.roll(values, HD // 2, 1) * sine


def column_of(row):
    n = row.shape[1]
    same = lax.broadcasted_iota(jnp.int32, (n, n), 0) == lax.broadcasted_iota(jnp.int32, (n, n), 1)
    return jnp.sum(jnp.where(same, row, f32(0.0)), axis=1, keepdims=True)


def halves(value):
    high = value.astype(bf16)
    return high, (value - high.astype(f32)).astype(bf16)


def attend_kernel(q_in, kv_in, table, resid, message, out, keys, values, r_all, docs_all):
    rows, feats = out.shape
    heads = feats // HD
    tokens = keys.shape[0]
    x_pos = lax.axis_index("x")
    lower = lax.broadcasted_iota(jnp.int32, (rows, HD), 1) < HD // 2
    for k in range(tokens // rows):
        first = kv_in[2 * k, pl.ds(0, rows), :].astype(f32)
        second = kv_in[2 * k + 1, pl.ds(0, rows), :].astype(f32)
        tail = kv_in[2 * k, pl.ds(rows, 16), :].astype(f32)
        block = pl.ds(k * rows, rows)
        key = jnp.where(lower, first, pltpu.roll(second, HD // 2, 1))
        high, low = halves(rotate(key, table[block, :]))
        keys[block, :] = jnp.concatenate([high, high, low], 1)
        value = jnp.where(lower, pltpu.roll(first, HD // 2, 1), second).astype(bf16)
        values[block, :] = value
        values[pl.ds(tokens + k * rows, rows), :] = value
        r_all[:, block] = total_of(tail)
        docs_all[:, block] = tail[3:4]

    own = pl.ds(pl.multiple_of(x_pos * rows, rows), rows)
    r_own = column_of(r_all[:, own]) * (1.0 / HD**0.5)
    key_ids = lax.broadcasted_iota(jnp.int32, (rows, tokens), 1)
    own_ids = lax.broadcasted_iota(jnp.int32, (rows, tokens), 0) + x_pos * rows
    allowed = (key_ids <= own_ids) & (docs_all[...] == column_of(docs_all[:, own]))
    squares = jnp.zeros((rows, 1), f32)
    for h in range(heads):
        query = jnp.sum(q_in[:, pl.ds(h * rows, rows), :].astype(f32), axis=0)
        high, low = halves(rotate(query, table[own, :]) * r_own)
        scores = lax.dot_general(
            jnp.concatenate([high, low, high], 1), keys[...], (((1,), (1,)), ((), ())),
            preferred_element_type=f32,
        )
        scores = jnp.where(allowed, scores * r_all[...], f32(-1e30))
        peak = jnp.max(scores, axis=-1, keepdims=True)
        weights = jnp.where(allowed, jnp.exp(scores - peak), f32(0.0))
        total = jnp.sum(weights, axis=-1, keepdims=True)
        weights = jnp.concatenate(halves(weights * r_all[...]), 1)
        context = jnp.dot(weights, values[...], preferred_element_type=f32) / total
        lanes = pl.ds(h * HD, HD)
        result = (resid[:, lanes].astype(f32) + context).astype(bf16)
        out[:, lanes] = result
        message[pl.ds(0, rows), lanes] = result
        result = result.astype(f32)
        squares += jnp.sum(result * result, axis=1, keepdims=True)
    message[pl.ds(rows, 16), :] = below(row_of(squares), feats)


def attend(q_in, kv_in, table, swapped):
    rows, feats = swapped.shape[0] - 16, swapped.shape[1]
    heads, tokens = feats // HD, table.shape[0]
    shape = swapped.shape
    return pl.pallas_call(
        attend_kernel,
        grid=(1,),
        in_specs=[
            fixed((q_in.shape[0], heads * rows, HD)),
            fixed(kv_in.shape),
            fixed(table.shape),
            fixed((rows, feats)),
        ],
        out_specs=[fixed(shape), fixed((rows, feats))],
        out_shape=[pltpu.HBM(shape, bf16), pltpu.HBM((rows, feats), bf16)],
        scratch_shapes=[
            pltpu.VMEM((tokens, 3 * HD), bf16),
            pltpu.VMEM((2 * tokens, HD), bf16),
            pltpu.VMEM((1, tokens), f32),
            pltpu.VMEM((1, tokens), f32),
        ],
        compiler_params=params(),
        name="attend",
    )(q_in, kv_in, table, swapped)


def attn_left_kernel(scale, own_rows, gain, kv, out):
    blocks, rows, feats = own_rows.shape
    for k in range(blocks):
        parts = kv[2 * k, pl.ds(rows, 16), :].astype(f32)
        r = parts[0:1] + parts[1:2] + parts[2:3]
        turned = (own_rows[k].astype(f32) * gain[...].astype(f32)).T
        out[:, pl.ds(k * rows, rows)] = (turned * (r * r * scale)).astype(bf16)


def attn_left(scale, own_rows, gain, kv_all):
    blocks, rows, feats = own_rows.shape
    arrays = (own_rows, gain, kv_all)
    return pl.pallas_call(
        functools.partial(attn_left_kernel, scale),
        grid=(1,),
        in_specs=[fixed(a.shape) for a in arrays],
        out_specs=fixed((feats, blocks * rows)),
        out_shape=jax.ShapeDtypeStruct((feats, blocks * rows), bf16),
        compiler_params=params(),
        name="attn_left",
    )(*arrays)


def hessian_kernel(
    scale, width, place, left_a, cols_a, gain_a, ffn_rows, gain_row, total, cols_f, gain_f,
    passed, out, diagonal, passed_out, left_f,
):
    blocks, rows, feats = cols_a.shape
    row, col = place[0], place[1] + pl.program_id(0)

    @pl.when(pl.program_id(0) == 0)
    def _():
        part = pl.ds(pl.multiple_of(lax.axis_index("seq") * rows, rows), rows)
        squares = jnp.zeros((1, rows), f32)
        for k in range(blocks):
            weight = column_of(scale / (total[k] / width + norm_eps))
            block = ffn_rows[k, pl.ds(0, rows), :].astype(f32) * gain_row[...].astype(f32)
            left_f[:, pl.ds(k * rows, rows)] = (block * weight).astype(bf16).T
            mine = ffn_rows[k, pl.ds(0, rows), part].astype(f32) * gain_row[:, part].astype(f32)
            squares += jnp.sum(mine * mine * weight, axis=0, keepdims=True)
        diagonal[...] = squares
        passed_out[...] = passed[...]

    def product(left, cols, gain):
        right = cols[...].reshape(blocks * rows, feats)
        return (jnp.dot(left[...], right, preferred_element_type=f32) * gain[...]).astype(bf16)

    @pl.when(row < col)
    def _():
        out[...] = product(left_a, cols_a, gain_a)

    @pl.when(row > col)
    def _():
        out[...] = product(left_f, cols_f, gain_f)

    @pl.when(row == col)
    def _():
        upper = product(left_a, cols_a, gain_a)
        lower = product(left_f, cols_f, gain_f)
        row_ids = lax.broadcasted_iota(jnp.int32, lower.shape, 0)
        col_ids = lax.broadcasted_iota(jnp.int32, lower.shape, 1)
        out[...] = jnp.where(row_ids <= col_ids, upper, lower)


def hessian(
    scale, width, place, left_a, cols_a, gain_a, ffn_rows, gain_row, total, cols_f, gain_f, passed
):
    blocks, parts, rows, feats = cols_a.shape
    tokens = blocks * rows

    def upper_at(z, at):
        return jnp.clip(jnp.maximum(z, at[0] - at[1]), 0, parts - 1)

    def lower_at(z, at):
        return jnp.clip(jnp.minimum(z, at[0] - at[1]), 0, parts - 1)

    gain = pl.BlockSpec((None, 1, feats), lambda z, at: (z, 0, 0))
    return pl.pallas_call(
        functools.partial(hessian_kernel, scale, width),
        grid_spec=pltpu.PrefetchScalarGridSpec(
            num_scalar_prefetch=1,
            grid=(parts,),
            in_specs=[
                fixed(left_a.shape),
                pl.BlockSpec((blocks, None, rows, feats), lambda z, at: (0, upper_at(z, at), 0, 0)),
                gain,
                fixed(ffn_rows.shape),
                fixed(gain_row.shape),
                fixed(total.shape),
                pl.BlockSpec((blocks, None, rows, feats), lambda z, at: (0, lower_at(z, at), 0, 0)),
                gain,
                fixed(passed.shape),
            ],
            out_specs=[
                pl.BlockSpec((feats, feats), lambda z, at: (0, z)),
                fixed((1, rows)),
                fixed(passed.shape),
            ],
            scratch_shapes=[pltpu.VMEM((feats, tokens), bf16)],
        ),
        out_shape=[
            jax.ShapeDtypeStruct((feats, parts * feats), bf16),
            jax.ShapeDtypeStruct((1, rows), f32),
            jax.ShapeDtypeStruct(passed.shape, bf16),
        ],
        compiler_params=params(),
        name="hessian",
    )(place, left_a, cols_a, gain_a, ffn_rows, gain_row, total, cols_f, gain_f, passed)


def on_device(hidden, segment_ids, gain_attn, gain_ffn, w_query, w_key, w_value):
    x_pos = lax.axis_index("x")
    zl_pos = lax.axis_index(ZL)
    seq_pos = lax.axis_index("seq")
    nx, nz, ns = lax.axis_size("x"), lax.axis_size(ZL), lax.axis_size("seq")
    rows, feats = hidden.shape[1:]
    tokens = rows * ns
    width = feats * nx * nz
    scale = 2.0 / tokens
    place = jnp.stack([x_pos * nz + zl_pos, seq_pos * nz])
    place = place.astype(jnp.int32)

    swapped = swap_x_seq(first_message(hidden[0], gain_attn, gain_ffn, segment_ids))
    half = HD // 2
    freq = rope_base ** (-(jnp.arange(half, dtype=f32) * 2.0 / HD))
    angle = jnp.arange(tokens, dtype=f32)[:, None] * freq[None, :]
    table = jnp.concatenate([jnp.cos(angle), jnp.sin(angle)], 1)
    group = lax.all_gather(swapped, ZL)
    copies, gain_a, gain_f = attn_copies(group, nx)
    attn_rows = lax.all_gather(hidden[0], "seq")
    attn_cols = lax.all_to_all(copies, "x", 0, 0)

    message = project(attn_cols, gain_a, w_query, w_key, w_value, attn_rows)
    arrived = lax.all_to_all(lax.all_to_all(message, "x", 0, 0), "seq", 0, 0)
    kv = lax.all_to_all(kv_sum(width, arrived, swapped, 2 * nx, table, place), ("x", "zb"), 0, 0)
    message, section_out = attend(arrived, kv, table, swapped)
    left_a = attn_left(scale, attn_rows, gain_attn, kv)

    out_rows = swap_x_seq(section_out)
    group = lax.all_gather(message, ZL)
    copies, message = ffn_copies(group, out_rows, nx, left_a)
    ffn_cols = lax.all_to_all(copies, "x", 0, 0)
    ffn_rows = lax.all_gather(message, "seq")
    total = jnp.sum(ffn_rows[:, rows : rows + 3, :rows].astype(f32), axis=(0, 1))
    total = lax.all_gather(total[None], "x")
    count = lax.axis_size("phase")
    passed = lax.dynamic_slice_in_dim(ffn_rows[:, :rows], seq_pos, 1, 0)
    passed = lax.ppermute(passed, "phase", [(p, (p + 1) % count) for p in range(count)])
    hessians, ffn_diagonal, passed = hessian(
        scale,
        width,
        place,
        left_a,
        attn_cols,
        gain_a,
        ffn_rows,
        gain_ffn,
        total,
        ffn_cols,
        gain_f,
        passed,
    )
    return (passed, hessians[None], ffn_diagonal)


def solution(mesh):
    phase, tensor, seq = (mesh.shape[a] for a in ("phase", "tensor", "seq"))
    lines = Mesh(
        mesh.devices.reshape(phase, tensor // 4, 2, 2, seq), ("phase", "x", "za", "zb", "seq")
    )
    tiled = P("phase", "seq", TENSOR)
    return jax.shard_map(
        on_device,
        mesh=lines,
        in_specs=(
            tiled,
            P("phase", "seq"),
            P("phase", TENSOR),
            P("phase", TENSOR),
            tiled,
            tiled,
            tiled,
        ),
        out_specs=(tiled, P("phase", TENSOR, "seq"), P("phase", GROUP)),
        check_vma=False,
    )
```

```python
import functools

import jax
import jax.numpy as jnp
from jax import lax
from jax.experimental import pallas as pl
from jax.experimental.pallas import tpu as pltpu
from jax.sharding import Mesh, PartitionSpec as P

HD = 128
norm_eps = 1e-05
rope_base = 500000.0
ZL = ("za", "zb")
TENSOR = ("x", "za", "zb")
GROUP = TENSOR + ("seq",)
f32 = jnp.float32
bf16 = jnp.bfloat16
LIMIT = 24 * 1024 * 1024
WIDE = 57 * 1024 * 1024
PROJECT = 24 * 1024 * 1024


def swap_x_seq(value):
    nx, nz, ns = lax.axis_size("x"), lax.axis_size(ZL), lax.axis_size("seq")
    pairs = [
        ((x * nz + z) * ns + s, (s * nz + z) * ns + x)
        for x in range(nx)
        for z in range(nz)
        for s in range(ns)
    ]
    return lax.ppermute(value, GROUP, pairs)


def project_kernel(cols, gain, wq, wk, wv, after, out, q_acc, kv_acc, squares, left):
    step = pl.program_id(0)
    blocks, parts, rows, feats = cols.shape
    part = jnp.zeros((blocks * rows, 1), f32)
    for z in range(parts):
        raw = cols[:, z].reshape(blocks * rows, feats).astype(f32)
        left[:, pl.ds(z * feats, feats)] = (raw * gain[z]).astype(bf16)
        part += jnp.sum(raw * raw, axis=1, keepdims=True)
    kv_w = jnp.concatenate([wk[...], wv[...]], 0)
    kv = lax.dot_general(left[...], kv_w, (((1,), (1,)), ((), ())), preferred_element_type=f32)
    q = jnp.dot(left[...], wq[...], preferred_element_type=f32)

    @pl.when(step == 0)
    def _():
        q_acc[...] = q
        kv_acc[...] = kv
        squares[...] = part

    @pl.when(step > 0)
    def _():
        q_acc[...] += q
        kv_acc[...] += kv
        squares[...] += part

    @pl.when(step == pl.num_programs(0) - 1)
    def _():
        heads = q_acc.shape[1] // HD
        for k in range(blocks):
            block = pl.ds(k * rows, rows)
            out[k, pl.ds(heads * rows, rows), :] = kv_acc[block, :].astype(bf16)
            sums = stacked(three_parts(row_of(squares[block, :])))
            out[k, pl.ds((heads + 1) * rows, 16), :] = sums
            for h in range(heads):
                out[k, pl.ds(h * rows, rows), :] = q_acc[block, pl.ds(h * HD, HD)].astype(bf16)


def project(cols, gain, w_query, w_key, w_value, after):
    blocks, parts, rows, feats = cols.shape
    q_width, kv_width = w_query.shape[2], 2 * w_key.shape[2]
    heads = q_width // HD
    pair = 2
    kv_spec = pl.BlockSpec((None, w_key.shape[2], pair * feats), lambda z: (0, 0, z))
    return pl.pallas_call(
        project_kernel,
        grid=(parts // pair,),
        in_specs=[
            pl.BlockSpec((blocks, pair, rows, feats), lambda z: (0, z, 0, 0)),
            pl.BlockSpec((pair, 1, feats), lambda z: (z, 0, 0)),
            pl.BlockSpec((None, pair * feats, q_width), lambda z: (0, z, 0)),
            kv_spec,
            kv_spec,
            pl.BlockSpec(memory_space=pl.ANY),
        ],
        out_specs=fixed((blocks, (heads + 1) * rows + 16, HD)),
        out_shape=pltpu.HBM((blocks, (heads + 1) * rows + 16, HD), bf16),
        scratch_shapes=[
            pltpu.VMEM((blocks * rows, q_width), f32),
            pltpu.VMEM((blocks * rows, kv_width), f32),
            pltpu.VMEM((blocks * rows, 1), f32),
            pltpu.VMEM((blocks * rows, pair * feats), bf16),
        ],
        compiler_params=params(PROJECT),
        name="project",
    )(cols, gain, w_query, w_key.swapaxes(1, 2), w_value.swapaxes(1, 2), after)


def fixed(shape):
    return pl.BlockSpec(shape, lambda *at: (0,) * len(shape))


def params(limit=LIMIT):
    return pltpu.CompilerParams(vmem_limit_bytes=limit)


def three_parts(value):
    parts = []
    for _ in range(3):
        part = value.astype(bf16)
        parts.append(part)
        value = value - part.astype(f32)
    return parts


def row_of(column):
    n = column.shape[0]
    same = lax.broadcasted_iota(jnp.int32, (n, n), 0) == lax.broadcasted_iota(jnp.int32, (n, n), 1)
    return jnp.sum(jnp.where(same, column, f32(0.0)), axis=0, keepdims=True)


def stacked(parts, more=()):
    rows = list(parts) + list(more)
    rows.append(jnp.zeros((16 - len(rows), rows[0].shape[1]), f32))
    return jnp.concatenate([row.astype(f32) for row in rows]).astype(bf16)


def attn_copies_kernel(group, copies, gain_a, gain_f):
    rows = copies.shape[1]
    for k in range(copies.shape[0]):
        copies[k] = group[pl.ds(0, rows), :]
    gains = group[pl.ds(rows, 16), :].astype(f32)
    gain_a[...] = gains[0:1]
    gain_f[...] = gains[1:2]


def attn_copies(group, count):
    parts, tall, feats = group.shape
    rows = tall - 16
    gain = pl.BlockSpec((None, 1, feats), lambda z: (z, 0, 0))
    gain_shape = pltpu.HBM((parts, 1, feats), f32)
    return pl.pallas_call(
        attn_copies_kernel,
        grid=(parts,),
        in_specs=[pl.BlockSpec((None, tall, feats), lambda z: (z, 0, 0))],
        out_specs=[
            pl.BlockSpec((count, None, rows, feats), lambda z: (0, z, 0, 0)),
            gain,
            gain,
        ],
        out_shape=[
            pltpu.HBM((count, parts, rows, feats), bf16),
            gain_shape,
            gain_shape,
        ],
        compiler_params=params(),
        name="attn_copies",
    )(group)


def first_message_kernel(hidden, gain_a, gain_f, ids, out):
    rows, feats = hidden.shape
    out[pl.ds(0, rows), :] = hidden[...]
    docs = jnp.concatenate([ids[...].astype(f32)] * (feats // rows), 1)
    out[pl.ds(rows, 16), :] = stacked([gain_a[...], gain_f[...], docs])


def first_message(hidden, gain_a, gain_f, ids):
    shape = (hidden.shape[0] + 16, hidden.shape[1])
    arrays = (hidden, gain_a, gain_f, ids)
    return pl.pallas_call(
        first_message_kernel,
        grid=(1,),
        in_specs=[fixed(a.shape) for a in arrays],
        out_specs=fixed(shape),
        out_shape=pltpu.HBM(shape, bf16),
        compiler_params=params(WIDE),
        name="first_message",
    )(*arrays)


def total_of(parts):
    parts = parts.astype(f32)
    return parts[0:1] + parts[1:2] + parts[2:3]


def below(row, feats):
    return jnp.concatenate([stacked(three_parts(row))] * (feats // row.shape[1]), 1)


def ffn_copies_kernel(group, own, after, copies, message, sums):
    step = pl.program_id(0)
    rows, feats = own.shape
    for k in range(copies.shape[0]):
        copies[k] = group[pl.ds(0, rows), :]
    part = total_of(group[pl.ds(rows, 16), :])[:, :rows]

    @pl.when(step == 0)
    def _():
        message[pl.ds(0, rows), :] = own[...]
        sums[...] = part

    @pl.when(step > 0)
    def _():
        sums[...] += part

    @pl.when(step == pl.num_programs(0) - 1)
    def _():
        message[pl.ds(rows, 16), :] = below(sums[...], feats)


def ffn_copies(group, own, count, after):
    parts, tall, feats = group.shape
    rows = own.shape[0]
    return pl.pallas_call(
        ffn_copies_kernel,
        grid=(parts,),
        in_specs=[
            pl.BlockSpec((None, tall, feats), lambda z: (z, 0, 0)),
            fixed(own.shape),
            pl.BlockSpec(memory_space=pl.ANY),
        ],
        out_specs=[
            pl.BlockSpec((count, None, rows, feats), lambda z: (0, z, 0, 0)),
            fixed((tall, feats)),
        ],
        out_shape=[
            pltpu.HBM((count, parts, rows, feats), bf16),
            pltpu.HBM((tall, feats), bf16),
        ],
        scratch_shapes=[pltpu.VMEM((1, rows), f32)],
        compiler_params=params(),
        name="ffn_copies",
    )(group, own, after)


def kv_sum_kernel(width, arrived, docs, table, out):
    rows = out.shape[1] - 16
    kv = jnp.sum(arrived[:, pl.ds(0, rows), :].astype(f32), axis=0).astype(bf16)
    sums = jnp.sum(arrived[:, pl.ds(rows, 16), :].astype(f32), axis=0)
    r = lax.rsqrt((sums[0:1] + sums[1:2] + sums[2:3]) / width + norm_eps)
    tail = stacked(three_parts(r), [docs[...].astype(f32)[2:3, :rows]])
    for copy in range(out.shape[0]):
        out[copy, pl.ds(0, rows), :] = kv
        out[copy, pl.ds(rows, 16), :] = tail


def kv_sum(width, arrived, docs, copies, *after):
    blocks, tall, lanes = arrived.shape
    rows = HD
    last = tall - rows - 16
    return pl.pallas_call(
        functools.partial(kv_sum_kernel, width),
        grid=(1,),
        in_specs=[
            pl.BlockSpec(
                (pl.Element(blocks), pl.Element(rows + 16), pl.Element(lanes)),
                lambda i: (0, last, 0),
            ),
            pl.BlockSpec((16, docs.shape[1]), lambda i: (rows // 16, 0)),
        ]
        + [pl.BlockSpec(memory_space=pl.ANY)] * len(after),
        out_specs=fixed((copies, rows + 16, lanes)),
        out_shape=pltpu.HBM((copies, rows + 16, lanes), bf16),
        compiler_params=params(),
        name="kv_sum",
    )(arrived, docs, *after)


def rotate(values, table):
    lower = lax.broadcasted_iota(jnp.int32, table.shape, 1) < HD // 2
    swapped = pltpu.roll(table, HD // 2, 1)
    cosine = jnp.where(lower, table, swapped)
    sine = jnp.where(lower, -swapped, table)
    return values * cosine + pltpu.roll(values, HD // 2, 1) * sine


def column_of(row):
    n = row.shape[1]
    same = lax.broadcasted_iota(jnp.int32, (n, n), 0) == lax.broadcasted_iota(jnp.int32, (n, n), 1)
    return jnp.sum(jnp.where(same, row, f32(0.0)), axis=1, keepdims=True)


def halves(value):
    high = value.astype(bf16)
    return high, (value - high.astype(f32)).astype(bf16)


def attend_kernel(q_in, kv_in, table, resid, copies, out, keys, values, r_all, docs_all):
    rows, feats = out.shape
    heads = feats // HD
    tokens = keys.shape[0]
    x_pos = lax.axis_index("x")
    lower = lax.broadcasted_iota(jnp.int32, (rows, HD), 1) < HD // 2
    for k in range(tokens // rows):
        first = kv_in[2 * k, pl.ds(0, rows), :].astype(f32)
        second = kv_in[2 * k + 1, pl.ds(0, rows), :].astype(f32)
        tail = kv_in[2 * k, pl.ds(rows, 16), :].astype(f32)
        block = pl.ds(k * rows, rows)
        key = jnp.where(lower, first, pltpu.roll(second, HD // 2, 1))
        high, low = halves(rotate(key, table[block, :]))
        keys[block, :] = jnp.concatenate([high, high, low], 1)
        value = jnp.where(lower, pltpu.roll(first, HD // 2, 1), second).astype(bf16)
        values[block, :] = value
        values[pl.ds(tokens + k * rows, rows), :] = value
        r_all[:, block] = total_of(tail)
        docs_all[:, block] = tail[3:4]

    own = pl.ds(pl.multiple_of(x_pos * rows, rows), rows)
    r_own = column_of(r_all[:, own]) * (1.0 / HD**0.5)
    key_ids = lax.broadcasted_iota(jnp.int32, (rows, tokens), 1)
    own_ids = lax.broadcasted_iota(jnp.int32, (rows, tokens), 0) + x_pos * rows
    allowed = (key_ids <= own_ids) & (docs_all[...] == column_of(docs_all[:, own]))
    squares = jnp.zeros((rows, 1), f32)
    for h in range(heads):
        query = jnp.sum(q_in[:, pl.ds(h * rows, rows), :].astype(f32), axis=0)
        high, low = halves(rotate(query, table[own, :]) * r_own)
        scores = lax.dot_general(
            jnp.concatenate([high, low, high], 1), keys[...], (((1,), (1,)), ((), ())),
            preferred_element_type=f32,
        )
        scores = jnp.where(allowed, scores * r_all[...], f32(-1e30))
        peak = jnp.max(scores, axis=-1, keepdims=True)
        weights = jnp.where(allowed, jnp.exp(scores - peak), f32(0.0))
        total = jnp.sum(weights, axis=-1, keepdims=True)
        weights = jnp.concatenate(halves(weights * r_all[...]), 1)
        context = jnp.dot(weights, values[...], preferred_element_type=f32) / total
        lanes = pl.ds(h * HD, HD)
        result = (resid[:, lanes].astype(f32) + context).astype(bf16)
        out[:, lanes] = result
        for copy in range(copies.shape[0]):
            copies[copy, pl.ds(0, rows), lanes] = result
        result = result.astype(f32)
        squares += jnp.sum(result * result, axis=1, keepdims=True)
    tail = below(row_of(squares), feats)
    for copy in range(copies.shape[0]):
        copies[copy, pl.ds(rows, 16), :] = tail


def attend(q_in, kv_in, table, swapped, copies):
    rows, feats = swapped.shape[0] - 16, swapped.shape[1]
    heads, tokens = feats // HD, table.shape[0]
    shape = (copies, rows + 16, feats)
    return pl.pallas_call(
        attend_kernel,
        grid=(1,),
        in_specs=[
            fixed((q_in.shape[0], heads * rows, HD)),
            fixed(kv_in.shape),
            fixed(table.shape),
            fixed((rows, feats)),
        ],
        out_specs=[fixed(shape), fixed((rows, feats))],
        out_shape=[pltpu.HBM(shape, bf16), pltpu.HBM((rows, feats), bf16)],
        scratch_shapes=[
            pltpu.VMEM((tokens, 3 * HD), bf16),
            pltpu.VMEM((2 * tokens, HD), bf16),
            pltpu.VMEM((1, tokens), f32),
            pltpu.VMEM((1, tokens), f32),
        ],
        compiler_params=params(),
        name="attend",
    )(q_in, kv_in, table, swapped)


def attn_left_kernel(scale, own_rows, gain, kv, after, out):
    blocks, rows, feats = own_rows.shape
    for k in range(blocks):
        parts = kv[2 * k, pl.ds(rows, 16), :].astype(f32)
        r = parts[0:1] + parts[1:2] + parts[2:3]
        turned = (own_rows[k].astype(f32) * gain[...].astype(f32)).T
        out[:, pl.ds(k * rows, rows)] = (turned * (r * r * scale)).astype(bf16)


def attn_left(scale, own_rows, gain, kv_all, after):
    blocks, rows, feats = own_rows.shape
    arrays = (own_rows, gain, kv_all)
    return pl.pallas_call(
        functools.partial(attn_left_kernel, scale),
        grid=(1,),
        in_specs=[fixed(a.shape) for a in arrays] + [pl.BlockSpec(memory_space=pl.ANY)],
        out_specs=fixed((feats, blocks * rows)),
        out_shape=jax.ShapeDtypeStruct((feats, blocks * rows), bf16),
        compiler_params=params(),
        name="attn_left",
    )(*arrays, after)


def hessian_kernel(
    scale, width, place, left_a, cols_a, gain_a, ffn_rows, gain_row, total, cols_f, gain_f,
    passed, out, diagonal, passed_out, left_f,
):
    blocks, rows, feats = cols_a.shape
    row, col = place[0], place[1] + pl.program_id(0)

    @pl.when(pl.program_id(0) == 0)
    def _():
        part = pl.ds(pl.multiple_of(lax.axis_index("seq") * rows, rows), rows)
        squares = jnp.zeros((1, rows), f32)
        for k in range(blocks):
            weight = column_of(scale / (total[k] / width + norm_eps))
            block = ffn_rows[k, pl.ds(0, rows), :].astype(f32) * gain_row[...].astype(f32)
            left_f[:, pl.ds(k * rows, rows)] = (block * weight).astype(bf16).T
            mine = ffn_rows[k, pl.ds(0, rows), part].astype(f32) * gain_row[:, part].astype(f32)
            squares += jnp.sum(mine * mine * weight, axis=0, keepdims=True)
        diagonal[...] = squares
        passed_out[...] = passed[...]

    def product(left, cols, gain):
        right = cols[...].reshape(blocks * rows, feats)
        return (jnp.dot(left[...], right, preferred_element_type=f32) * gain[...]).astype(bf16)

    @pl.when(row < col)
    def _():
        out[...] = product(left_a, cols_a, gain_a)

    @pl.when(row > col)
    def _():
        out[...] = product(left_f, cols_f, gain_f)

    @pl.when(row == col)
    def _():
        upper = product(left_a, cols_a, gain_a)
        lower = product(left_f, cols_f, gain_f)
        row_ids = lax.broadcasted_iota(jnp.int32, lower.shape, 0)
        col_ids = lax.broadcasted_iota(jnp.int32, lower.shape, 1)
        out[...] = jnp.where(row_ids <= col_ids, upper, lower)


def hessian(
    scale, width, place, left_a, cols_a, gain_a, ffn_rows, gain_row, total, cols_f, gain_f, passed
):
    blocks, parts, rows, feats = cols_a.shape
    tokens = blocks * rows

    def upper_at(z, at):
        return jnp.clip(jnp.maximum(z, at[0] - at[1]), 0, parts - 1)

    def lower_at(z, at):
        return jnp.clip(jnp.minimum(z, at[0] - at[1]), 0, parts - 1)

    gain = pl.BlockSpec((None, 1, feats), lambda z, at: (z, 0, 0))
    return pl.pallas_call(
        functools.partial(hessian_kernel, scale, width),
        grid_spec=pltpu.PrefetchScalarGridSpec(
            num_scalar_prefetch=1,
            grid=(parts,),
            in_specs=[
                fixed(left_a.shape),
                pl.BlockSpec((blocks, None, rows, feats), lambda z, at: (0, upper_at(z, at), 0, 0)),
                gain,
                fixed(ffn_rows.shape),
                fixed(gain_row.shape),
                fixed(total.shape),
                pl.BlockSpec((blocks, None, rows, feats), lambda z, at: (0, lower_at(z, at), 0, 0)),
                gain,
                fixed(passed.shape),
            ],
            out_specs=[
                pl.BlockSpec((feats, feats), lambda z, at: (0, z)),
                fixed((1, rows)),
                fixed(passed.shape),
            ],
            scratch_shapes=[pltpu.VMEM((feats, tokens), bf16)],
        ),
        out_shape=[
            jax.ShapeDtypeStruct((feats, parts * feats), bf16),
            jax.ShapeDtypeStruct((1, rows), f32),
            jax.ShapeDtypeStruct(passed.shape, bf16),
        ],
        compiler_params=params(),
        name="hessian",
    )(place, left_a, cols_a, gain_a, ffn_rows, gain_row, total, cols_f, gain_f, passed)


def on_device(hidden, segment_ids, gain_attn, gain_ffn, w_query, w_key, w_value):
    x_pos = lax.axis_index("x")
    zl_pos = lax.axis_index(ZL)
    seq_pos = lax.axis_index("seq")
    nx, nz, ns = lax.axis_size("x"), lax.axis_size(ZL), lax.axis_size("seq")
    rows, feats = hidden.shape[1:]
    tokens = rows * ns
    width = feats * nx * nz
    scale = 2.0 / tokens
    place = jnp.stack([x_pos * nz + zl_pos, seq_pos * nz])
    place = place.astype(jnp.int32)

    swapped = swap_x_seq(first_message(hidden[0], gain_attn, gain_ffn, segment_ids))
    half = HD // 2
    freq = rope_base ** (-(jnp.arange(half, dtype=f32) * 2.0 / HD))
    angle = jnp.arange(tokens, dtype=f32)[:, None] * freq[None, :]
    table = jnp.concatenate([jnp.cos(angle), jnp.sin(angle)], 1)
    group = lax.all_gather(swapped, ZL)
    swapped = pltpu.with_memory_space_constraint(swapped, pltpu.HBM)
    copies, gain_a, gain_f = attn_copies(group, nx)
    attn_rows = lax.all_gather(hidden[0], "seq")
    attn_cols = lax.all_to_all(copies, "x", 0, 0)

    w_query = pltpu.with_memory_space_constraint(w_query, pltpu.HBM)
    message = project(attn_cols, gain_a, w_query, w_key, w_value, attn_rows)
    arrived = lax.all_to_all(lax.all_to_all(message, "x", 0, 0), "seq", 0, 0)
    kv = lax.all_to_all(kv_sum(width, arrived, swapped, 2 * nx, table), ("x", "zb"), 0, 0)
    copies, section_out = attend(arrived, kv, table, swapped, nz)
    left_a = attn_left(scale, attn_rows, gain_attn, kv, place)

    out_rows = pltpu.with_memory_space_constraint(swap_x_seq(section_out), pltpu.HBM)
    group = lax.all_to_all(copies, ZL, 0, 0)
    copies, message = ffn_copies(group, out_rows, nx, left_a)
    ffn_cols = lax.all_to_all(copies, "x", 0, 0)
    ffn_rows = lax.all_gather(message, "seq")
    total = jnp.sum(ffn_rows[:, rows : rows + 3, :rows].astype(f32), axis=(0, 1))
    total = lax.all_gather(total[None], "x")
    count = lax.axis_size("phase")
    passed = lax.dynamic_slice_in_dim(ffn_rows[:, :rows], seq_pos, 1, 0)
    passed = lax.ppermute(passed, "phase", [(p, (p + 1) % count) for p in range(count)])
    hessians, ffn_diagonal, passed = hessian(
        scale,
        width,
        place,
        left_a,
        attn_cols,
        gain_a,
        ffn_rows,
        gain_ffn,
        total,
        ffn_cols,
        gain_f,
        passed,
    )
    return (passed, hessians[None], ffn_diagonal)


def solution(mesh):
    phase, tensor, seq = (mesh.shape[a] for a in ("phase", "tensor", "seq"))
    lines = Mesh(
        mesh.devices.reshape(phase, tensor // 4, 2, 2, seq), ("phase", "x", "za", "zb", "seq")
    )
    tiled = P("phase", "seq", TENSOR)
    return jax.shard_map(
        on_device,
        mesh=lines,
        in_specs=(
            tiled,
            P("phase", "seq"),
            P("phase", TENSOR),
            P("phase", TENSOR),
            tiled,
            tiled,
            tiled,
        ),
        out_specs=(tiled, P("phase", TENSOR, "seq"), P("phase", GROUP)),
        check_vma=False,
    )
```

```python
import functools

import jax
import jax.numpy as jnp
from jax import lax
from jax.experimental import pallas as pl
from jax.experimental.pallas import tpu as pltpu
from jax.sharding import Mesh, PartitionSpec as P

HD = 128
norm_eps = 1e-05
rope_base = 500000.0
ZL = ("za", "zb")
TENSOR = ("x", "za", "zb")
GROUP = TENSOR + ("seq",)
f32 = jnp.float32
bf16 = jnp.bfloat16
LIMIT = 24 * 1024 * 1024
WIDE = 57 * 1024 * 1024
PROJECT = 57 * 1024 * 1024


def swap_x_seq(value):
    nx, nz, ns = lax.axis_size("x"), lax.axis_size(ZL), lax.axis_size("seq")
    pairs = [
        ((x * nz + z) * ns + s, (s * nz + z) * ns + x)
        for x in range(nx)
        for z in range(nz)
        for s in range(ns)
    ]
    return lax.ppermute(value, GROUP, pairs)


def project_kernel(cols, gain, wq, wk, wv, after, out, q_acc, kv_acc, squares, left):
    step = pl.program_id(0)
    blocks, parts, rows, feats = cols.shape
    part = jnp.zeros((blocks * rows, 1), f32)
    for z in range(parts):
        raw = cols[:, z].reshape(blocks * rows, feats).astype(f32)
        left[:, pl.ds(z * feats, feats)] = (raw * gain[z]).astype(bf16)
        part += jnp.sum(raw * raw, axis=1, keepdims=True)
    kv_w = jnp.concatenate([wk[...], wv[...]], 0)
    kv = lax.dot_general(left[...], kv_w, (((1,), (1,)), ((), ())), preferred_element_type=f32)
    q = jnp.dot(left[...], wq[...], preferred_element_type=f32)

    @pl.when(step == 0)
    def _():
        q_acc[...] = q
        kv_acc[...] = kv
        squares[...] = part

    @pl.when(step > 0)
    def _():
        q_acc[...] += q
        kv_acc[...] += kv
        squares[...] += part

    @pl.when(step == pl.num_programs(0) - 1)
    def _():
        heads = q_acc.shape[1] // HD
        for k in range(blocks):
            block = pl.ds(k * rows, rows)
            out[k, pl.ds(heads * rows, rows), :] = kv_acc[block, :].astype(bf16)
            sums = stacked(three_parts(row_of(squares[block, :])))
            out[k, pl.ds((heads + 1) * rows, 16), :] = sums
            for h in range(heads):
                out[k, pl.ds(h * rows, rows), :] = q_acc[block, pl.ds(h * HD, HD)].astype(bf16)


def project(cols, gain, w_query, w_key, w_value, after):
    blocks, parts, rows, feats = cols.shape
    q_width, kv_width = w_query.shape[2], 2 * w_key.shape[2]
    heads = q_width // HD
    pair = 2
    kv_spec = pl.BlockSpec((None, w_key.shape[2], pair * feats), lambda z: (0, 0, z))
    return pl.pallas_call(
        project_kernel,
        grid=(parts // pair,),
        in_specs=[
            pl.BlockSpec((blocks, pair, rows, feats), lambda z: (0, z, 0, 0)),
            pl.BlockSpec((pair, 1, feats), lambda z: (z, 0, 0)),
            pl.BlockSpec((None, pair * feats, q_width), lambda z: (0, z, 0)),
            kv_spec,
            kv_spec,
            pl.BlockSpec(memory_space=pl.ANY),
        ],
        out_specs=fixed((blocks, (heads + 1) * rows + 16, HD)),
        out_shape=pltpu.HBM((blocks, (heads + 1) * rows + 16, HD), bf16),
        scratch_shapes=[
            pltpu.VMEM((blocks * rows, q_width), f32),
            pltpu.VMEM((blocks * rows, kv_width), f32),
            pltpu.VMEM((blocks * rows, 1), f32),
            pltpu.VMEM((blocks * rows, pair * feats), bf16),
        ],
        compiler_params=params(PROJECT),
        name="project",
    )(cols, gain, w_query, w_key.swapaxes(1, 2), w_value.swapaxes(1, 2), after)


def fixed(shape):
    return pl.BlockSpec(shape, lambda *at: (0,) * len(shape))


def params(limit=LIMIT):
    return pltpu.CompilerParams(vmem_limit_bytes=limit)


def three_parts(value):
    parts = []
    for _ in range(3):
        part = value.astype(bf16)
        parts.append(part)
        value = value - part.astype(f32)
    return parts


def row_of(column):
    n = column.shape[0]
    same = lax.broadcasted_iota(jnp.int32, (n, n), 0) == lax.broadcasted_iota(jnp.int32, (n, n), 1)
    return jnp.sum(jnp.where(same, column, f32(0.0)), axis=0, keepdims=True)


def stacked(parts, more=()):
    rows = list(parts) + list(more)
    rows.append(jnp.zeros((16 - len(rows), rows[0].shape[1]), f32))
    return jnp.concatenate([row.astype(f32) for row in rows]).astype(bf16)


def attn_copies_kernel(group, copies, gain_a, gain_f):
    rows = copies.shape[1]
    for k in range(copies.shape[0]):
        copies[k] = group[pl.ds(0, rows), :]
    gains = group[pl.ds(rows, 16), :].astype(f32)
    gain_a[...] = gains[0:1]
    gain_f[...] = gains[1:2]


def attn_copies(group, count):
    parts, tall, feats = group.shape
    rows = tall - 16
    gain = pl.BlockSpec((None, 1, feats), lambda z: (z, 0, 0))
    gain_shape = pltpu.HBM((parts, 1, feats), f32)
    return pl.pallas_call(
        attn_copies_kernel,
        grid=(parts,),
        in_specs=[pl.BlockSpec((None, tall, feats), lambda z: (z, 0, 0))],
        out_specs=[
            pl.BlockSpec((count, None, rows, feats), lambda z: (0, z, 0, 0)),
            gain,
            gain,
        ],
        out_shape=[
            pltpu.HBM((count, parts, rows, feats), bf16),
            gain_shape,
            gain_shape,
        ],
        compiler_params=params(),
        name="attn_copies",
    )(group)


def first_message_kernel(hidden, gain_a, gain_f, ids, out):
    rows, feats = hidden.shape
    out[pl.ds(0, rows), :] = hidden[...]
    docs = jnp.concatenate([ids[...].astype(f32)] * (feats // rows), 1)
    out[pl.ds(rows, 16), :] = stacked([gain_a[...], gain_f[...], docs])


def first_message(hidden, gain_a, gain_f, ids):
    shape = (hidden.shape[0] + 16, hidden.shape[1])
    arrays = (hidden, gain_a, gain_f, ids)
    return pl.pallas_call(
        first_message_kernel,
        grid=(1,),
        in_specs=[fixed(a.shape) for a in arrays],
        out_specs=fixed(shape),
        out_shape=pltpu.HBM(shape, bf16),
        compiler_params=params(WIDE),
        name="first_message",
    )(*arrays)


def total_of(parts):
    parts = parts.astype(f32)
    return parts[0:1] + parts[1:2] + parts[2:3]


def below(row, feats):
    return jnp.concatenate([stacked(three_parts(row))] * (feats // row.shape[1]), 1)


def ffn_copies_kernel(group, own, after, copies, message, sums):
    step = pl.program_id(0)
    rows, feats = own.shape
    for k in range(copies.shape[0]):
        copies[k] = group[pl.ds(0, rows), :]
    part = total_of(group[pl.ds(rows, 16), :])[:, :rows]

    @pl.when(step == 0)
    def _():
        message[pl.ds(0, rows), :] = own[...]
        sums[...] = part

    @pl.when(step > 0)
    def _():
        sums[...] += part

    @pl.when(step == pl.num_programs(0) - 1)
    def _():
        message[pl.ds(rows, 16), :] = below(sums[...], feats)


def ffn_copies(group, own, count, after):
    parts, tall, feats = group.shape
    rows = own.shape[0]
    return pl.pallas_call(
        ffn_copies_kernel,
        grid=(parts,),
        in_specs=[
            pl.BlockSpec((None, tall, feats), lambda z: (z, 0, 0)),
            fixed(own.shape),
            pl.BlockSpec(memory_space=pl.ANY),
        ],
        out_specs=[
            pl.BlockSpec((count, None, rows, feats), lambda z: (0, z, 0, 0)),
            fixed((tall, feats)),
        ],
        out_shape=[
            pltpu.HBM((count, parts, rows, feats), bf16),
            pltpu.HBM((tall, feats), bf16),
        ],
        scratch_shapes=[pltpu.VMEM((1, rows), f32)],
        compiler_params=params(),
        name="ffn_copies",
    )(group, own, after)


def kv_sum_kernel(width, arrived, docs, table, place, out):
    rows = out.shape[1] - 16
    kv = jnp.sum(arrived[:, pl.ds(0, rows), :].astype(f32), axis=0).astype(bf16)
    sums = jnp.sum(arrived[:, pl.ds(rows, 16), :].astype(f32), axis=0)
    r = lax.rsqrt((sums[0:1] + sums[1:2] + sums[2:3]) / width + norm_eps)
    tail = stacked(three_parts(r), [docs[...].astype(f32)[2:3, :rows]])
    for copy in range(out.shape[0]):
        out[copy, pl.ds(0, rows), :] = kv
        out[copy, pl.ds(rows, 16), :] = tail


def kv_sum(width, arrived, docs, copies, *after):
    blocks, tall, lanes = arrived.shape
    rows = HD
    last = tall - rows - 16
    return pl.pallas_call(
        functools.partial(kv_sum_kernel, width),
        grid=(1,),
        in_specs=[
            pl.BlockSpec(
                (pl.Element(blocks), pl.Element(rows + 16), pl.Element(lanes)),
                lambda i: (0, last, 0),
            ),
            pl.BlockSpec((16, docs.shape[1]), lambda i: (rows // 16, 0)),
        ]
        + [pl.BlockSpec(memory_space=pl.ANY)] * len(after),
        out_specs=fixed((copies, rows + 16, lanes)),
        out_shape=pltpu.HBM((copies, rows + 16, lanes), bf16),
        compiler_params=params(),
        name="kv_sum",
    )(arrived, docs, *after)


def rotate(values, table):
    lower = lax.broadcasted_iota(jnp.int32, table.shape, 1) < HD // 2
    swapped = pltpu.roll(table, HD // 2, 1)
    cosine = jnp.where(lower, table, swapped)
    sine = jnp.where(lower, -swapped, table)
    return values * cosine + pltpu.roll(values, HD // 2, 1) * sine


def column_of(row):
    n = row.shape[1]
    same = lax.broadcasted_iota(jnp.int32, (n, n), 0) == lax.broadcasted_iota(jnp.int32, (n, n), 1)
    return jnp.sum(jnp.where(same, row, f32(0.0)), axis=1, keepdims=True)


def halves(value):
    high = value.astype(bf16)
    return high, (value - high.astype(f32)).astype(bf16)


def attend_kernel(q_in, kv_in, table, resid, copies, out, keys, values, r_all, docs_all):
    rows, feats = out.shape
    heads = feats // HD
    tokens = keys.shape[0]
    x_pos = lax.axis_index("x")
    lower = lax.broadcasted_iota(jnp.int32, (rows, HD), 1) < HD // 2
    for k in range(tokens // rows):
        first = kv_in[2 * k, pl.ds(0, rows), :].astype(f32)
        second = kv_in[2 * k + 1, pl.ds(0, rows), :].astype(f32)
        tail = kv_in[2 * k, pl.ds(rows, 16), :].astype(f32)
        block = pl.ds(k * rows, rows)
        key = jnp.where(lower, first, pltpu.roll(second, HD // 2, 1))
        high, low = halves(rotate(key, table[block, :]))
        keys[block, :] = jnp.concatenate([high, high, low], 1)
        value = jnp.where(lower, pltpu.roll(first, HD // 2, 1), second).astype(bf16)
        values[block, :] = value
        values[pl.ds(tokens + k * rows, rows), :] = value
        r_all[:, block] = total_of(tail)
        docs_all[:, block] = tail[3:4]

    own = pl.ds(pl.multiple_of(x_pos * rows, rows), rows)
    r_own = column_of(r_all[:, own]) * (1.0 / HD**0.5)
    key_ids = lax.broadcasted_iota(jnp.int32, (rows, tokens), 1)
    own_ids = lax.broadcasted_iota(jnp.int32, (rows, tokens), 0) + x_pos * rows
    allowed = (key_ids <= own_ids) & (docs_all[...] == column_of(docs_all[:, own]))
    squares = jnp.zeros((rows, 1), f32)
    for h in range(heads):
        query = jnp.sum(q_in[:, pl.ds(h * rows, rows), :].astype(f32), axis=0)
        high, low = halves(rotate(query, table[own, :]) * r_own)
        scores = lax.dot_general(
            jnp.concatenate([high, low, high], 1), keys[...], (((1,), (1,)), ((), ())),
            preferred_element_type=f32,
        )
        scores = jnp.where(allowed, scores * r_all[...], f32(-1e30))
        peak = jnp.max(scores, axis=-1, keepdims=True)
        weights = jnp.where(allowed, jnp.exp(scores - peak), f32(0.0))
        total = jnp.sum(weights, axis=-1, keepdims=True)
        weights = jnp.concatenate(halves(weights * r_all[...]), 1)
        context = jnp.dot(weights, values[...], preferred_element_type=f32) / total
        lanes = pl.ds(h * HD, HD)
        result = (resid[:, lanes].astype(f32) + context).astype(bf16)
        out[:, lanes] = result
        for copy in range(copies.shape[0]):
            copies[copy, pl.ds(0, rows), lanes] = result
        result = result.astype(f32)
        squares += jnp.sum(result * result, axis=1, keepdims=True)
    tail = below(row_of(squares), feats)
    for copy in range(copies.shape[0]):
        copies[copy, pl.ds(rows, 16), :] = tail


def attend(q_in, kv_in, table, swapped, copies):
    rows, feats = swapped.shape[0] - 16, swapped.shape[1]
    heads, tokens = feats // HD, table.shape[0]
    shape = (copies, rows + 16, feats)
    return pl.pallas_call(
        attend_kernel,
        grid=(1,),
        in_specs=[
            fixed((q_in.shape[0], heads * rows, HD)),
            fixed(kv_in.shape),
            fixed(table.shape),
            fixed((rows, feats)),
        ],
        out_specs=[fixed(shape), fixed((rows, feats))],
        out_shape=[pltpu.HBM(shape, bf16), pltpu.HBM((rows, feats), bf16)],
        scratch_shapes=[
            pltpu.VMEM((tokens, 3 * HD), bf16),
            pltpu.VMEM((2 * tokens, HD), bf16),
            pltpu.VMEM((1, tokens), f32),
            pltpu.VMEM((1, tokens), f32),
        ],
        compiler_params=params(),
        name="attend",
    )(q_in, kv_in, table, swapped)


def attn_left_kernel(scale, own_rows, gain, kv, out):
    blocks, rows, feats = own_rows.shape
    for k in range(blocks):
        parts = kv[2 * k, pl.ds(rows, 16), :].astype(f32)
        r = parts[0:1] + parts[1:2] + parts[2:3]
        turned = (own_rows[k].astype(f32) * gain[...].astype(f32)).T
        out[:, pl.ds(k * rows, rows)] = (turned * (r * r * scale)).astype(bf16)


def attn_left(scale, own_rows, gain, kv_all):
    blocks, rows, feats = own_rows.shape
    arrays = (own_rows, gain, kv_all)
    return pl.pallas_call(
        functools.partial(attn_left_kernel, scale),
        grid=(1,),
        in_specs=[fixed(a.shape) for a in arrays],
        out_specs=fixed((feats, blocks * rows)),
        out_shape=jax.ShapeDtypeStruct((feats, blocks * rows), bf16),
        compiler_params=params(),
        name="attn_left",
    )(*arrays)


def hessian_kernel(
    scale, width, place, left_a, cols_a, gain_a, ffn_rows, gain_row, total, cols_f, gain_f,
    passed, out, diagonal, passed_out, left_f,
):
    blocks, rows, feats = cols_a.shape
    row, col = place[0], place[1] + pl.program_id(0)

    @pl.when(pl.program_id(0) == 0)
    def _():
        part = pl.ds(pl.multiple_of(lax.axis_index("seq") * rows, rows), rows)
        squares = jnp.zeros((1, rows), f32)
        for k in range(blocks):
            weight = column_of(scale / (total[k] / width + norm_eps))
            block = ffn_rows[k, pl.ds(0, rows), :].astype(f32) * gain_row[...].astype(f32)
            left_f[:, pl.ds(k * rows, rows)] = (block * weight).astype(bf16).T
            mine = ffn_rows[k, pl.ds(0, rows), part].astype(f32) * gain_row[:, part].astype(f32)
            squares += jnp.sum(mine * mine * weight, axis=0, keepdims=True)
        diagonal[...] = squares
        passed_out[...] = passed[...]

    def product(left, cols, gain):
        right = cols[...].reshape(blocks * rows, feats)
        return (jnp.dot(left[...], right, preferred_element_type=f32) * gain[...]).astype(bf16)

    @pl.when(row < col)
    def _():
        out[...] = product(left_a, cols_a, gain_a)

    @pl.when(row > col)
    def _():
        out[...] = product(left_f, cols_f, gain_f)

    @pl.when(row == col)
    def _():
        upper = product(left_a, cols_a, gain_a)
        lower = product(left_f, cols_f, gain_f)
        row_ids = lax.broadcasted_iota(jnp.int32, lower.shape, 0)
        col_ids = lax.broadcasted_iota(jnp.int32, lower.shape, 1)
        out[...] = jnp.where(row_ids <= col_ids, upper, lower)


def hessian(
    scale, width, place, left_a, cols_a, gain_a, ffn_rows, gain_row, total, cols_f, gain_f, passed
):
    blocks, parts, rows, feats = cols_a.shape
    tokens = blocks * rows

    def upper_at(z, at):
        return jnp.clip(jnp.maximum(z, at[0] - at[1]), 0, parts - 1)

    def lower_at(z, at):
        return jnp.clip(jnp.minimum(z, at[0] - at[1]), 0, parts - 1)

    gain = pl.BlockSpec((None, 1, feats), lambda z, at: (z, 0, 0))
    return pl.pallas_call(
        functools.partial(hessian_kernel, scale, width),
        grid_spec=pltpu.PrefetchScalarGridSpec(
            num_scalar_prefetch=1,
            grid=(parts,),
            in_specs=[
                fixed(left_a.shape),
                pl.BlockSpec((blocks, None, rows, feats), lambda z, at: (0, upper_at(z, at), 0, 0)),
                gain,
                fixed(ffn_rows.shape),
                fixed(gain_row.shape),
                fixed(total.shape),
                pl.BlockSpec((blocks, None, rows, feats), lambda z, at: (0, lower_at(z, at), 0, 0)),
                gain,
                fixed(passed.shape),
            ],
            out_specs=[
                pl.BlockSpec((feats, feats), lambda z, at: (0, z)),
                fixed((1, rows)),
                fixed(passed.shape),
            ],
            scratch_shapes=[pltpu.VMEM((feats, tokens), bf16)],
        ),
        out_shape=[
            jax.ShapeDtypeStruct((feats, parts * feats), bf16),
            jax.ShapeDtypeStruct((1, rows), f32),
            jax.ShapeDtypeStruct(passed.shape, bf16),
        ],
        compiler_params=params(),
        name="hessian",
    )(place, left_a, cols_a, gain_a, ffn_rows, gain_row, total, cols_f, gain_f, passed)


def on_device(hidden, segment_ids, gain_attn, gain_ffn, w_query, w_key, w_value):
    x_pos = lax.axis_index("x")
    zl_pos = lax.axis_index(ZL)
    seq_pos = lax.axis_index("seq")
    nx, nz, ns = lax.axis_size("x"), lax.axis_size(ZL), lax.axis_size("seq")
    rows, feats = hidden.shape[1:]
    tokens = rows * ns
    width = feats * nx * nz
    scale = 2.0 / tokens
    place = jnp.stack([x_pos * nz + zl_pos, seq_pos * nz])
    place = place.astype(jnp.int32)

    swapped = swap_x_seq(first_message(hidden[0], gain_attn, gain_ffn, segment_ids))
    half = HD // 2
    freq = rope_base ** (-(jnp.arange(half, dtype=f32) * 2.0 / HD))
    angle = jnp.arange(tokens, dtype=f32)[:, None] * freq[None, :]
    table = jnp.concatenate([jnp.cos(angle), jnp.sin(angle)], 1)
    group = lax.all_gather(swapped, ZL)
    copies, gain_a, gain_f = attn_copies(group, nx)
    attn_rows = lax.all_gather(hidden[0], "seq")
    attn_cols = lax.all_to_all(copies, "x", 0, 0)

    message = project(attn_cols, gain_a, w_query, w_key, w_value, attn_rows)
    arrived = lax.all_to_all(lax.all_to_all(message, "x", 0, 0), "seq", 0, 0)
    kv = lax.all_to_all(kv_sum(width, arrived, swapped, 2 * nx, table, place), ("x", "zb"), 0, 0)
    copies, section_out = attend(arrived, kv, table, swapped, nz)
    left_a = attn_left(scale, attn_rows, gain_attn, kv)

    out_rows = swap_x_seq(section_out)
    group = lax.all_to_all(copies, ZL, 0, 0)
    copies, message = ffn_copies(group, out_rows, nx, left_a)
    ffn_cols = lax.all_to_all(copies, "x", 0, 0)
    ffn_rows = lax.all_gather(message, "seq")
    total = jnp.sum(ffn_rows[:, rows : rows + 3, :rows].astype(f32), axis=(0, 1))
    total = lax.all_gather(total[None], "x")
    count = lax.axis_size("phase")
    passed = lax.dynamic_slice_in_dim(ffn_rows[:, :rows], seq_pos, 1, 0)
    passed = lax.ppermute(passed, "phase", [(p, (p + 1) % count) for p in range(count)])
    hessians, ffn_diagonal, passed = hessian(
        scale,
        width,
        place,
        left_a,
        attn_cols,
        gain_a,
        ffn_rows,
        gain_ffn,
        total,
        ffn_cols,
        gain_f,
        passed,
    )
    return (passed, hessians[None], ffn_diagonal)


def solution(mesh):
    phase, tensor, seq = (mesh.shape[a] for a in ("phase", "tensor", "seq"))
    lines = Mesh(
        mesh.devices.reshape(phase, tensor // 4, 2, 2, seq), ("phase", "x", "za", "zb", "seq")
    )
    tiled = P("phase", "seq", TENSOR)
    return jax.shard_map(
        on_device,
        mesh=lines,
        in_specs=(
            tiled,
            P("phase", "seq"),
            P("phase", TENSOR),
            P("phase", TENSOR),
            tiled,
            tiled,
            tiled,
        ),
        out_specs=(tiled, P("phase", TENSOR, "seq"), P("phase", GROUP)),
        check_vma=False,
    )
```
